32 devices in a mesh: seq: 8 (over z, x), batch: 4 (over y, core).
Axes of the slice: x: 2, y: 2, z: 4, core: 2. Of those that a mesh axis runs over, the one named last changes fastest.
Arguments:
- layer_input: bfloat16 [4, 2048, 768], P('batch', 'seq'), may hold values from -6 to 6
- cotangent: bfloat16 [4, 2048, 768], P('batch', 'seq'), may hold values from -6 to 6
- doc_lengths: int32 [4, 4], P('batch'), may hold values from 8 to 2024, as said below
- routes: int32 [3, 4, 256], P(None, 'batch', 'seq'), may hold values from 0 to 7
- norm_gains: bfloat16 [768, 2], P(('seq', 'batch')), may hold values from 0.5 to 1.5
- router: bfloat16 [768, 3], P(('seq', 'batch')), may hold values from -0.21875 to 0.21875
- light_qkv: bfloat16 [768, 2304], P(('seq', 'batch')), may hold values from -0.21875 to 0.21875
- light_out: bfloat16 [768, 768], P(('seq', 'batch')), may hold values from -0.875 to 0.875
- heavy_qkv: bfloat16 [768, 2304], P(('seq', 'batch')), may hold values from -0.21875 to 0.21875
- heavy_out: bfloat16 [768, 768], P(('seq', 'batch')), may hold values from -1.25 to 1.25
- light_in: bfloat16 [768, 2048], P(('seq', 'batch')), may hold values from -0.21875 to 0.21875
- light_down: bfloat16 [1024, 768], P(('seq', 'batch')), may hold values from -0.1875 to 0.1875
- heavy_in: bfloat16 [768, 8192], P(('seq', 'batch')), may hold values from -0.21875 to 0.21875
- heavy_down: bfloat16 [4096, 768], P(('seq', 'batch')), may hold values from -0.09375 to 0.09375
Outputs:
- layer_output: bfloat16 [4, 2048, 768], P('batch', 'seq')
- input_grad: float32 [4, 2048, 768], P('batch', 'seq')
- grad_norm_gains: float32 [768, 2], P(('seq', 'batch'))
- grad_router: float32 [768, 3], P(('seq', 'batch'))
- grad_light_qkv: float32 [768, 2304], P(('seq', 'batch'))
- grad_light_out: float32 [768, 768], P(('seq', 'batch'))
- grad_heavy_qkv: float32 [768, 2304], P(('seq', 'batch'))
- grad_heavy_out: float32 [768, 768], P(('seq', 'batch'))
- grad_light_in: float32 [768, 2048], P(('seq', 'batch'))
- grad_light_down: float32 [1024, 768], P(('seq', 'batch'))
- grad_heavy_in: float32 [768, 8192], P(('seq', 'batch'))
- grad_heavy_down: float32 [4096, 768], P(('seq', 'batch'))
The draws below stay inside these ranges and needn't reach their ends.
Inputs may be any that keep to these rules, and one draw needn't show every extreme that they name: `doc_lengths`: every length is a multiple of 8 and the lengths of a group sum to its positions. The second document of every group starts within its first 256 positions and ends within its last 256; the other documents lie before or after it. Each branch routes exactly one token of every aligned block of 8 positions.
All inputs are finite; a program needn't handle non-finite values.
Results may differ from the reference program's by a relative error of at most 0.014.
Values may be sent and summed in bfloat16 or wider, within the bound.
No kernel may reach another device: no remote copies, remote signals or barrier semaphores. Data moves between devices by JAX's collectives and lax.ppermute only.
A program may use at most 320 MiB of HBM per device.

```python
import math
import jax
import jax.numpy as jnp
from jax import lax

D = 768
HL = 8
DL = 96
HH = 12
DH = 64
FL = 1024
FH = 4096
TOK_DEV = 256
WIN = 128
ROUTE = 8
GROUP = 2048
GROUPS = 4
ROUTED = 256


def draw_doc_lengths(key, part):
    key = jax.random.fold_in(key, 5)
    blocks_dev = TOK_DEV // ROUTE
    first_key, remainder_key, third_key, chosen_key = jax.random.split(key, 4)
    leading = jax.random.randint(first_key, (GROUPS,), 1, blocks_dev)
    remainder = jax.random.randint(remainder_key, (GROUPS,), 2, blocks_dev)
    trailing = jax.random.randint(third_key, (GROUPS,), 1, remainder)
    chosen_group = jax.random.randint(chosen_key, (), 0, GROUPS)
    is_chosen = jnp.arange(GROUPS, dtype=jnp.int32) == chosen_group
    leading = jnp.where(is_chosen, 1, leading)
    remainder = jnp.where(is_chosen, 2, remainder)
    trailing = jnp.where(is_chosen, 1, trailing)
    closing = remainder - trailing
    spanning = GROUP - (leading + remainder) * ROUTE
    return jnp.stack([leading * ROUTE, spanning, trailing * ROUTE, closing * ROUTE], axis=1).astype(jnp.int32)


def touch_ends(result, stream_key, low, top_value):
    dims = result.shape
    place = [jax.random.randint(jax.random.fold_in(stream_key, axis), (), 0, dims[axis]) for axis in range(len(dims))]
    result = result.at[tuple(place)].set(low)
    longest = dims.index(max(dims))
    place[longest] = (place[longest] + 1) % dims[longest]
    return result.at[tuple(place)].set(top_value)


def levels(own_key, shape, shards, smallest, high):
    def one(dim, blocks):
        draws = jax.random.uniform(jax.random.fold_in(jax.random.fold_in(own_key, 6), dim), (blocks,), jnp.float32, smallest / len(shards), high / len(shards))
        return jnp.repeat(jnp.exp(draws), shape[dim] // blocks).reshape((-1,) + (1,) * (len(shape) - dim - 1))

    factor_of = one(*shards[0])
    for cut in shards[1:]:
        factor_of = factor_of * one(*cut)
    return factor_of


def normal_values(rng, shape, deviation, bound, cuts=(), kind=jnp.bfloat16):
    level = levels(rng, shape, cuts, -0.22, 0.18) if cuts else 1.0
    array = jax.random.normal(rng, shape, jnp.float32) * deviation * level
    return jnp.minimum(jnp.maximum(array, -bound), bound).astype(kind)


def setup_inputs(seed: int = 0) -> dict:
    key_of = jax.random.split(jax.random.key(seed), 15)
    layer_input = normal_values(key_of[0], (GROUPS, GROUP, D), 1.0, 6.0, ((0, 4), (1, 8)))
    cotangent = normal_values(key_of[1], (GROUPS, GROUP, D), 1.0, 6.0, ((0, 4), (1, 8)))
    doc_lengths = draw_doc_lengths(jax.random.fold_in(key_of[14], 71), 0)
    routes = touch_ends(jax.random.randint(key_of[3], (3, GROUPS, ROUTED), 0, ROUTE), jax.random.fold_in(key_of[3], 1), 0, ROUTE - 1).astype(jnp.int32)
    norm_gains = jnp.clip(1.0 + 0.1 * jax.random.normal(key_of[4], (D, 2), jnp.float32), 0.5, 1.5).astype(jnp.bfloat16)
    router = normal_values(key_of[5], (D, 3), D ** -0.5, 0.21875, ((0, 32),))
    light_qkv = normal_values(key_of[6], (D, 3 * D), D ** -0.5, 0.21875, ((0, 32),))
    light_out = normal_values(key_of[7], (D, D), (D // 16) ** -0.5, 0.875, ((0, 32),))
    heavy_qkv = normal_values(key_of[8], (D, 3 * D), D ** -0.5, 0.21875, ((0, 32),))
    heavy_out = normal_values(key_of[9], (D, D), (D // 32) ** -0.5, 1.25, ((0, 32),))
    light_in = normal_values(key_of[10], (D, 2 * FL), D ** -0.5, 0.21875, ((0, 32),))
    light_down = normal_values(key_of[11], (FL, D), FL ** -0.5, 0.1875, ((0, 32),))
    heavy_in = normal_values(key_of[12], (D, 2 * FH), D ** -0.5, 0.21875, ((0, 32),))
    heavy_down = normal_values(key_of[13], (FH, D), FH ** -0.5, 0.09375, ((0, 32),))
    return dict(layer_input=layer_input, cotangent=cotangent, doc_lengths=doc_lengths, routes=routes, norm_gains=norm_gains, router=router, light_qkv=light_qkv, light_out=light_out, heavy_qkv=heavy_qkv, heavy_out=heavy_out, light_in=light_in, light_down=light_down, heavy_in=heavy_in, heavy_down=heavy_down)


epsilon = 1e-06
highest = lax.Precision.HIGHEST

@jax.custom_vjp
def low(v):
    return lax.optimization_barrier(v.astype(jnp.bfloat16)).astype(jnp.float32)

@jax.custom_vjp
def low_back(v):
    return v

def low_keep(v):
    return (low(v), None)

def low_pass(kept, grad):
    return (grad,)

def back_keep(v):
    return (v, None)

def back_low(kept, grad):
    return (low(grad),)
low.defvjp(low_keep, low_pass)
low_back.defvjp(back_keep, back_low)

def matmul(left, right):
    return jnp.dot(left, right, precision=highest)

def rms_scale(values, gain):
    return values * lax.rsqrt(lax.optimization_barrier(jnp.mean(values * values, axis=-1, keepdims=True)) + epsilon) * gain

def geglu(both):
    half = both.shape[-1] // 2
    return jax.nn.gelu(both[:, :half]) * both[:, half:]

def document_of(positions, lengths):
    ends = jnp.cumsum(lengths)
    return lax.optimization_barrier(jnp.sum((positions[:, None] >= ends[None, :]).astype(jnp.int32), axis=1)).astype(jnp.int32)

def select_rows(rows, picks):
    routed = picks.shape[0]
    blocks = rows.reshape(routed, rows.shape[0] // routed, rows.shape[1])
    onehot = (lax.broadcasted_iota(jnp.int32, (routed, blocks.shape[1]), 1) == picks[:, None]).astype(rows.dtype)
    return lax.optimization_barrier(jnp.sum(blocks * onehot[:, :, None], axis=1))

def spread_rows(rows, picks):
    routed = picks.shape[0]
    onehot = (lax.broadcasted_iota(jnp.int32, (routed, ROUTE), 1) == picks[:, None]).astype(rows.dtype)
    return (onehot[:, :, None] * rows[:, None, :]).reshape(routed * ROUTE, rows.shape[1])

def attention_core(queries, keys, values, allowed, scale):
    scores = jnp.einsum('qhe,khe->hqk', queries, keys, precision=highest) * scale
    scores = low_back(jnp.where(allowed[None], scores, -1e+30))
    probs = low(jax.nn.softmax(scores, axis=-1))
    mixed = jnp.einsum('hqk,khe->qhe', probs, values, precision=highest)
    return mixed.reshape(queries.shape[0], -1)

def light_attention(qkv, documents, features):
    total = qkv.shape[0]
    block = math.gcd(total, 512)
    queries = qkv[:, :features].reshape(total, HL, DL)
    padded = jnp.pad(qkv[:, features:], ((WIN, WIN), (0, 0)))
    padded_docs = jnp.pad(documents, (WIN, WIN), constant_values=-1)

    def one_block(first):
        query_rows = lax.dynamic_slice_in_dim(queries, first, block, 0)
        pair_rows = lax.dynamic_slice_in_dim(padded, first, block + 2 * WIN, 0)
        query_docs = lax.dynamic_slice_in_dim(documents, first, block, 0)
        key_docs = lax.dynamic_slice_in_dim(padded_docs, first, block + 2 * WIN, 0)
        query_pos = first + jnp.arange(block, dtype=jnp.int32)
        key_pos = first - WIN + jnp.arange(block + 2 * WIN, dtype=jnp.int32)
        allowed = (jnp.abs(query_pos[:, None] - key_pos[None, :]) < WIN) & (query_docs[:, None] == key_docs[None, :])
        keys = pair_rows[:, :features].reshape(-1, HL, DL)
        values = pair_rows[:, features:].reshape(-1, HL, DL)
        return attention_core(query_rows, keys, values, allowed, DL ** (-0.5))
    firsts = jnp.arange(total // block, dtype=jnp.int32) * block
    mixed = lax.map(jax.checkpoint(one_block), firsts)
    return mixed.reshape(total, features)

def heavy_attention(queries, keyvals, routed_docs, features):
    routed = queries.shape[0]
    block = math.gcd(routed, 512)
    query_heads = queries.reshape(routed, HH, DH)
    keys = keyvals[:, :features].reshape(-1, HH, DH)
    values = keyvals[:, features:].reshape(-1, HH, DH)

    def one_block(first):
        query_rows = lax.dynamic_slice_in_dim(query_heads, first, block, 0)
        query_docs = lax.dynamic_slice_in_dim(routed_docs, first, block, 0)
        allowed = query_docs[:, None] == routed_docs[None, :]
        return attention_core(query_rows, keys, values, allowed, DH ** (-0.5))
    firsts = jnp.arange(routed // block, dtype=jnp.int32) * block
    mixed = lax.map(jax.checkpoint(one_block), firsts)
    return mixed.reshape(routed, features)

def group_forward(weights, rows, lengths, picks):
    gains, router, light_qkv, light_out, heavy_qkv, heavy_out, light_in, light_down, heavy_in, heavy_down = weights
    total, features = rows.shape
    documents = document_of(jnp.arange(total, dtype=jnp.int32), lengths)
    normed = rms_scale(rows, gains[:, 0])
    normed_low = low(normed)
    qkv = low_back(low(matmul(normed_low, light_qkv)))
    light_mixed = low_back(low(light_attention(qkv, documents, features)))
    light_branch = low_back(matmul(light_mixed, light_out))
    query_in = select_rows(normed_low, picks[0])
    key_in = select_rows(normed_low, picks[1])
    query_gate = jax.nn.sigmoid(matmul(select_rows(normed, picks[0]), router[:, 0]))
    key_gate = jax.nn.sigmoid(matmul(select_rows(normed, picks[1]), router[:, 1]))
    heavy_q = low_back(low(matmul(query_in, heavy_qkv[:, :features])))
    key_raw = low_back(matmul(key_in, heavy_qkv[:, features:]))
    heavy_kv = low_back(low(jnp.concatenate([key_raw[:, :features], key_raw[:, features:] * key_gate[:, None]], axis=1)))
    routed_docs = document_of(jnp.arange(total // ROUTE, dtype=jnp.int32) * ROUTE, lengths)
    heavy_mixed = low_back(low(heavy_attention(heavy_q, heavy_kv, routed_docs, features)))
    heavy_rows = low_back(matmul(heavy_mixed, heavy_out)) * query_gate[:, None]
    middle = rows + light_branch + spread_rows(heavy_rows, picks[0])
    normed2 = rms_scale(middle, gains[:, 1])
    normed2_low = low(normed2)
    light_pair = low_back(matmul(normed2_low, light_in))
    light_ffn = low_back(matmul(low(geglu(light_pair)), light_down))
    ffn_gate = jax.nn.sigmoid(matmul(select_rows(normed2, picks[2]), router[:, 2]))
    heavy_pair = low_back(matmul(select_rows(normed2_low, picks[2]), heavy_in))
    heavy_ffn = low_back(matmul(low(geglu(heavy_pair)), heavy_down)) * ffn_gate[:, None]
    return middle + light_ffn + spread_rows(heavy_ffn, picks[2])

def reference(layer_input, cotangent, doc_lengths, routes, norm_gains, router, light_qkv, light_out, heavy_qkv, heavy_out, light_in, light_down, heavy_in, heavy_down):
    weights = (norm_gains.astype(jnp.float32), router.astype(jnp.float32), light_qkv.astype(jnp.float32), light_out.astype(jnp.float32), heavy_qkv.astype(jnp.float32), heavy_out.astype(jnp.float32), light_in.astype(jnp.float32), light_down.astype(jnp.float32), heavy_in.astype(jnp.float32), heavy_down.astype(jnp.float32))

    def forward(params, inputs):
        results = [group_forward(params, inputs[group], doc_lengths[group], routes[:, group]) for group in range(GROUPS)]
        return jnp.stack(results)
    output, pullback = jax.vjp(forward, weights, layer_input.astype(jnp.float32))
    grads, input_grad = pullback(cotangent.astype(jnp.float32))
    return (output.astype(jnp.bfloat16), input_grad, grads[0], grads[1], grads[2], grads[3], grads[4], grads[5], grads[6], grads[7], grads[8], grads[9])
```

```python
import functools

import jax
import jax.numpy as jnp
import numpy as np
from jax import lax
from jax.experimental import pallas as pl
from jax.experimental.pallas import tpu as pltpu
from jax.sharding import PartitionSpec as P

HL = 8
DL = 96
HH = 12
DH = 64
WIN = 128
ROUTE = 8
SMALL = 128
CHUNK = 256
PARTS = 4
LANES = 256
EPS = 1e-06
BF = jnp.bfloat16
F32 = jnp.float32
BOTH = ("seq", "batch")
highest = lax.Precision.HIGHEST
VMEM_LIMIT = 60 * 1024 * 1024


def nn(left, right):
    return jnp.dot(left, right, preferred_element_type=F32)


def nt(left, right):
    return lax.dot_general(left, right, (((1,), (1,)), ((), ())), preferred_element_type=F32)


def tn(left, right):
    return lax.dot_general(left, right, (((0,), (0,)), ((), ())), preferred_element_type=F32)


def exact(left, right):
    return jnp.dot(left, right, precision=highest, preferred_element_type=F32)


def low(values):
    return values.astype(BF)


def row_sum(values):
    return jnp.sum(values, axis=-1, keepdims=True)


def rms_inverse(values):
    return lax.rsqrt(jnp.mean(values * values, axis=-1, keepdims=True) + EPS)


def rms_back(grad, values, inverse, gain):
    scaled = grad * gain
    inner = jnp.mean(scaled * values, axis=-1, keepdims=True)
    return inverse * scaled - values * (inverse * inverse * inverse * inner)


def geglu_parts(pair):
    half = pair.shape[-1] // 2
    u = pair[:, :half]
    up = pair[:, half:]
    c = 0.7978845608028654
    t = jnp.tanh(c * (u + 0.044715 * (u * u * u)))
    gelu = 0.5 * u * (1.0 + t)
    slope = 0.5 * (1.0 + t) + 0.5 * u * (1.0 - t * t) * (c * (1.0 + 3.0 * 0.044715 * (u * u)))
    return gelu, slope, up


def documents(positions, meta):
    found = (positions >= meta[0]).astype(jnp.int32)
    for i in range(1, 4):
        found = found + (positions >= meta[i]).astype(jnp.int32)
    return found


def head_rows(width, size):
    lanes = lax.broadcasted_iota(jnp.int32, (1, width), 1)
    inside = [(lanes >= i * size) & (lanes < (i + 1) * size) for i in range(width // size)]
    return [jnp.where(one, 1.0, 0.0) for one in inside]


def stack_heads(rows, masks):
    return jnp.concatenate([rows * low(mask) for mask in masks], axis=0)


def merge_heads(stacked, masks):
    count = stacked.shape[0] // len(masks)
    total = stacked[:count] * masks[0]
    for i in range(1, len(masks)):
        total = total + stacked[i * count : (i + 1) * count] * masks[i]
    return total


def softmax(scores):
    weights = jnp.exp(scores - jnp.max(scores, axis=-1, keepdims=True))
    return weights * (1.0 / row_sum(weights))


def light_bias(meta, block, tokens):
    query = meta[4] + block * WIN + lax.broadcasted_iota(jnp.int32, (WIN, 1), 0)
    key = meta[4] + (block - 1) * WIN + lax.broadcasted_iota(jnp.int32, (1, 3 * WIN), 1)
    key_doc = jnp.where((key >= 0) & (key < meta[5]), documents(key, meta), -1)
    seen = (jnp.abs(query - key) < WIN) & (documents(query, meta) == key_doc)
    return jnp.where(seen, 0.0, -1e30)


def heavy_bias(meta, count, keys):
    query = (meta[6] + lax.broadcasted_iota(jnp.int32, (count, 1), 0)) * ROUTE
    key = lax.broadcasted_iota(jnp.int32, (1, keys), 1) * ROUTE
    return jnp.where(documents(query, meta) == documents(key, meta), 0.0, -1e30)


def light_units(tokens):
    return [(block, part) for block in range(tokens // WIN) for part in range(2)]


def sigmoid_dot(rows, vector):
    return jax.nn.sigmoid(row_sum(rows * vector))


def load(full_ref, places, sems):
    copies = []
    for i, ((first, last), buffer) in enumerate(places):
        copies.append(pltpu.make_async_copy(full_ref.at[:, first:last], buffer, sems.at[i]))
        copies[-1].start()
    return copies


def two_lanes(column):
    lanes = lax.broadcasted_iota(jnp.int32, (column.shape[0], SMALL), 1)
    high = low(column).astype(F32)
    return low(jnp.where(lanes == 0, high, jnp.where(lanes == 1, column - high, 0.0)))


def from_two_lanes(block):
    lanes = lax.broadcasted_iota(jnp.int32, block.shape, 1)
    return row_sum(jnp.where(lanes < 2, block.astype(F32), 0.0))


def sum_blocks(ref, count):
    total = ref[0:count].astype(F32)
    for i in range(1, ref.shape[0] // count):
        total = total + ref[i * count : (i + 1) * count].astype(F32)
    return total


def heavy_forward(
    meta,
    xq_ref,
    xk_ref,
    wx_ref,
    out_ref,
    raw_ref,
    q_ref,
    kv_ref,
    mixed_ref,
    small_ref,
):
    count = xq_ref.shape[0]
    keys = xk_ref.shape[0]
    at = 0
    small = jnp.transpose(wx_ref[:, 3 * LANES :].astype(F32))[:8]
    small_ref[...] = small
    gain_1 = small[0:1]
    xq = xq_ref[...].astype(F32)
    q_norm = xq * rms_inverse(xq) * gain_1
    q_ref[...] = low(nn(low(q_norm), wx_ref[:, at : at + LANES]))
    size = min(CHUNK, keys)
    for start in range(0, keys, size):
        xk = xk_ref[start : start + size].astype(F32)
        k_norm = xk * rms_inverse(xk) * gain_1
        k_gate = sigmoid_dot(k_norm, small[3:4])
        raw = nn(low(k_norm), wx_ref[:, at + LANES : at + 3 * LANES])
        kv_ref[start : start + size, :LANES] = low(raw[:, :LANES])
        kv_ref[start : start + size, LANES:] = low(raw[:, LANES:] * k_gate)
    masks = head_rows(LANES, DH)[: HH // PARTS]
    bias = jnp.concatenate([heavy_bias(meta, count, keys)] * len(masks), axis=0)
    stacked = stack_heads(q_ref[...], masks)
    probs = softmax(nt(stacked, kv_ref[:, :LANES]) * DH ** (-0.5) + bias)
    mixed = low(merge_heads(nn(low(probs), kv_ref[:, LANES:]), masks))
    mixed_ref[...] = mixed
    raw_ref[...] = jnp.zeros_like(raw_ref)
    raw_ref[pl.ds(pl.multiple_of(meta[6], count), count)] = low(nn(mixed, out_ref[...]))


def light_forward(
    layout,
    meta,
    below_ref,
    x_ref,
    above_ref,
    xq_ref,
    raw_ref,
    pq_t_ref,
    pf_ref,
    small_ref,
    full_ref,
    q_ref,
    kv_ref,
    mixed_ref,
    heavy_raw_ref,
    middle_ref,
    normed2_ref,
    f_norm_ref,
    f_sent_ref,
    w_qkv,
    w_lo,
    sems,
):
    tokens, features = x_ref.shape
    routed = xq_ref.shape[0]
    copies = load(full_ref, [(layout["light_qkv"], w_qkv), (layout["light_out"], w_lo)], sems)
    small = small_ref[...]
    gain_1, gain_2 = small[0:1], small[1:2]
    xe = jnp.concatenate([below_ref[...], x_ref[...], above_ref[...]], axis=0).astype(F32)
    ne = low(xe * rms_inverse(xe) * gain_1)
    xq = xq_ref[...].astype(F32)
    q_gate = sigmoid_dot(xq * rms_inverse(xq) * gain_1, small[2:3])
    heavy_raw = sum_blocks(raw_ref, routed)
    heavy_raw_ref[...] = heavy_raw
    base = x_ref[...].astype(F32) + exact(pq_t_ref[...], heavy_raw * q_gate)
    copies[0].wait()
    q_ref[...] = low(nn(ne[WIN : WIN + tokens], w_qkv[:, :features]))
    kv_ref[...] = low(nn(ne, w_qkv[:, features:]))
    width = features // 2
    masks = head_rows(width, DL)
    scale = DL ** (-0.5)
    for block, part in light_units(tokens):
        cols = slice(part * width, (part + 1) * width)
        rows = slice(block * WIN, (block + 1) * WIN)
        key_rows = slice(block * WIN, (block + 3) * WIN)
        bias = jnp.concatenate([light_bias(meta, block, tokens)] * len(masks), axis=0)
        stacked = stack_heads(q_ref[rows, cols], masks)
        probs = softmax(nt(stacked, kv_ref[key_rows, cols]) * scale + bias)
        values = kv_ref[key_rows, features + part * width : features + (part + 1) * width]
        mixed_ref[rows, cols] = low(merge_heads(nn(low(probs), values), masks))
    copies[1].wait()
    middle = base + nn(mixed_ref[...], w_lo[...])
    middle_ref[...] = middle
    normed2 = middle * rms_inverse(middle) * gain_2
    normed2_ref[...] = low(normed2)
    f_norm = exact(pf_ref[...], normed2)
    f_norm_ref[...] = f_norm
    sent = jnp.concatenate([low(f_norm), two_lanes(sigmoid_dot(f_norm, small[4:5]))], axis=1)
    for i in range(f_sent_ref.shape[0] // routed):
        f_sent_ref[i * routed : (i + 1) * routed] = sent


def unpack_down(packed, down_ref, work_ref, devices):
    features = down_ref.shape[1]
    rows = packed.shape[0] // devices
    more = down_ref.shape[0] // devices - rows
    width = packed.shape[1] - features
    if rows % 8 == 0 and more % 8 == 0:
        work_ref[...] = packed.astype(F32)
        for i in range(devices):
            own = work_ref[i * rows : (i + 1) * rows, :features]
            parts = [
                work_ref[i * rows + j * more : i * rows + (j + 1) * more, features:]
                for j in range(rows // more)
            ]
            whole = jnp.concatenate([own, jnp.concatenate(parts, axis=1)], axis=0)
            down_ref[i * (rows + more) : (i + 1) * (rows + more)] = low(whole)
    else:
        for j in range(rows // more):
            cols = slice(j * width, (j + 1) * width)
            first, second = down_places(down_ref.shape[0], packed.shape[0], rows, more, j)
            down_ref[:, cols] = low(nn(first, packed[:, cols]) + nn(second, packed[:, features:]))


def down_places(units, packed_rows, rows, more, j):
    unit = lax.broadcasted_iota(jnp.int32, (units, packed_rows), 0)
    row = lax.broadcasted_iota(jnp.int32, (units, packed_rows), 1)
    total = rows + more
    device, inner = unit // total, unit % total
    first = (inner < rows) & (row == device * rows + inner)
    second = (inner >= rows) & (row == device * rows + j * more + inner - rows)
    return low(jnp.where(first, 1.0, 0.0)), low(jnp.where(second, 1.0, 0.0))


def pack_down(grad, out_ref, at, devices, rows):
    features = grad.shape[1]
    more = grad.shape[0] // devices - rows
    width = features * more // rows
    if rows % 8 == 0 and more % 8 == 0:
        pieces = []
        for i in range(devices):
            start = i * (rows + more)
            rest = grad[start + rows : start + rows + more]
            parts = [rest[:, j * width : (j + 1) * width] for j in range(rows // more)]
            pieces.append(
                jnp.concatenate([grad[start : start + rows], jnp.concatenate(parts, axis=0)], axis=1)
            )
        out_ref[:, at:] = low(jnp.concatenate(pieces, axis=0))
    else:
        total = None
        for j in range(rows // more):
            cols = slice(j * width, (j + 1) * width)
            first, second = down_places(grad.shape[0], devices * rows, rows, more, j)
            block = low(grad[:, cols])
            out_ref[:, at + j * width : at + (j + 1) * width] = low(tn(first, block))
            part = tn(second, block)
            total = part if total is None else total + part
        out_ref[:, at + features :] = low(total)


def light_ffn(
    layout,
    devices,
    normed2_ref,
    g_ref,
    order_ref,
    full_ref,
    ffn_ref,
    grad_ref,
    send_ref,
    keep_ref,
    w_in,
    w_packed,
    w_down,
    work_ref,
    pack_ref,
    sems,
):
    features = normed2_ref.shape[1]
    half = features // 2
    order = order_ref[...]
    copies = []
    for i, (name, buffer) in enumerate([("light_in", w_in), ("light_down", w_packed)]):
        first, last = layout[name]
        copy = pltpu.make_async_copy(full_ref.at[:, first:last], buffer, sems.at[i])
        copy.start()
        copies.append(copy)
    copies[0].wait()
    copies[1].wait()
    unpack_down(w_packed[...], w_down, work_ref, devices)
    gelu, slope, up = geglu_parts(nn(normed2_ref[...], w_in[...]))
    hidden = low(gelu * up)
    ffn_ref[...] = nn(hidden, w_down[...])
    grad_hidden = nt(g_ref[...], w_down[...])
    grad_pair = low(jnp.concatenate([grad_hidden * up * slope, grad_hidden * gelu], axis=1))
    grad_ref[...] = nt(grad_pair, w_in[...])
    wide = w_in.shape[1]
    left = low(nn(normed2_ref[...], order))
    for at in range(0, wide, 512):
        block = low(tn(left, grad_pair[:, at : at + 512]))
        send_ref[:, at : at + 512] = block[:half]
        keep_ref[:, at : at + 512] = block[half:]
    pack_down(tn(hidden, g_ref[...]), pack_ref, 0, devices, features // devices)
    block = low(tn(order, pack_ref[...]))
    send_ref[:, wide:] = block[:half]
    keep_ref[:, wide:] = block[half:]


def heavy_ffn(
    batch_n,
    sent_ref,
    t_ref,
    in_ref,
    down_ref,
    order_ref,
    order_units_ref,
    back_ref,
    ffn_ref,
    send_ref,
    keep_ref,
):
    features = in_ref.shape[0]
    hidden_n = down_ref.shape[0]
    w_in = in_ref[...]
    f_in = sent_ref[:, :features]
    gate = from_two_lanes(sent_ref[:, features:])
    t = t_ref[...].astype(F32)
    grad_ffn = low(t * gate)
    gelu, slope, up = geglu_parts(nn(f_in, w_in))
    hidden = low(gelu * up)
    ffn = nn(hidden, down_ref[...])
    ffn_ref[...] = low(ffn)
    grad_hidden = nt(grad_ffn, down_ref[...])
    grad_pair = low(jnp.concatenate([grad_hidden * up * slope, grad_hidden * gelu], axis=1))
    back_ref[:, :features] = low(nt(grad_pair, w_in))
    back_ref[:, features:] = two_lanes(row_sum(t * ffn))
    grad_in = low(tn(low(nn(f_in, order_ref[...])), grad_pair))
    grad_down = low(tn(low(nn(hidden, order_units_ref[...])), grad_ffn))
    put_blocks(send_ref, keep_ref, batch_n, grad_in, grad_down)


def put_blocks(send_ref, keep_ref, batch_n, upper, lower):
    upper_rows = upper.shape[0] // batch_n
    lower_rows = lower.shape[0] // batch_n
    total = upper_rows + lower_rows
    width = send_ref.shape[1]
    for i in range(batch_n):
        ref = send_ref if i < batch_n // 2 else keep_ref
        start = i % (batch_n // 2) * total
        places = [(start, upper_rows, upper), (start + upper_rows, lower_rows, lower)]
        for first, count, values in places:
            ref[first : first + count, : values.shape[1]] = values[i * count : (i + 1) * count]
            if values.shape[1] < width:
                ref[first : first + count, values.shape[1] :] = jnp.zeros(
                    (count, width - values.shape[1]), BF
                )


def light_backward(
    layout,
    meta,
    below_ref,
    x_ref,
    above_ref,
    xq_ref,
    pq_ref,
    pq_t_ref,
    pf_t_ref,
    g_ref,
    order_ref,
    q_ref,
    kv_ref,
    mixed_ref,
    heavy_raw_ref,
    middle_ref,
    f_norm_ref,
    small_ref,
    grad_n2_ref,
    back_ref,
    full_ref,
    grad_middle_ref,
    grad_normed_ref,
    halo_below_ref,
    halo_above_ref,
    grad_raw_ref,
    small_grad_ref,
    send_ref,
    keep_ref,
    w_qkv,
    w_lo,
    dq_ref,
    dkv_ref,
    stage,
    sems,
    out_sems,
):
    tokens, features = x_ref.shape
    routed = xq_ref.shape[0]
    half = features // 2
    copies = load(full_ref, [(layout["light_out"], w_lo), (layout["light_qkv"], w_qkv)], sems)
    small = small_ref[...]
    gain_1, gain_2 = small[0:1], small[1:2]
    started = []

    def put(at, grad):
        width = grad.shape[1]
        slot = len(started) % stage.shape[0]
        if len(started) >= stage.shape[0]:
            for copy in started[-stage.shape[0]]:
                copy.wait()
        stage[slot, :, :width] = low(grad)
        both = []
        for i, ref in enumerate((send_ref, keep_ref)):
            source = stage.at[slot, i * half : (i + 1) * half, :width]
            both.append(
                pltpu.make_async_copy(source, ref.at[:, at : at + width], out_sems.at[slot, i])
            )
            both[-1].start()
        started.append(both)

    sums = sum_blocks(back_ref, routed)
    f_norm = f_norm_ref[...]
    f_gate = sigmoid_dot(f_norm, small[4:5])
    f_logit = (sums[:, features : features + 1] + sums[:, features + 1 : features + 2]) * (
        f_gate * (1.0 - f_gate)
    )
    router_f = jnp.sum(f_norm * f_logit, axis=0, keepdims=True)
    f_back = sums[:, :features] + f_logit * small[4:5]
    middle = middle_ref[...]
    grad_n2 = grad_n2_ref[...] + exact(pf_t_ref[...], f_back)
    inverse_2 = rms_inverse(middle)
    gain_2_grad = jnp.sum(grad_n2 * (middle * inverse_2), axis=0, keepdims=True)
    grad_middle = g_ref[...].astype(F32) + rms_back(grad_n2, middle, inverse_2, gain_2)
    grad_middle_ref[...] = grad_middle
    middle_low = low(grad_middle)

    q_rows = exact(pq_ref[...], grad_middle)
    xq = xq_ref[...].astype(F32)
    q_plain = xq * rms_inverse(xq)
    q_norm = q_plain * gain_1
    q_gate = sigmoid_dot(q_norm, small[2:3])
    grad_raw = low(q_rows * q_gate)
    for i in range(grad_raw_ref.shape[0] // routed):
        grad_raw_ref[i * routed : (i + 1) * routed] = grad_raw
    q_logit = row_sum(q_rows * heavy_raw_ref[...]) * q_gate * (1.0 - q_gate)
    q_back = q_logit * small[2:3]
    router_q = jnp.sum(q_norm * q_logit, axis=0, keepdims=True)
    gain_1_grad = jnp.sum(q_back * q_plain, axis=0, keepdims=True)

    copies[0].wait()
    order = order_ref[...]
    put(3 * features, tn(low(nn(mixed_ref[...], order)), middle_low))
    do = low(nt(middle_low, w_lo[...]))
    width = features // 2
    masks = head_rows(width, DL)
    scale = DL ** (-0.5)
    dkv_ref[...] = jnp.zeros_like(dkv_ref)
    for block, part in light_units(tokens):
        cols = slice(part * width, (part + 1) * width)
        value_cols = slice(features + part * width, features + (part + 1) * width)
        rows = slice(block * WIN, (block + 1) * WIN)
        key_rows = slice(block * WIN, (block + 3) * WIN)
        bias = jnp.concatenate([light_bias(meta, block, tokens)] * len(masks), axis=0)
        stacked = stack_heads(q_ref[rows, cols], masks)
        do_stacked = stack_heads(do[rows, cols], masks)
        key = kv_ref[key_rows, cols]
        probs = softmax(nt(stacked, key) * scale + bias)
        grad_probs = nt(do_stacked, kv_ref[key_rows, value_cols])
        ds = low(probs * (grad_probs - row_sum(probs * grad_probs)))
        dq_ref[rows, cols] = low(merge_heads(nn(ds, key), masks) * scale)
        dkv_ref[key_rows, cols] += tn(ds, stacked) * scale
        dkv_ref[key_rows, value_cols] += tn(low(probs), do_stacked)

    copies[1].wait()
    xe = jnp.concatenate([below_ref[...], x_ref[...], above_ref[...]], axis=0).astype(F32)
    plain = xe * rms_inverse(xe)
    left = low(nn(low(plain * gain_1), order))
    dk = low(dkv_ref[:, :features])
    dv = low(dkv_ref[:, features:])
    inner = slice(WIN, WIN + tokens)
    put(0, tn(left[inner], dq_ref[...]))
    put(features, tn(left, dk))
    put(2 * features, tn(left, dv))
    back = nt(dk, w_qkv[:, features : 2 * features]) + nt(dv, w_qkv[:, 2 * features :])
    own = back[inner] + nt(dq_ref[...], w_qkv[:, :features])
    halo_below_ref[...] = low(back[:WIN])
    halo_above_ref[...] = low(back[WIN + tokens :])
    gain_1_grad = gain_1_grad + jnp.sum(own * plain[inner], axis=0, keepdims=True)
    gain_1_grad = gain_1_grad + jnp.sum(back[:WIN] * plain[:WIN], axis=0, keepdims=True)
    gain_1_grad = gain_1_grad + jnp.sum(
        back[WIN + tokens :] * plain[WIN + tokens :], axis=0, keepdims=True
    )
    grad_normed_ref[...] = own + exact(pq_t_ref[...], q_back)
    rest = jnp.zeros((4, features), F32)
    small_grad_ref[...] = jnp.concatenate(
        [gain_1_grad, gain_2_grad, router_q, router_f, rest], axis=0
    )
    for both in started[-stage.shape[0] :]:
        for copy in both:
            copy.wait()


def heavy_backward(
    batch_n,
    meta,
    xq_ref,
    xk_ref,
    grad_raw_ref,
    q_ref,
    kv_ref,
    mixed_ref,
    small_ref,
    small_grad_ref,
    wx_ref,
    out_ref,
    order_ref,
    order_out_ref,
    backs_ref,
    send_ref,
    keep_ref,
):
    at = 0
    count = xq_ref.shape[0]
    keys = xk_ref.shape[0]
    features = wx_ref.shape[0]
    small = small_ref[...]
    gain_1 = small[0:1]
    place = pl.ds(pl.multiple_of(meta[6], count), count)
    grad_raw = grad_raw_ref[place]
    do = low(nt(grad_raw, out_ref[...]))
    masks = head_rows(LANES, DH)[: HH // PARTS]
    scale = DH ** (-0.5)
    bias = jnp.concatenate([heavy_bias(meta, count, keys)] * len(masks), axis=0)
    stacked = stack_heads(q_ref[...], masks)
    do_stacked = stack_heads(do, masks)
    probs = softmax(nt(stacked, kv_ref[:, :LANES]) * scale + bias)
    grad_probs = nt(do_stacked, kv_ref[:, LANES:])
    ds = low(probs * (grad_probs - row_sum(probs * grad_probs)))
    probs = low(probs)
    dq = low(merge_heads(nn(ds, kv_ref[:, :LANES]), masks) * scale)
    q_back = nt(dq, wx_ref[:, at : at + LANES])
    backs_ref[:, :features] = jnp.zeros((keys, features), BF)
    backs_ref[place, :features] = low(q_back)
    xq = xq_ref[...].astype(F32)
    q_plain = xq * rms_inverse(xq)
    order = order_ref[...]
    gain_1_grad = jnp.sum(q_back * q_plain, axis=0, keepdims=True)
    q_grads = tn(low(nn(low(q_plain * gain_1), order)), dq)
    router_k = None
    size = min(CHUNK, keys)
    for start in range(0, keys, size):
        rows = slice(start, start + size)
        xk = xk_ref[rows].astype(F32)
        k_plain = xk * rms_inverse(xk)
        k_norm = k_plain * gain_1
        k_low = low(k_norm)
        k_gate = sigmoid_dot(k_norm, small[3:4])
        dk = tn(ds[:, rows], stacked) * scale
        dv = tn(probs[:, rows], do_stacked)
        raw = nn(k_low, wx_ref[:, at + 2 * LANES : at + 3 * LANES])
        k_logit = row_sum(dv * raw) * k_gate * (1.0 - k_gate)
        grad_raw_k = low(jnp.concatenate([dk, dv * k_gate], axis=1))
        k_back = nt(grad_raw_k, wx_ref[:, at + LANES : at + 3 * LANES]) + k_logit * small[3:4]
        backs_ref[rows, features:] = low(k_back)
        one_router = jnp.sum(k_norm * k_logit, axis=0, keepdims=True)
        gain_1_grad = gain_1_grad + jnp.sum(k_back * k_plain, axis=0, keepdims=True)
        one_grads = tn(low(nn(k_low, order)), grad_raw_k)
        router_k = one_router if router_k is None else router_k + one_router
        kv_grads = one_grads if start == 0 else kv_grads + one_grads
    out_grads = low(tn(low(nn(mixed_ref[...], order_out_ref[...])), grad_raw))
    start_grads = small_grad_ref[...]
    vectors = [start_grads[0:1] + gain_1_grad, start_grads[1:2], start_grads[2:3], router_k]
    vectors += [start_grads[3:4], jnp.zeros((SMALL - 5, features), F32)]
    vectors = low(jnp.concatenate(vectors, axis=0))
    small_cols = low(jnp.transpose(nn(vectors, order)))
    upper = jnp.concatenate([low(q_grads), low(kv_grads), small_cols], axis=1)
    put_blocks(send_ref, keep_ref, batch_n, upper, out_grads[: HH * DH // PARTS])


def finish(
    x_ref,
    small_ref,
    grad_middle_ref,
    grad_normed_ref,
    from_below_ref,
    from_above_ref,
    backs_ref,
    pq_t_ref,
    pk_t_ref,
    pf_t_ref,
    middle_ref,
    light_ref,
    f_norm_ref,
    ffn_ref,
    output_ref,
    input_grad_ref,
):
    tokens, features = x_ref.shape
    routed = f_norm_ref.shape[0]
    small = small_ref[...]
    gate = sigmoid_dot(f_norm_ref[...], small[4:5])
    heavy = exact(pf_t_ref[...], sum_blocks(ffn_ref, routed) * gate)
    output_ref[...] = low(middle_ref[...] + light_ref[...] + heavy)
    backs = sum_blocks(backs_ref, routed)
    grad = grad_normed_ref[...] + exact(pq_t_ref[...], backs[:, :features])
    grad = grad + exact(pk_t_ref[...], backs[:, features:])
    below = from_below_ref[...].astype(F32)
    above = from_above_ref[...].astype(F32)
    grad = grad + jnp.concatenate([below, above], axis=0)
    x = x_ref[...].astype(F32)
    input_grad_ref[...] = grad_middle_ref[...] + rms_back(grad, x, rms_inverse(x), small[0:1])


def pair_sum(keep_ref, got_ref, send_out_ref, keep_out_ref):
    count = send_out_ref.shape[0]
    total = keep_ref[...].astype(F32) + got_ref[...].astype(F32)
    send_out_ref[...] = low(total[:count])
    keep_out_ref[...] = low(total[count:])


def sum_leading(ref, cols):
    total = ref[0, :, cols].astype(F32)
    for i in range(1, ref.shape[0]):
        total = total + ref[i, :, cols].astype(F32)
    return total


def pack_blocks(*refs):
    out = refs[-1]
    at = 0
    for ref in refs[:-1]:
        out[:, at : at + ref.shape[1]] = ref[...]
        at += ref.shape[1]


def call(kernel, args, memory, outs, scratch, flops, name, far=0):
    spaces = {"v": pltpu.VMEM, "s": pltpu.SMEM, "h": pl.ANY}
    return pl.pallas_call(
        kernel,
        out_shape=[jax.ShapeDtypeStruct(shape, kind) for shape, kind in outs],
        in_specs=[pl.BlockSpec(memory_space=spaces[one]) for one in memory],
        out_specs=[pl.BlockSpec(memory_space=pltpu.VMEM)] * (len(outs) - far)
        + [pl.BlockSpec(memory_space=pl.ANY)] * far,
        scratch_shapes=scratch,
        compiler_params=pltpu.CompilerParams(vmem_limit_bytes=VMEM_LIMIT),
        cost_estimate=pl.CostEstimate(flops=flops, bytes_accessed=20_000_000, transcendentals=0),
        name=name,
    )(*args)


def select_rows(rows, mask):
    blocks = rows.astype(F32).reshape(mask.shape[0], ROUTE, rows.shape[1])
    return jnp.sum(jnp.where(mask[:, :, None], blocks, 0.0), axis=1)


def shifted(block, axis, distance):
    devices = range(lax.axis_size(axis))
    route = [(i - distance, i) for i in devices if i - distance in devices]
    return lax.ppermute(block, axis, route)


def swapped(block, distance):
    return lax.ppermute(block, "batch", [(i, i ^ distance) for i in range(lax.axis_size("batch"))])


def exchange(blocks, axis):
    return lax.all_to_all(blocks, axis, 0, 0, tiled=True)


def spread_to_all(block, axis):
    count = lax.axis_size(axis)
    return exchange(jnp.broadcast_to(block[None], (count,) + block.shape), axis)


def presum(blocks):
    if blocks.shape[0] > 16:
        return jnp.sum(blocks.astype(F32), axis=0)
    return blocks.reshape(-1, blocks.shape[2])


def summed(blocks, axis):
    return jnp.sum(exchange(blocks, axis).astype(F32), axis=0)


def pack_rows(down, rows):
    width = down.shape[1] * (down.shape[0] - rows) // rows
    rest = down[rows:]
    pieces = [rest[:, i : i + width] for i in range(0, down.shape[1], width)]
    return jnp.concatenate([down[:rows], jnp.concatenate(pieces, axis=0)], axis=1)


def halves_summed(keep, got, height, width):
    count = height // 2
    steps = width // 128
    block = 128 * max(i for i in range(1, 7) if steps % i == 0)
    rows_in = pl.BlockSpec((height, block), lambda i: (0, i))
    rows_out = pl.BlockSpec((count, block), lambda i: (0, i))
    return pl.pallas_call(
        pair_sum,
        grid=(width // block,),
        out_shape=[jax.ShapeDtypeStruct((count, width), BF)] * 2,
        in_specs=[rows_in] * 2,
        out_specs=[rows_out] * 2,
        compiler_params=pltpu.CompilerParams(vmem_limit_bytes=VMEM_LIMIT),
        cost_estimate=pl.CostEstimate(
            flops=height * width, bytes_accessed=6 * height * width, transcendentals=0
        ),
        name="pair_sum",
    )(keep, got)


def batch_summed(send, keep):
    height, width = keep.shape
    send, keep = halves_summed(keep, swapped(send, 1), height, width)
    return low(keep.astype(F32) + swapped(send, 2).astype(F32))


def canonical(piece, core, pair):
    other = swapped(piece, 2)
    piece = jnp.where(pair == 0, jnp.stack([piece, other]), jnp.stack([other, piece]))
    other = swapped(piece, 1)
    piece = jnp.where(core == 0, jnp.stack([piece, other], 1), jnp.stack([other, piece], 1))
    return piece.reshape((4,) + piece.shape[2:])


def unpack_rows(packed, features):
    rows = packed.shape[0]
    width = packed.shape[1] - features
    count = features // width
    rest = packed[:, features:].reshape(count, rows // count, width)
    rest = jnp.concatenate([rest[i] for i in range(count)], axis=1)
    return jnp.concatenate([packed[:, :features], rest], axis=0)


def pad_cols(block, width):
    return jnp.pad(block, ((0, 0), (0, width - block.shape[1])))


def order_matrix(order):
    size = order.shape[0]
    return low((lax.broadcasted_iota(jnp.int32, (size, size), 0) == order[None, :]).astype(F32))


def other_first(index, axis, own):
    flipped = np.flip(index, axis)
    return jnp.where(own == 0, jnp.asarray(flipped), jnp.asarray(index))


def local(
    layer_input,
    cotangent,
    doc_lengths,
    routes,
    norm_gains,
    router,
    light_qkv,
    light_out,
    heavy_qkv,
    heavy_out,
    light_in,
    light_down,
    heavy_in,
    heavy_down,
):
    seq_n = lax.axis_size("seq")
    batch_n = lax.axis_size("batch")
    devices = seq_n * batch_n
    rows = light_qkv.shape[0]
    x = layer_input[0]
    g = cotangent[0]
    tokens, features = x.shape
    routed = tokens // ROUTE
    keys = routed * seq_n
    wide = light_qkv.shape[1]
    seq = lax.axis_index("seq")
    own = lax.axis_index("batch")
    core, pair = own % 2, own // 2
    offset = seq * tokens

    small = pad_cols(jnp.concatenate([norm_gains, router], axis=1), SMALL)
    sources = [
        ("light_qkv", light_qkv),
        ("light_out", light_out),
        ("light_in", light_in),
        ("light_down", pack_rows(light_down, rows)),
    ]
    layout = {}
    at = 0
    for name, block in sources:
        layout[name] = (at, at + block.shape[1])
        at += block.shape[1]
    packed = call(
        pack_blocks,
        [block for _, block in sources],
        "v" * len(sources),
        [((rows, at), BF)],
        [],
        1_000_000,
        "pack",
    )[0]
    full = lax.all_gather(packed, BOTH, axis=0, tiled=True)

    masks = [
        lax.broadcasted_iota(jnp.int32, (routed, ROUTE), 1) == routes[i, 0][:, None]
        for i in range(3)
    ]
    xq = low(select_rows(x, masks[0]))
    xk = low(select_rows(x, masks[1]))
    t = low(select_rows(g, masks[2]))
    query_parts = seq_n // PARTS
    count = keys // query_parts
    part = seq // query_parts
    query_first = (seq % query_parts) * count
    head_width = features // PARTS
    head_all = 3 * LANES + SMALL
    hidden = heavy_in.shape[1] // 2 // seq_n
    in_rows = features // batch_n
    every = lambda block: jnp.broadcast_to(block[None], (seq_n,) + block.shape)
    tall = lambda blocks: jnp.pad(blocks, ((0, 0), (0, routed - rows), (0, 0)))
    head_cols = heavy_qkv.reshape(rows, 3, PARTS, head_width)
    head_cols = jnp.pad(head_cols, ((0, 0), (0, 0), (0, 0), (0, LANES - head_width)))
    head_cols = head_cols.transpose(2, 0, 1, 3).reshape(PARTS, rows, 3 * LANES)
    head_cols = jnp.repeat(head_cols, query_parts, axis=0)
    head_cols = jnp.concatenate([head_cols, every(small)], axis=2)
    sent = jnp.concatenate([every(jnp.concatenate([xq, xk], axis=1)), tall(head_cols)], axis=2)
    travel = exchange(sent, "seq")
    in_cols = heavy_in.reshape(rows, 2, seq_n, hidden).transpose(2, 0, 1, 3)
    in_cols = in_cols.reshape(seq_n, rows, 2 * hidden)
    late = exchange(jnp.concatenate([every(t), tall(in_cols)], axis=2), "seq")
    if query_parts == 2:
        other = lax.ppermute(heavy_out, "seq", [(i, i ^ 1) for i in range(seq_n)])
        out_rows = jnp.where(
            seq % 2 == 0, jnp.stack([heavy_out, other]), jnp.stack([other, heavy_out])
        )
    else:
        groups = [list(range(i, i + query_parts)) for i in range(0, seq_n, query_parts)]
        out_rows = jnp.broadcast_to(heavy_out[None], (query_parts,) + heavy_out.shape)
        out_rows = lax.all_to_all(out_rows, "seq", 0, 0, tiled=True, axis_index_groups=groups)
    out_count = query_parts * rows
    out_rows = pad_cols(out_rows.reshape(out_count, features), head_all)
    piece = travel[:, :rows, 2 * features :].reshape(in_rows, head_all)
    piece = canonical(jnp.concatenate([piece, out_rows], axis=0), core, pair)
    index = np.arange(features).reshape(seq_n, 2, 2, rows)
    order_h = order_matrix(jnp.asarray(index.transpose(1, 2, 0, 3).reshape(-1)))
    wx = low(nn(order_h, piece[:, :in_rows].reshape(features, head_all)))
    h_out = piece[:, in_rows:, :features].reshape(batch_n, query_parts, rows, features)
    h_out = h_out.transpose(1, 0, 2, 3).reshape(head_width, features)
    h_out = jnp.pad(h_out, ((0, LANES - head_width), (0, 0)))
    pack_width = max(2 * hidden, features)
    piece = late[:, :rows, features:].reshape(in_rows, 2 * hidden)
    piece = [pad_cols(piece, pack_width), pad_cols(heavy_down, pack_width)]
    piece = canonical(jnp.concatenate(piece, axis=0), core, pair)
    h_in = low(nn(order_h, piece[:, :in_rows, : 2 * hidden].reshape(features, 2 * hidden)))
    h_down = piece[:, in_rows:, :features].reshape(hidden, features)
    t_all = late[:, :, :features].reshape(keys, features)
    below = shifted(x[tokens - WIN :], "seq", 1)
    above = shifted(x[:WIN], "seq", -1)

    def relative(array):
        array = jnp.where(core == 0, np.flip(array, 0), array)
        return jnp.where(pair == 0, jnp.flip(array, 1), array).reshape(-1)

    order = order_matrix(relative(index.transpose(2, 1, 0, 3)))
    units = np.arange(hidden).reshape(2, 2, -1)
    order_units = order_matrix(relative(units.transpose(1, 0, 2)))
    out_index = np.arange(head_width).reshape(query_parts, 2, 2, rows)
    out_index = relative(out_index.transpose(2, 1, 0, 3))
    rest = jnp.arange(head_width, LANES, dtype=out_index.dtype)
    order_out = order_matrix(jnp.concatenate([out_index, rest]))
    ends = jnp.cumsum(doc_lengths[0])
    meta = jnp.stack([ends[0], ends[1], ends[2], ends[3], offset, tokens * seq_n, query_first])
    meta = meta.astype(jnp.int32)
    place = lax.broadcasted_iota(jnp.int32, (routed, tokens), 1)
    first = lax.broadcasted_iota(jnp.int32, (routed, tokens), 0) * ROUTE
    picks = [(place == first + routes[i, 0][:, None]).astype(F32) for i in range(3)]
    place_t = lax.broadcasted_iota(jnp.int32, (tokens, routed), 0)
    first_t = lax.broadcasted_iota(jnp.int32, (tokens, routed), 1) * ROUTE
    picks_t = [(place_t == first_t + routes[i, 0][None, :]).astype(F32) for i in range(3)]

    xq_all = travel[:, :, :features].reshape(keys, features)
    xq_part = lax.dynamic_slice_in_dim(xq_all, query_first, count, 0)
    xk_all = travel[:, :, features : 2 * features].reshape(keys, features)
    raw, heavy_q, heavy_kv, heavy_mixed, small_rows = call(
        heavy_forward,
        (meta, xq_part, xk_all, wx, h_out),
        "svvvv",
        [
            ((keys, features), BF),
            ((count, LANES), BF),
            ((keys, 2 * LANES), BF),
            ((count, LANES), BF),
            ((8, features), F32),
        ],
        [],
        2_000_000_000,
        "heavy_forward",
    )
    raw = presum(exchange(raw.reshape(seq_n, routed, features), "seq"))

    weight = lambda columns: pltpu.VMEM((features, columns), BF)
    q, kv, mixed, heavy_raw, middle, normed2, f_norm, f_sent = call(
        functools.partial(light_forward, layout),
        (meta, below, x, above, xq, raw, picks_t[0], picks[2], small_rows, full),
        "svvvvvvvvh",
        [
            ((tokens, features), BF),
            ((tokens + 2 * WIN, 2 * features), BF),
            ((tokens, features), BF),
            ((routed, features), F32),
            ((tokens, features), F32),
            ((tokens, features), BF),
            ((routed, features), F32),
            ((keys, features + SMALL), BF),
        ],
        [weight(wide), weight(features), pltpu.SemaphoreType.DMA((2,))],
        8_000_000_000,
        "light_forward",
    )
    f_sent = exchange(f_sent.reshape(seq_n, routed, features + SMALL), "seq")
    light_hidden = light_in.shape[1] // 2
    down_width = layout["light_down"][1] - layout["light_down"][0]
    half = features // 2
    ffn_width = light_in.shape[1] + down_width
    ffn, grad_n2, light_send, light_keep = call(
        functools.partial(light_ffn, layout, devices),
        (normed2, g, order, full),
        "vvvh",
        [
            ((tokens, features), F32),
            ((tokens, features), F32),
            ((half, ffn_width), BF),
            ((half, ffn_width), BF),
        ],
        [
            weight(light_in.shape[1]),
            weight(down_width),
            pltpu.VMEM((light_hidden, features), BF),
            pltpu.VMEM((features, down_width), F32),
            weight(down_width),
            pltpu.SemaphoreType.DMA((2,)),
        ],
        8_000_000_000,
        "light_ffn",
    )
    down_rows = hidden // batch_n
    back, ffn_part, ffn_send, ffn_keep = call(
        functools.partial(heavy_ffn, batch_n),
        (f_sent.reshape(keys, features + SMALL), t_all, h_in, h_down, order, order_units),
        "vvvvvv",
        [
            ((keys, features + SMALL), BF),
            ((keys, features), BF),
            ((batch_n // 2 * (in_rows + down_rows), pack_width), BF),
            ((batch_n // 2 * (in_rows + down_rows), pack_width), BF),
        ],
        [],
        4_000_000_000,
        "heavy_ffn",
    )
    back = presum(exchange(back.reshape(seq_n, routed, features + SMALL), "seq"))

    ffn_total = batch_summed(ffn_send, ffn_keep)
    light_total = batch_summed(light_send, light_keep)
    ffn_rows = ffn_total[:in_rows, : 2 * hidden].reshape(seq_n, rows, 2 * hidden)
    light_rows = light_total.reshape(seq_n, rows, ffn_width)
    ffn_rows = exchange(jnp.concatenate([light_rows, ffn_rows], axis=2), "seq").astype(F32)
    grad_h_down = ffn_total[in_rows:, :features].astype(F32)
    grad_h_in = ffn_rows[:, :, ffn_width:].reshape(seq_n, rows, 2, hidden).transpose(1, 2, 0, 3)
    grad_h_in = grad_h_in.reshape(rows, 2 * hidden * seq_n)
    shard_f = jnp.sum(ffn_rows[:, :, :ffn_width], axis=0)

    (
        grad_middle,
        grad_normed,
        halo_below,
        halo_above,
        grad_raw,
        small_grad,
        light_send,
        light_keep,
    ) = call(
        functools.partial(light_backward, layout),
        (
            meta,
            below,
            x,
            above,
            xq,
            picks[0],
            picks_t[0],
            picks_t[2],
            g,
            order,
            q,
            kv,
            mixed,
            heavy_raw,
            middle,
            f_norm,
            small_rows,
            grad_n2,
            back,
            full,
        ),
        "s" + "v" * 18 + "h",
        [
            ((tokens, features), F32),
            ((tokens, features), F32),
            ((WIN, features), BF),
            ((WIN, features), BF),
            ((keys, features), BF),
            ((8, features), F32),
            ((half, wide + features), BF),
            ((half, wide + features), BF),
        ],
        [
            weight(wide),
            weight(features),
            pltpu.VMEM((tokens, features), BF),
            pltpu.VMEM((tokens + 2 * WIN, 2 * features), F32),
            pltpu.VMEM((3, features, features), BF),
            pltpu.SemaphoreType.DMA((2,)),
            pltpu.SemaphoreType.DMA((3, 2)),
        ],
        16_000_000_000,
        "light_backward",
        2,
    )

    light_total = batch_summed(light_send, light_keep)

    both = jnp.concatenate([grad_raw, ffn_part], axis=1).reshape(seq_n, routed, 2 * features)
    both = exchange(both, "seq")
    grad_raw = both[:, :, :features].reshape(keys, features)
    ffn_part = presum(both[:, :, features:])
    head_rows_n = head_width // batch_n
    backs, head_send, head_keep = call(
        functools.partial(heavy_backward, batch_n),
        (
            meta,
            xq_part,
            xk_all,
            grad_raw,
            heavy_q,
            heavy_kv,
            heavy_mixed,
            small_rows,
            small_grad,
            wx,
            h_out,
            order,
            order_out,
        ),
        "s" + "v" * 12,
        [
            ((keys, 2 * features), BF),
            ((batch_n // 2 * (in_rows + head_rows_n), head_all), BF),
            ((batch_n // 2 * (in_rows + head_rows_n), head_all), BF),
        ],
        [],
        4_000_000_000,
        "heavy_backward",
    )
    backs = presum(exchange(backs.reshape(seq_n, routed, 2 * features), "seq"))

    head_total = batch_summed(head_send, head_keep)
    out_grads = head_total[in_rows:, :features].reshape(query_parts, rows, features)
    out_grads = lax.dynamic_update_slice(
        jnp.zeros((seq_n, rows, features), BF), out_grads, (part * query_parts, 0, 0)
    )
    light_width = wide + features
    total = jnp.concatenate(
        [
            light_total.reshape(seq_n, rows, light_width),
            head_total[:in_rows].reshape(seq_n, rows, head_all),
            out_grads,
        ],
        axis=2,
    )
    total = exchange(total, "seq").astype(F32)
    grad_light = jnp.sum(total[:, :, :light_width], axis=0)
    head_grads = total[:, :, light_width:]
    grad_heavy_out = jnp.sum(head_grads[:, :, head_all:], axis=0)
    grad_small = jnp.sum(head_grads[:, :, 3 * LANES : head_all], axis=0)
    grad_heads = head_grads[:, :, : 3 * LANES].reshape(PARTS, query_parts, rows, 3, LANES)
    grad_heads = jnp.sum(grad_heads, axis=1)[:, :, :, :head_width]
    grad_heads = grad_heads.transpose(1, 2, 0, 3).reshape(rows, wide)

    from_above = shifted(halo_below, "seq", -1)
    from_below = shifted(halo_above, "seq", 1)
    output, input_grad = call(
        finish,
        (
            x,
            small_rows,
            grad_middle,
            grad_normed,
            from_below,
            from_above,
            backs,
            picks_t[0],
            picks_t[1],
            picks_t[2],
            middle,
            ffn,
            f_norm,
            ffn_part,
        ),
        "v" * 14,
        [((tokens, features), BF), ((tokens, features), F32)],
        [],
        1_000_000_000,
        "finish",
    )
    return (
        output[None],
        input_grad[None],
        grad_small[:, :2],
        grad_small[:, 2:5],
        grad_light[:, :wide],
        grad_light[:, wide:],
        grad_heads,
        grad_heavy_out,
        shard_f[:, : light_in.shape[1]],
        unpack_rows(shard_f[:, light_in.shape[1] :], features),
        grad_h_in,
        grad_h_down,
    )


def solution(mesh):
    weight = P(BOTH, None)
    rows = P("batch", "seq", None)
    return jax.shard_map(
        local,
        mesh=mesh,
        in_specs=(rows, rows, P("batch", None), P(None, "batch", "seq")) + (weight,) * 10,
        out_specs=(rows, rows) + (weight,) * 10,
        check_vma=False,
    )
```

```python
import functools

import jax
import jax.numpy as jnp
import numpy as np
from jax import lax
from jax.experimental import pallas as pl
from jax.experimental.pallas import tpu as pltpu
from jax.sharding import PartitionSpec as P

HL = 8
DL = 96
HH = 12
DH = 64
WIN = 128
ROUTE = 8
SMALL = 128
CHUNK = 256
PARTS = 4
LANES = 256
EPS = 1e-06
BF = jnp.bfloat16
F32 = jnp.float32
BOTH = ("seq", "batch")
highest = lax.Precision.HIGHEST
VMEM_LIMIT = 60 * 1024 * 1024


def nn(left, right):
    return jnp.dot(left, right, preferred_element_type=F32)


def nt(left, right):
    return lax.dot_general(left, right, (((1,), (1,)), ((), ())), preferred_element_type=F32)


def tn(left, right):
    return lax.dot_general(left, right, (((0,), (0,)), ((), ())), preferred_element_type=F32)


def exact(left, right):
    return jnp.dot(left, right, precision=highest, preferred_element_type=F32)


def low(values):
    return values.astype(BF)


def row_sum(values):
    return jnp.sum(values, axis=-1, keepdims=True)


def rms_inverse(values):
    return lax.rsqrt(jnp.mean(values * values, axis=-1, keepdims=True) + EPS)


def rms_back(grad, values, inverse, gain):
    scaled = grad * gain
    inner = jnp.mean(scaled * values, axis=-1, keepdims=True)
    return inverse * scaled - values * (inverse * inverse * inverse * inner)


def geglu_parts(pair):
    half = pair.shape[-1] // 2
    u = pair[:, :half]
    up = pair[:, half:]
    c = 0.7978845608028654
    t = jnp.tanh(c * (u + 0.044715 * (u * u * u)))
    gelu = 0.5 * u * (1.0 + t)
    slope = 0.5 * (1.0 + t) + 0.5 * u * (1.0 - t * t) * (c * (1.0 + 3.0 * 0.044715 * (u * u)))
    return gelu, slope, up


def documents(positions, meta):
    found = (positions >= meta[0]).astype(jnp.int32)
    for i in range(1, 4):
        found = found + (positions >= meta[i]).astype(jnp.int32)
    return found


def head_rows(width, size):
    lanes = lax.broadcasted_iota(jnp.int32, (1, width), 1)
    inside = [(lanes >= i * size) & (lanes < (i + 1) * size) for i in range(width // size)]
    return [jnp.where(one, 1.0, 0.0) for one in inside]


def stack_heads(rows, masks):
    return jnp.concatenate([rows * low(mask) for mask in masks], axis=0)


def merge_heads(stacked, masks):
    count = stacked.shape[0] // len(masks)
    total = stacked[:count] * masks[0]
    for i in range(1, len(masks)):
        total = total + stacked[i * count : (i + 1) * count] * masks[i]
    return total


def softmax(scores):
    weights = jnp.exp(scores - jnp.max(scores, axis=-1, keepdims=True))
    return weights * (1.0 / row_sum(weights))


def light_bias(meta, block, tokens):
    query = meta[4] + block * WIN + lax.broadcasted_iota(jnp.int32, (WIN, 1), 0)
    key = meta[4] + (block - 1) * WIN + lax.broadcasted_iota(jnp.int32, (1, 3 * WIN), 1)
    key_doc = jnp.where((key >= 0) & (key < meta[5]), documents(key, meta), -1)
    seen = (jnp.abs(query - key) < WIN) & (documents(query, meta) == key_doc)
    return jnp.where(seen, 0.0, -1e30)


def heavy_bias(meta, count, keys):
    query = (meta[6] + lax.broadcasted_iota(jnp.int32, (count, 1), 0)) * ROUTE
    key = lax.broadcasted_iota(jnp.int32, (1, keys), 1) * ROUTE
    return jnp.where(documents(query, meta) == documents(key, meta), 0.0, -1e30)


def light_units(tokens):
    return [(block, part) for block in range(tokens // WIN) for part in range(2)]


def sigmoid_dot(rows, vector):
    return jax.nn.sigmoid(row_sum(rows * vector))


def load(full_ref, places, sems):
    copies = []
    for i, ((first, last), buffer) in enumerate(places):
        copies.append(pltpu.make_async_copy(full_ref.at[:, first:last], buffer, sems.at[i]))
        copies[-1].start()
    return copies


def two_lanes(column):
    lanes = lax.broadcasted_iota(jnp.int32, (column.shape[0], SMALL), 1)
    high = low(column).astype(F32)
    return low(jnp.where(lanes == 0, high, jnp.where(lanes == 1, column - high, 0.0)))


def from_two_lanes(block):
    lanes = lax.broadcasted_iota(jnp.int32, block.shape, 1)
    return row_sum(jnp.where(lanes < 2, block.astype(F32), 0.0))


def sum_blocks(ref, count, cols=slice(None)):
    total = ref[0:count, cols].astype(F32)
    for i in range(1, ref.shape[0] // count):
        total = total + ref[i * count : (i + 1) * count, cols].astype(F32)
    return total


def heavy_forward(
    meta,
    xq_ref,
    xk_ref,
    wx_ref,
    out_ref,
    raw_ref,
    q_ref,
    kv_ref,
    mixed_ref,
    small_ref,
):
    count = xq_ref.shape[0]
    keys = xk_ref.shape[0]
    at = 0
    small = jnp.transpose(wx_ref[:, 3 * LANES :].astype(F32))[:8]
    small_ref[...] = small
    gain_1 = small[0:1]
    xq = xq_ref[...].astype(F32)
    q_norm = xq * rms_inverse(xq) * gain_1
    q_ref[...] = low(nn(low(q_norm), wx_ref[:, at : at + LANES]))
    size = min(CHUNK, keys)
    for start in range(0, keys, size):
        xk = xk_ref[start : start + size].astype(F32)
        k_norm = xk * rms_inverse(xk) * gain_1
        k_gate = sigmoid_dot(k_norm, small[3:4])
        raw = nn(low(k_norm), wx_ref[:, at + LANES : at + 3 * LANES])
        kv_ref[start : start + size, :LANES] = low(raw[:, :LANES])
        kv_ref[start : start + size, LANES:] = low(raw[:, LANES:] * k_gate)
    masks = head_rows(LANES, DH)[: HH // PARTS]
    bias = jnp.concatenate([heavy_bias(meta, count, keys)] * len(masks), axis=0)
    stacked = stack_heads(q_ref[...], masks)
    probs = softmax(nt(stacked, kv_ref[:, :LANES]) * DH ** (-0.5) + bias)
    mixed = low(merge_heads(nn(low(probs), kv_ref[:, LANES:]), masks))
    mixed_ref[...] = mixed
    raw_ref[...] = low(nn(mixed, out_ref[...]))


def light_forward(
    layout,
    meta,
    below_ref,
    x_ref,
    above_ref,
    xq_ref,
    raw_ref,
    pq_t_ref,
    pf_ref,
    small_ref,
    full_ref,
    q_ref,
    kv_ref,
    mixed_ref,
    heavy_raw_ref,
    middle_ref,
    normed2_ref,
    f_norm_ref,
    f_sent_ref,
    w_qkv,
    w_lo,
    sems,
):
    tokens, features = x_ref.shape
    routed = xq_ref.shape[0]
    copies = load(full_ref, [(layout["light_qkv"], w_qkv), (layout["light_out"], w_lo)], sems)
    small = small_ref[...]
    gain_1, gain_2 = small[0:1], small[1:2]
    xe = jnp.concatenate([below_ref[...], x_ref[...], above_ref[...]], axis=0).astype(F32)
    ne = low(xe * rms_inverse(xe) * gain_1)
    xq = xq_ref[...].astype(F32)
    q_gate = sigmoid_dot(xq * rms_inverse(xq) * gain_1, small[2:3])
    heavy_raw = sum_blocks(raw_ref, routed)
    heavy_raw_ref[...] = heavy_raw
    base = x_ref[...].astype(F32) + exact(pq_t_ref[...], heavy_raw * q_gate)
    copies[0].wait()
    q_ref[...] = low(nn(ne[WIN : WIN + tokens], w_qkv[:, :features]))
    kv_ref[...] = low(nn(ne, w_qkv[:, features:]))
    width = features // 2
    masks = head_rows(width, DL)
    scale = DL ** (-0.5)
    for block, part in light_units(tokens):
        cols = slice(part * width, (part + 1) * width)
        rows = slice(block * WIN, (block + 1) * WIN)
        key_rows = slice(block * WIN, (block + 3) * WIN)
        bias = jnp.concatenate([light_bias(meta, block, tokens)] * len(masks), axis=0)
        stacked = stack_heads(q_ref[rows, cols], masks)
        probs = softmax(nt(stacked, kv_ref[key_rows, cols]) * scale + bias)
        values = kv_ref[key_rows, features + part * width : features + (part + 1) * width]
        mixed_ref[rows, cols] = low(merge_heads(nn(low(probs), values), masks))
    copies[1].wait()
    middle = base + nn(mixed_ref[...], w_lo[...])
    middle_ref[...] = middle
    normed2 = middle * rms_inverse(middle) * gain_2
    normed2_ref[...] = low(normed2)
    f_norm = exact(pf_ref[...], normed2)
    f_norm_ref[...] = f_norm
    sent = jnp.concatenate([low(f_norm), two_lanes(sigmoid_dot(f_norm, small[4:5]))], axis=1)
    for i in range(f_sent_ref.shape[0] // routed):
        f_sent_ref[i * routed : (i + 1) * routed] = sent


def unpack_down(packed, down_ref, work_ref, devices):
    features = down_ref.shape[1]
    rows = packed.shape[0] // devices
    more = down_ref.shape[0] // devices - rows
    width = packed.shape[1] - features
    if rows % 8 == 0 and more % 8 == 0:
        work_ref[...] = packed.astype(F32)
        for i in range(devices):
            own = work_ref[i * rows : (i + 1) * rows, :features]
            parts = [
                work_ref[i * rows + j * more : i * rows + (j + 1) * more, features:]
                for j in range(rows // more)
            ]
            whole = jnp.concatenate([own, jnp.concatenate(parts, axis=1)], axis=0)
            down_ref[i * (rows + more) : (i + 1) * (rows + more)] = low(whole)
    else:
        for j in range(rows // more):
            cols = slice(j * width, (j + 1) * width)
            first, second = down_places(down_ref.shape[0], packed.shape[0], rows, more, j)
            down_ref[:, cols] = low(nn(first, packed[:, cols]) + nn(second, packed[:, features:]))


def down_places(units, packed_rows, rows, more, j):
    unit = lax.broadcasted_iota(jnp.int32, (units, packed_rows), 0)
    row = lax.broadcasted_iota(jnp.int32, (units, packed_rows), 1)
    total = rows + more
    device, inner = unit // total, unit % total
    first = (inner < rows) & (row == device * rows + inner)
    second = (inner >= rows) & (row == device * rows + j * more + inner - rows)
    return low(jnp.where(first, 1.0, 0.0)), low(jnp.where(second, 1.0, 0.0))


def pack_down(grad, out_ref, at, devices, rows):
    features = grad.shape[1]
    more = grad.shape[0] // devices - rows
    width = features * more // rows
    if rows % 8 == 0 and more % 8 == 0:
        pieces = []
        for i in range(devices):
            start = i * (rows + more)
            rest = grad[start + rows : start + rows + more]
            parts = [rest[:, j * width : (j + 1) * width] for j in range(rows // more)]
            pieces.append(
                jnp.concatenate([grad[start : start + rows], jnp.concatenate(parts, axis=0)], axis=1)
            )
        out_ref[:, at:] = low(jnp.concatenate(pieces, axis=0))
    else:
        total = None
        for j in range(rows // more):
            cols = slice(j * width, (j + 1) * width)
            first, second = down_places(grad.shape[0], devices * rows, rows, more, j)
            block = low(grad[:, cols])
            out_ref[:, at + j * width : at + (j + 1) * width] = low(tn(first, block))
            part = tn(second, block)
            total = part if total is None else total + part
        out_ref[:, at + features :] = low(total)


def light_ffn(
    layout,
    devices,
    normed2_ref,
    g_ref,
    order_ref,
    full_ref,
    ffn_ref,
    grad_ref,
    send_ref,
    keep_ref,
    w_in,
    w_packed,
    w_down,
    work_ref,
    pack_ref,
    sems,
):
    features = normed2_ref.shape[1]
    half = features // 2
    order = order_ref[...]
    copies = []
    for i, (name, buffer) in enumerate([("light_in", w_in), ("light_down", w_packed)]):
        first, last = layout[name]
        copy = pltpu.make_async_copy(full_ref.at[:, first:last], buffer, sems.at[i])
        copy.start()
        copies.append(copy)
    copies[0].wait()
    copies[1].wait()
    unpack_down(w_packed[...], w_down, work_ref, devices)
    gelu, slope, up = geglu_parts(nn(normed2_ref[...], w_in[...]))
    hidden = low(gelu * up)
    ffn_ref[...] = nn(hidden, w_down[...])
    grad_hidden = nt(g_ref[...], w_down[...])
    grad_pair = low(jnp.concatenate([grad_hidden * up * slope, grad_hidden * gelu], axis=1))
    grad_ref[...] = nt(grad_pair, w_in[...])
    wide = w_in.shape[1]
    left = low(nn(normed2_ref[...], order))
    for at in range(0, wide, 512):
        block = low(tn(left, grad_pair[:, at : at + 512]))
        send_ref[:, at : at + 512] = block[:half]
        keep_ref[:, at : at + 512] = block[half:]
    pack_down(tn(hidden, g_ref[...]), pack_ref, 0, devices, features // devices)
    block = low(tn(order, pack_ref[...]))
    send_ref[:, wide:] = block[:half]
    keep_ref[:, wide:] = block[half:]


def heavy_ffn(
    batch_n,
    sent_ref,
    t_ref,
    in_ref,
    down_ref,
    order_ref,
    order_units_ref,
    back_ref,
    ffn_ref,
    send_ref,
    keep_ref,
):
    features = in_ref.shape[0]
    hidden_n = down_ref.shape[0]
    w_in = in_ref[...]
    f_in = sent_ref[:, :features]
    gate = from_two_lanes(sent_ref[:, features:])
    t = t_ref[...].astype(F32)
    grad_ffn = low(t * gate)
    gelu, slope, up = geglu_parts(nn(f_in, w_in))
    hidden = low(gelu * up)
    ffn = nn(hidden, down_ref[...])
    ffn_ref[...] = low(ffn)
    grad_hidden = nt(grad_ffn, down_ref[...])
    grad_pair = low(jnp.concatenate([grad_hidden * up * slope, grad_hidden * gelu], axis=1))
    back_ref[:, :features] = low(nt(grad_pair, w_in))
    back_ref[:, features:] = two_lanes(row_sum(t * ffn))
    grad_in = low(tn(low(nn(f_in, order_ref[...])), grad_pair))
    grad_down = low(tn(low(nn(hidden, order_units_ref[...])), grad_ffn))
    put_blocks(send_ref, keep_ref, batch_n, grad_in, grad_down)


def put_blocks(send_ref, keep_ref, batch_n, upper, lower):
    upper_rows = upper.shape[0] // batch_n
    lower_rows = lower.shape[0] // batch_n
    total = upper_rows + lower_rows
    width = send_ref.shape[1]
    for i in range(batch_n):
        ref = send_ref if i < batch_n // 2 else keep_ref
        start = i % (batch_n // 2) * total
        places = [(start, upper_rows, upper), (start + upper_rows, lower_rows, lower)]
        for first, count, values in places:
            ref[first : first + count, : values.shape[1]] = values[i * count : (i + 1) * count]
            if values.shape[1] < width:
                ref[first : first + count, values.shape[1] :] = jnp.zeros(
                    (count, width - values.shape[1]), BF
                )


def light_backward(
    layout,
    meta,
    below_ref,
    x_ref,
    above_ref,
    xq_ref,
    pq_ref,
    pq_t_ref,
    pf_t_ref,
    g_ref,
    order_ref,
    q_ref,
    kv_ref,
    mixed_ref,
    heavy_raw_ref,
    middle_ref,
    f_norm_ref,
    small_ref,
    grad_n2_ref,
    back_ref,
    full_ref,
    grad_middle_ref,
    grad_normed_ref,
    halo_below_ref,
    halo_above_ref,
    grad_raw_ref,
    small_grad_ref,
    send_ref,
    keep_ref,
    w_qkv,
    w_lo,
    dq_ref,
    dkv_ref,
    stage,
    sems,
    out_sems,
):
    tokens, features = x_ref.shape
    routed = xq_ref.shape[0]
    half = features // 2
    copies = load(full_ref, [(layout["light_out"], w_lo), (layout["light_qkv"], w_qkv)], sems)
    small = small_ref[...]
    gain_1, gain_2 = small[0:1], small[1:2]
    started = []

    def put(at, grad):
        width = grad.shape[1]
        slot = len(started) % stage.shape[0]
        if len(started) >= stage.shape[0]:
            for copy in started[-stage.shape[0]]:
                copy.wait()
        stage[slot, :, :width] = low(grad)
        both = []
        for i, ref in enumerate((send_ref, keep_ref)):
            source = stage.at[slot, i * half : (i + 1) * half, :width]
            both.append(
                pltpu.make_async_copy(source, ref.at[:, at : at + width], out_sems.at[slot, i])
            )
            both[-1].start()
        started.append(both)

    sums = sum_blocks(back_ref, routed)
    f_norm = f_norm_ref[...]
    f_gate = sigmoid_dot(f_norm, small[4:5])
    f_logit = (sums[:, features : features + 1] + sums[:, features + 1 : features + 2]) * (
        f_gate * (1.0 - f_gate)
    )
    router_f = jnp.sum(f_norm * f_logit, axis=0, keepdims=True)
    f_back = sums[:, :features] + f_logit * small[4:5]
    middle = middle_ref[...]
    grad_n2 = grad_n2_ref[...] + exact(pf_t_ref[...], f_back)
    inverse_2 = rms_inverse(middle)
    gain_2_grad = jnp.sum(grad_n2 * (middle * inverse_2), axis=0, keepdims=True)
    grad_middle = g_ref[...].astype(F32) + rms_back(grad_n2, middle, inverse_2, gain_2)
    grad_middle_ref[...] = grad_middle
    middle_low = low(grad_middle)

    q_rows = exact(pq_ref[...], grad_middle)
    xq = xq_ref[...].astype(F32)
    q_plain = xq * rms_inverse(xq)
    q_norm = q_plain * gain_1
    q_gate = sigmoid_dot(q_norm, small[2:3])
    grad_raw = low(q_rows * q_gate)
    grad_raw_ref[...] = grad_raw
    q_logit = row_sum(q_rows * heavy_raw_ref[...]) * q_gate * (1.0 - q_gate)
    q_back = q_logit * small[2:3]
    router_q = jnp.sum(q_norm * q_logit, axis=0, keepdims=True)
    gain_1_grad = jnp.sum(q_back * q_plain, axis=0, keepdims=True)

    copies[0].wait()
    order = order_ref[...]
    put(3 * features, tn(low(nn(mixed_ref[...], order)), middle_low))
    do = low(nt(middle_low, w_lo[...]))
    width = features // 2
    masks = head_rows(width, DL)
    scale = DL ** (-0.5)
    dkv_ref[...] = jnp.zeros_like(dkv_ref)
    for block, part in light_units(tokens):
        cols = slice(part * width, (part + 1) * width)
        value_cols = slice(features + part * width, features + (part + 1) * width)
        rows = slice(block * WIN, (block + 1) * WIN)
        key_rows = slice(block * WIN, (block + 3) * WIN)
        bias = jnp.concatenate([light_bias(meta, block, tokens)] * len(masks), axis=0)
        stacked = stack_heads(q_ref[rows, cols], masks)
        do_stacked = stack_heads(do[rows, cols], masks)
        key = kv_ref[key_rows, cols]
        probs = softmax(nt(stacked, key) * scale + bias)
        grad_probs = nt(do_stacked, kv_ref[key_rows, value_cols])
        ds = low(probs * (grad_probs - row_sum(probs * grad_probs)))
        dq_ref[rows, cols] = low(merge_heads(nn(ds, key), masks) * scale)
        dkv_ref[key_rows, cols] += tn(ds, stacked) * scale
        dkv_ref[key_rows, value_cols] += tn(low(probs), do_stacked)

    copies[1].wait()
    xe = jnp.concatenate([below_ref[...], x_ref[...], above_ref[...]], axis=0).astype(F32)
    plain = xe * rms_inverse(xe)
    left = low(nn(low(plain * gain_1), order))
    dk = low(dkv_ref[:, :features])
    dv = low(dkv_ref[:, features:])
    inner = slice(WIN, WIN + tokens)
    put(0, tn(left[inner], dq_ref[...]))
    put(features, tn(left, dk))
    put(2 * features, tn(left, dv))
    back = nt(dk, w_qkv[:, features : 2 * features]) + nt(dv, w_qkv[:, 2 * features :])
    own = back[inner] + nt(dq_ref[...], w_qkv[:, :features])
    halo_below_ref[...] = low(back[:WIN])
    halo_above_ref[...] = low(back[WIN + tokens :])
    gain_1_grad = gain_1_grad + jnp.sum(own * plain[inner], axis=0, keepdims=True)
    gain_1_grad = gain_1_grad + jnp.sum(back[:WIN] * plain[:WIN], axis=0, keepdims=True)
    gain_1_grad = gain_1_grad + jnp.sum(
        back[WIN + tokens :] * plain[WIN + tokens :], axis=0, keepdims=True
    )
    grad_normed_ref[...] = own + exact(pq_t_ref[...], q_back)
    rest = jnp.zeros((4, features), F32)
    small_grad_ref[...] = jnp.concatenate(
        [gain_1_grad, gain_2_grad, router_q, router_f, rest], axis=0
    )
    for both in started[-stage.shape[0] :]:
        for copy in both:
            copy.wait()


def heavy_backward(
    batch_n,
    meta,
    xq_ref,
    xk_ref,
    grad_raw_ref,
    q_ref,
    kv_ref,
    mixed_ref,
    small_ref,
    small_grad_ref,
    wx_ref,
    out_ref,
    order_ref,
    order_out_ref,
    backs_ref,
    send_ref,
    keep_ref,
):
    at = 0
    count = xq_ref.shape[0]
    keys = xk_ref.shape[0]
    features = wx_ref.shape[0]
    small = small_ref[...]
    gain_1 = small[0:1]
    place = pl.ds(pl.multiple_of(meta[6], count), count)
    grad_raw = grad_raw_ref[...]
    do = low(nt(grad_raw, out_ref[...]))
    masks = head_rows(LANES, DH)[: HH // PARTS]
    scale = DH ** (-0.5)
    bias = jnp.concatenate([heavy_bias(meta, count, keys)] * len(masks), axis=0)
    stacked = stack_heads(q_ref[...], masks)
    do_stacked = stack_heads(do, masks)
    probs = softmax(nt(stacked, kv_ref[:, :LANES]) * scale + bias)
    grad_probs = nt(do_stacked, kv_ref[:, LANES:])
    ds = low(probs * (grad_probs - row_sum(probs * grad_probs)))
    probs = low(probs)
    dq = low(merge_heads(nn(ds, kv_ref[:, :LANES]), masks) * scale)
    q_back = nt(dq, wx_ref[:, at : at + LANES])
    backs_ref[:, :features] = jnp.zeros((keys, features), BF)
    backs_ref[place, :features] = low(q_back)
    xq = xq_ref[...].astype(F32)
    q_plain = xq * rms_inverse(xq)
    order = order_ref[...]
    gain_1_grad = jnp.sum(q_back * q_plain, axis=0, keepdims=True)
    q_grads = tn(low(nn(low(q_plain * gain_1), order)), dq)
    router_k = None
    size = min(CHUNK, keys)
    for start in range(0, keys, size):
        rows = slice(start, start + size)
        xk = xk_ref[rows].astype(F32)
        k_plain = xk * rms_inverse(xk)
        k_norm = k_plain * gain_1
        k_low = low(k_norm)
        k_gate = sigmoid_dot(k_norm, small[3:4])
        dk = tn(ds[:, rows], stacked) * scale
        dv = tn(probs[:, rows], do_stacked)
        raw = nn(k_low, wx_ref[:, at + 2 * LANES : at + 3 * LANES])
        k_logit = row_sum(dv * raw) * k_gate * (1.0 - k_gate)
        grad_raw_k = low(jnp.concatenate([dk, dv * k_gate], axis=1))
        k_back = nt(grad_raw_k, wx_ref[:, at + LANES : at + 3 * LANES]) + k_logit * small[3:4]
        backs_ref[rows, features:] = low(k_back)
        one_router = jnp.sum(k_norm * k_logit, axis=0, keepdims=True)
        gain_1_grad = gain_1_grad + jnp.sum(k_back * k_plain, axis=0, keepdims=True)
        one_grads = tn(low(nn(k_low, order)), grad_raw_k)
        router_k = one_router if router_k is None else router_k + one_router
        kv_grads = one_grads if start == 0 else kv_grads + one_grads
    out_grads = low(tn(low(nn(mixed_ref[...], order_out_ref[...])), grad_raw))
    start_grads = small_grad_ref[...]
    vectors = [start_grads[0:1] + gain_1_grad, start_grads[1:2], start_grads[2:3], router_k]
    vectors += [start_grads[3:4], jnp.zeros((SMALL - 5, features), F32)]
    vectors = low(jnp.concatenate(vectors, axis=0))
    small_cols = low(jnp.transpose(nn(vectors, order)))
    upper = jnp.concatenate([low(q_grads), low(kv_grads), small_cols], axis=1)
    put_blocks(send_ref, keep_ref, batch_n, upper, out_grads[: HH * DH // PARTS])


def finish(
    x_ref,
    small_ref,
    grad_middle_ref,
    grad_normed_ref,
    from_below_ref,
    from_above_ref,
    backs_ref,
    pq_t_ref,
    pk_t_ref,
    pf_t_ref,
    middle_ref,
    light_ref,
    f_norm_ref,
    output_ref,
    input_grad_ref,
):
    tokens, features = x_ref.shape
    routed = f_norm_ref.shape[0]
    small = small_ref[...]
    gate = sigmoid_dot(f_norm_ref[...], small[4:5])
    backs = sum_blocks(backs_ref, routed, slice(0, 3 * features))
    heavy = exact(pf_t_ref[...], backs[:, 2 * features :] * gate)
    output_ref[...] = low(middle_ref[...] + light_ref[...] + heavy)
    grad = grad_normed_ref[...] + exact(pq_t_ref[...], backs[:, :features])
    grad = grad + exact(pk_t_ref[...], backs[:, features : 2 * features])
    below = from_below_ref[...].astype(F32)
    above = from_above_ref[...].astype(F32)
    grad = grad + jnp.concatenate([below, above], axis=0)
    x = x_ref[...].astype(F32)
    input_grad_ref[...] = grad_middle_ref[...] + rms_back(grad, x, rms_inverse(x), small[0:1])


def pair_sum(keep_ref, got_ref, send_out_ref, keep_out_ref):
    count = send_out_ref.shape[0]
    total = keep_ref[...].astype(F32) + got_ref[...].astype(F32)
    send_out_ref[...] = low(total[:count])
    keep_out_ref[...] = low(total[count:])


def sum_leading(ref, cols):
    total = ref[0, :, cols].astype(F32)
    for i in range(1, ref.shape[0]):
        total = total + ref[i, :, cols].astype(F32)
    return total


def join_blocks(out_ref, at, first_ref, second_ref, width):
    rows = out_ref.shape[1]
    total = first_ref[: out_ref.shape[0] * rows, :width].astype(F32)
    total = total + second_ref[: out_ref.shape[0] * rows, :width].astype(F32)
    for i in range(out_ref.shape[0]):
        out_ref[i, :, at : at + width] = low(total[i * rows : (i + 1) * rows])


def join_light(keep_ref, got_ref, out_ref):
    join_blocks(out_ref, 0, keep_ref, got_ref, keep_ref.shape[1])


def join_back(backs_ref, ffn_ref, keep_ref, got_ref, out_ref, down_ref):
    blocks, routed, width = out_ref.shape
    features = ffn_ref.shape[1]
    in_rows = keep_ref.shape[0] - down_ref.shape[0]
    rows = in_rows // blocks
    hidden = width - 3 * features
    total = keep_ref[...].astype(F32) + got_ref[...].astype(F32)
    down_ref[...] = total[in_rows:, :features]
    for i in range(blocks):
        out_ref[i, :, : 2 * features] = backs_ref[i * routed : (i + 1) * routed]
        out_ref[i, :, 2 * features : 3 * features] = ffn_ref[i * routed : (i + 1) * routed]
        out_ref[i, :rows, 3 * features :] = low(total[i * rows : (i + 1) * rows, :hidden])
        out_ref[i, rows:, 3 * features :] = jnp.zeros((routed - rows, hidden), BF)


def join_attention(keep_ref, got_ref, head_keep_ref, head_got_ref, out_ref, rest_ref):
    wide = keep_ref.shape[1]
    join_blocks(out_ref, 0, keep_ref, got_ref, wide)
    join_blocks(out_ref, wide, head_keep_ref, head_got_ref, out_ref.shape[2] - wide)
    start = out_ref.shape[0] * out_ref.shape[1]
    count, features = rest_ref.shape
    rest = head_keep_ref[start : start + count, :features].astype(F32)
    rest_ref[...] = low(rest + head_got_ref[start : start + count, :features].astype(F32))


def in_order(pair, own_ref, other_ref, out_ref):
    out_ref[pair[0]] = own_ref[...]
    out_ref[1 - pair[0]] = other_ref[...]


def pack_late(t_ref, in_ref, out_ref):
    features = t_ref.shape[1]
    rows = in_ref.shape[0]
    hidden = in_ref.shape[1] // 2 // out_ref.shape[0]
    for i in range(out_ref.shape[0]):
        out_ref[i, :, :features] = t_ref[...]
        for half in range(2):
            at = half * in_ref.shape[1] // 2 + i * hidden
            to = features + half * hidden
            out_ref[i, :rows, to : to + hidden] = in_ref[:, at : at + hidden]
            out_ref[i, rows:, to : to + hidden] = jnp.zeros((out_ref.shape[1] - rows, hidden), BF)


def light_results(total_ref, light_in_ref, light_down_ref):
    rows, features = total_ref.shape[1], light_down_ref.shape[1]
    wide = light_in_ref.shape[1]
    more = light_down_ref.shape[0] - rows
    width = features * more // rows
    light_in_ref[...] = sum_leading(total_ref, slice(0, wide))
    light_down_ref[:rows] = sum_leading(total_ref, slice(wide, wide + features))
    rest = sum_leading(total_ref, slice(wide + features, wide + features + width))
    for i in range(rows // more):
        light_down_ref[rows:, i * width : (i + 1) * width] = rest[i * more : (i + 1) * more]


def hidden_results(total_ref, heavy_in_ref):
    blocks = total_ref.shape[0]
    rows = heavy_in_ref.shape[0]
    hidden = heavy_in_ref.shape[1] // 2 // blocks
    first = total_ref.shape[2] - 2 * hidden
    for i in range(blocks):
        for half in range(2):
            at = half * heavy_in_ref.shape[1] // 2 + i * hidden
            cols = slice(first + half * hidden, first + (half + 1) * hidden)
            heavy_in_ref[:, at : at + hidden] = total_ref[i, :, cols].astype(F32)[:rows]


def attention_results(total_ref, light_qkv_ref, light_out_ref, heavy_ref, small_ref):
    blocks = total_ref.shape[0]
    wide = light_qkv_ref.shape[1]
    features = light_out_ref.shape[1]
    light_qkv_ref[...] = sum_leading(total_ref, slice(0, wide))
    light_out_ref[...] = sum_leading(total_ref, slice(wide, wide + features))
    first = wide + features
    each = blocks // PARTS
    width = features // PARTS
    for kind in range(3):
        cols = slice(first + kind * LANES, first + (kind + 1) * LANES)
        pieces = []
        for part in range(PARTS):
            total = total_ref[part * each, :, cols].astype(F32)
            for i in range(1, each):
                total = total + total_ref[part * each + i, :, cols].astype(F32)
            pieces.append(total[:, :width])
        heavy_ref[:, kind * features : (kind + 1) * features] = jnp.concatenate(pieces, axis=1)
    small_ref[...] = sum_leading(total_ref, slice(first + 3 * LANES, first + 3 * LANES + SMALL))


def pack_blocks(*refs):
    out = refs[-1]
    at = 0
    for ref in refs[:-1]:
        out[:, at : at + ref.shape[1]] = ref[...]
        at += ref.shape[1]


def after(kernel, count, extra):
    def body(*refs):
        kernel(*refs[:count], *refs[count + extra :])

    return body if extra else kernel


def call(kernel, args, memory, outs, scratch, flops, name, far=0, needs=()):
    spaces = {"v": pltpu.VMEM, "s": pltpu.SMEM, "h": pl.ANY}
    kernel = after(kernel, len(args), len(needs))
    args = tuple(args) + tuple(needs)
    memory = memory + "h" * len(needs)
    return pl.pallas_call(
        kernel,
        out_shape=[jax.ShapeDtypeStruct(shape, kind) for shape, kind in outs],
        in_specs=[pl.BlockSpec(memory_space=spaces[one]) for one in memory],
        out_specs=[pl.BlockSpec(memory_space=pltpu.VMEM)] * (len(outs) - far)
        + [pl.BlockSpec(memory_space=pl.ANY)] * far,
        scratch_shapes=scratch,
        compiler_params=pltpu.CompilerParams(vmem_limit_bytes=VMEM_LIMIT),
        cost_estimate=pl.CostEstimate(flops=flops, bytes_accessed=20_000_000, transcendentals=0),
        name=name,
    )(*args)


def select_rows(rows, mask):
    blocks = rows.astype(F32).reshape(mask.shape[0], ROUTE, rows.shape[1])
    return jnp.sum(jnp.where(mask[:, :, None], blocks, 0.0), axis=1)


def shifted(block, axis, distance):
    devices = range(lax.axis_size(axis))
    route = [(i - distance, i) for i in devices if i - distance in devices]
    return lax.ppermute(block, axis, route)


def swapped(block, distance):
    return lax.ppermute(block, "batch", [(i, i ^ distance) for i in range(lax.axis_size("batch"))])


def exchange(blocks, axis):
    return lax.all_to_all(blocks, axis, 0, 0, tiled=True)


def spread_to_all(block, axis):
    count = lax.axis_size(axis)
    return exchange(jnp.broadcast_to(block[None], (count,) + block.shape), axis)


def presum(blocks):
    if blocks.shape[0] > 16:
        return jnp.sum(blocks.astype(F32), axis=0)
    return blocks.reshape(-1, blocks.shape[2])


def summed(blocks, axis):
    return jnp.sum(exchange(blocks, axis).astype(F32), axis=0)


def pack_rows(down, rows):
    width = down.shape[1] * (down.shape[0] - rows) // rows
    rest = down[rows:]
    pieces = [rest[:, i : i + width] for i in range(0, down.shape[1], width)]
    return jnp.concatenate([down[:rows], jnp.concatenate(pieces, axis=0)], axis=1)


def halves_summed(keep, got, needs=()):
    height, width = keep.shape
    count = height // 2
    steps = width // 128
    block = 128 * max(i for i in range(1, 9) if steps % i == 0)
    rows_in = pl.BlockSpec((height, block), lambda i: (0, i))
    rows_out = pl.BlockSpec((count, block), lambda i: (0, i))
    return pl.pallas_call(
        after(pair_sum, 2, len(needs)),
        grid=(width // block,),
        out_shape=[jax.ShapeDtypeStruct((count, width), BF)] * 2,
        in_specs=[rows_in] * 2 + [pl.BlockSpec(memory_space=pl.ANY)] * len(needs),
        out_specs=[rows_out] * 2,
        compiler_params=pltpu.CompilerParams(vmem_limit_bytes=VMEM_LIMIT),
        cost_estimate=pl.CostEstimate(
            flops=height * width, bytes_accessed=6 * height * width, transcendentals=0
        ),
        name="pair_sum",
    )(keep, got, *needs)


def canonical(piece, core, pair):
    other = swapped(piece, 2)
    piece = jnp.where(pair == 0, jnp.stack([piece, other]), jnp.stack([other, piece]))
    other = swapped(piece, 1)
    piece = jnp.where(core == 0, jnp.stack([piece, other], 1), jnp.stack([other, piece], 1))
    return piece.reshape((4,) + piece.shape[2:])


def pad_cols(block, width):
    return jnp.pad(block, ((0, 0), (0, width - block.shape[1])))


def order_matrix(order):
    size = order.shape[0]
    return low((lax.broadcasted_iota(jnp.int32, (size, size), 0) == order[None, :]).astype(F32))


def other_first(index, axis, own):
    flipped = np.flip(index, axis)
    return jnp.where(own == 0, jnp.asarray(flipped), jnp.asarray(index))


def local(
    layer_input,
    cotangent,
    doc_lengths,
    routes,
    norm_gains,
    router,
    light_qkv,
    light_out,
    heavy_qkv,
    heavy_out,
    light_in,
    light_down,
    heavy_in,
    heavy_down,
):
    seq_n = lax.axis_size("seq")
    batch_n = lax.axis_size("batch")
    devices = seq_n * batch_n
    rows = light_qkv.shape[0]
    x = layer_input[0]
    g = cotangent[0]
    tokens, features = x.shape
    routed = tokens // ROUTE
    keys = routed * seq_n
    wide = light_qkv.shape[1]
    seq = lax.axis_index("seq")
    own = lax.axis_index("batch")
    core, pair = own % 2, own // 2
    offset = seq * tokens

    small = pad_cols(jnp.concatenate([norm_gains, router], axis=1), SMALL)
    sources = [
        ("light_qkv", light_qkv),
        ("light_out", light_out),
        ("light_in", light_in),
        ("light_down", pack_rows(light_down, rows)),
    ]
    layout = {}
    at = 0
    for name, block in sources:
        layout[name] = (at, at + block.shape[1])
        at += block.shape[1]
    packed = call(
        pack_blocks,
        [block for _, block in sources],
        "v" * len(sources),
        [((rows, at), BF)],
        [],
        1_000_000,
        "pack",
    )[0]
    full = lax.all_gather(packed, BOTH, axis=0, tiled=True)

    masks = [
        lax.broadcasted_iota(jnp.int32, (routed, ROUTE), 1) == routes[i, 0][:, None]
        for i in range(3)
    ]
    xq = low(select_rows(x, masks[0]))
    xk = low(select_rows(x, masks[1]))
    t = low(select_rows(g, masks[2]))
    query_parts = seq_n // PARTS
    count = keys // query_parts
    part = seq // query_parts
    query_first = (seq % query_parts) * count
    head_width = features // PARTS
    head_all = 3 * LANES + SMALL
    hidden = heavy_in.shape[1] // 2 // seq_n
    in_rows = features // batch_n
    every = lambda block: jnp.broadcast_to(block[None], (seq_n,) + block.shape)
    tall = lambda blocks: jnp.pad(blocks, ((0, 0), (0, routed - rows), (0, 0)))
    head_cols = heavy_qkv.reshape(rows, 3, PARTS, head_width)
    head_cols = jnp.pad(head_cols, ((0, 0), (0, 0), (0, 0), (0, LANES - head_width)))
    head_cols = head_cols.transpose(2, 0, 1, 3).reshape(PARTS, rows, 3 * LANES)
    head_cols = jnp.repeat(head_cols, query_parts, axis=0)
    head_cols = jnp.concatenate([head_cols, every(small)], axis=2)
    sent = jnp.concatenate([every(jnp.concatenate([xq, xk], axis=1)), tall(head_cols)], axis=2)
    travel = exchange(sent, "seq")
    if query_parts == 2:
        other = lax.ppermute(heavy_out, "seq", [(i, i ^ 1) for i in range(seq_n)])
        out_rows = jnp.where(
            seq % 2 == 0, jnp.stack([heavy_out, other]), jnp.stack([other, heavy_out])
        )
    else:
        groups = [list(range(i, i + query_parts)) for i in range(0, seq_n, query_parts)]
        out_rows = jnp.broadcast_to(heavy_out[None], (query_parts,) + heavy_out.shape)
        out_rows = lax.all_to_all(out_rows, "seq", 0, 0, tiled=True, axis_index_groups=groups)
    out_count = query_parts * rows
    out_rows = pad_cols(out_rows.reshape(out_count, features), head_all)
    piece = travel[:, :rows, 2 * features :].reshape(in_rows, head_all)
    piece = canonical(jnp.concatenate([piece, out_rows], axis=0), core, pair)
    index = np.arange(features).reshape(seq_n, 2, 2, rows)
    order_h = order_matrix(jnp.asarray(index.transpose(1, 2, 0, 3).reshape(-1)))
    wx = low(nn(order_h, piece[:, :in_rows].reshape(features, head_all)))
    h_out = piece[:, in_rows:, :features].reshape(batch_n, query_parts, rows, features)
    h_out = h_out.transpose(1, 0, 2, 3).reshape(head_width, features)
    h_out = jnp.pad(h_out, ((0, LANES - head_width), (0, 0)))
    below = shifted(x[tokens - WIN :], "seq", 1)
    above = shifted(x[:WIN], "seq", -1)

    def relative(array):
        array = jnp.where(core == 0, np.flip(array, 0), array)
        return jnp.where(pair == 0, jnp.flip(array, 1), array).reshape(-1)

    order = order_matrix(relative(index.transpose(2, 1, 0, 3)))
    units = np.arange(hidden).reshape(2, 2, -1)
    order_units = order_matrix(relative(units.transpose(1, 0, 2)))
    out_index = np.arange(head_width).reshape(query_parts, 2, 2, rows)
    out_index = relative(out_index.transpose(2, 1, 0, 3))
    rest = jnp.arange(head_width, LANES, dtype=out_index.dtype)
    order_out = order_matrix(jnp.concatenate([out_index, rest]))
    ends = jnp.cumsum(doc_lengths[0])
    meta = jnp.stack([ends[0], ends[1], ends[2], ends[3], offset, tokens * seq_n, query_first])
    meta = meta.astype(jnp.int32)
    place = lax.broadcasted_iota(jnp.int32, (routed, tokens), 1)
    first = lax.broadcasted_iota(jnp.int32, (routed, tokens), 0) * ROUTE
    picks = [(place == first + routes[i, 0][:, None]).astype(F32) for i in range(3)]
    place_t = lax.broadcasted_iota(jnp.int32, (tokens, routed), 0)
    first_t = lax.broadcasted_iota(jnp.int32, (tokens, routed), 1) * ROUTE
    picks_t = [(place_t == first_t + routes[i, 0][None, :]).astype(F32) for i in range(3)]

    xq_all = travel[:, :, :features].reshape(keys, features)
    xq_part = lax.dynamic_slice_in_dim(xq_all, query_first, count, 0)
    xk_all = travel[:, :, features : 2 * features].reshape(keys, features)
    raw, heavy_q, heavy_kv, heavy_mixed, small_rows = call(
        heavy_forward,
        (meta, xq_part, xk_all, wx, h_out),
        "svvvv",
        [
            ((count, features), BF),
            ((count, LANES), BF),
            ((keys, 2 * LANES), BF),
            ((count, LANES), BF),
            ((8, features), F32),
        ],
        [],
        2_000_000_000,
        "heavy_forward",
    )
    part_of, query_of = lambda i: i // query_parts, lambda i: i % query_parts
    owner = lambda i, step: query_of(i) * PARTS + (part_of(i) + step) % PARTS
    steps = range(PARTS)
    raw = raw.reshape(PARTS, routed, features)
    raw = [lax.dynamic_index_in_dim(raw, (part + step) % PARTS, 0, False) for step in steps]
    raw = [
        lax.ppermute(block, "seq", [(i, owner(i, step)) for i in range(seq_n)])
        for step, block in zip(steps, raw)
    ]
    raw = jnp.concatenate(raw, axis=0)

    late = call(
        pack_late,
        (t, heavy_in),
        "vv",
        [((seq_n, routed, features + 2 * hidden), BF)],
        [],
        1_000_000,
        "pack_late",
        needs=[travel],
    )[0]
    late = exchange(late, "seq")
    pack_width = max(2 * hidden, features)
    piece = late[:, :rows, features:].reshape(in_rows, 2 * hidden)
    piece = [pad_cols(piece, pack_width), pad_cols(heavy_down, pack_width)]
    late_piece = jnp.concatenate(piece, axis=0)
    late_other = swapped(late_piece, 2)
    weight = lambda columns: pltpu.VMEM((features, columns), BF)
    q, kv, mixed, heavy_raw, middle, normed2, f_norm, f_sent = call(
        functools.partial(light_forward, layout),
        (meta, below, x, above, xq, raw, picks_t[0], picks[2], small_rows, full),
        "svvvvvvvvh",
        [
            ((tokens, features), BF),
            ((tokens + 2 * WIN, 2 * features), BF),
            ((tokens, features), BF),
            ((routed, features), F32),
            ((tokens, features), F32),
            ((tokens, features), BF),
            ((routed, features), F32),
            ((keys, features + SMALL), BF),
        ],
        [weight(wide), weight(features), pltpu.SemaphoreType.DMA((2,))],
        8_000_000_000,
        "light_forward",
    )
    f_sent = exchange(f_sent.reshape(seq_n, routed, features + SMALL), "seq")
    piece = call(
        in_order,
        (pair.reshape(1).astype(jnp.int32), late_piece, late_other),
        "svv",
        [((2,) + late_piece.shape, BF)],
        [],
        1_000_000,
        "in_order",
        needs=[middle],
    )[0]
    other = swapped(piece, 1)
    piece = jnp.where(core == 0, jnp.stack([piece, other], 1), jnp.stack([other, piece], 1))
    piece = piece.reshape((batch_n,) + late_piece.shape)
    h_in = low(nn(order_h, piece[:, :in_rows, : 2 * hidden].reshape(features, 2 * hidden)))
    h_down = piece[:, in_rows:, :features].reshape(hidden, features)
    t_all = late[:, :, :features].reshape(keys, features)

    light_hidden = light_in.shape[1] // 2
    down_width = layout["light_down"][1] - layout["light_down"][0]
    half = features // 2
    ffn_width = light_in.shape[1] + down_width
    ffn, grad_n2, light_send, light_keep = call(
        functools.partial(light_ffn, layout, devices),
        (normed2, g, order, full),
        "vvvh",
        [
            ((tokens, features), F32),
            ((tokens, features), F32),
            ((half, ffn_width), BF),
            ((half, ffn_width), BF),
        ],
        [
            weight(light_in.shape[1]),
            weight(down_width),
            pltpu.VMEM((light_hidden, features), BF),
            pltpu.VMEM((features, down_width), F32),
            weight(down_width),
            pltpu.SemaphoreType.DMA((2,)),
        ],
        8_000_000_000,
        "light_ffn",
    )
    light_got = swapped(light_send, 1)
    light_send, light_keep = halves_summed(light_keep, light_got)
    light_got = swapped(light_send, 2)
    down_rows = hidden // batch_n
    back, ffn_part, ffn_send, ffn_keep = call(
        functools.partial(heavy_ffn, batch_n),
        (f_sent.reshape(keys, features + SMALL), t_all, h_in, h_down, order, order_units),
        "vvvvvv",
        [
            ((keys, features + SMALL), BF),
            ((keys, features), BF),
            ((batch_n // 2 * (in_rows + down_rows), pack_width), BF),
            ((batch_n // 2 * (in_rows + down_rows), pack_width), BF),
        ],
        [],
        4_000_000_000,
        "heavy_ffn",
        needs=[light_keep],
    )
    back = presum(exchange(back.reshape(seq_n, routed, features + SMALL), "seq"))

    ffn_got = swapped(ffn_send, 1)
    ffn_send, ffn_keep = halves_summed(ffn_keep, ffn_got)
    ffn_got = swapped(ffn_send, 2)
    light_rows = call(
        join_light,
        (light_keep, light_got),
        "vv",
        [((seq_n, rows, ffn_width), BF)],
        [],
        10_000_000,
        "join_light",
        needs=[ffn_keep],
    )[0]
    light_sums = exchange(light_rows, "seq")

    (
        grad_middle,
        grad_normed,
        halo_below,
        halo_above,
        grad_raw,
        small_grad,
        attn_send,
        attn_keep,
    ) = call(
        functools.partial(light_backward, layout),
        (
            meta,
            below,
            x,
            above,
            xq,
            picks[0],
            picks_t[0],
            picks_t[2],
            g,
            order,
            q,
            kv,
            mixed,
            heavy_raw,
            middle,
            f_norm,
            small_rows,
            grad_n2,
            back,
            full,
        ),
        "s" + "v" * 18 + "h",
        [
            ((tokens, features), F32),
            ((tokens, features), F32),
            ((WIN, features), BF),
            ((WIN, features), BF),
            ((routed, features), BF),
            ((8, features), F32),
            ((half, wide + features), BF),
            ((half, wide + features), BF),
        ],
        [
            weight(wide),
            weight(features),
            pltpu.VMEM((tokens, features), BF),
            pltpu.VMEM((tokens + 2 * WIN, 2 * features), F32),
            pltpu.VMEM((3, features, features), BF),
            pltpu.SemaphoreType.DMA((2,)),
            pltpu.SemaphoreType.DMA((3, 2)),
        ],
        16_000_000_000,
        "light_backward",
        2,
        [light_rows],
    )

    attn_got = swapped(attn_send, 1)
    attn_send, attn_keep = halves_summed(attn_keep, attn_got)
    attn_got = swapped(attn_send, 2)

    blocks = [
        lax.ppermute(grad_raw, "seq", [(owner(i, step), i) for i in range(seq_n)])
        for step in steps
    ]
    blocks = jnp.stack(blocks)
    blocks = [lax.dynamic_index_in_dim(blocks, (m - part) % PARTS, 0, False) for m in steps]
    grad_raw = jnp.concatenate(blocks, axis=0)
    head_rows_n = head_width // batch_n
    backs, head_send, head_keep = call(
        functools.partial(heavy_backward, batch_n),
        (
            meta,
            xq_part,
            xk_all,
            grad_raw,
            heavy_q,
            heavy_kv,
            heavy_mixed,
            small_rows,
            small_grad,
            wx,
            h_out,
            order,
            order_out,
        ),
        "s" + "v" * 12,
        [
            ((keys, 2 * features), BF),
            ((batch_n // 2 * (in_rows + head_rows_n), head_all), BF),
            ((batch_n // 2 * (in_rows + head_rows_n), head_all), BF),
        ],
        [],
        4_000_000_000,
        "heavy_backward",
        needs=[attn_keep, light_sums],
    )
    backs, grad_h_down = call(
        join_back,
        (backs, ffn_part, ffn_keep, ffn_got),
        "vvvv",
        [((seq_n, routed, 3 * features + 2 * hidden), BF), (heavy_down.shape, F32)],
        [],
        10_000_000,
        "join_back",
    )
    backs = exchange(backs, "seq")
    back_rows = presum(backs[:, :, : 3 * features]) if seq_n > 16 else backs.reshape(keys, -1)

    head_got = swapped(head_send, 1)
    head_send, head_keep = halves_summed(head_keep, head_got)
    total, out_grads = call(
        join_attention,
        (attn_keep, attn_got, head_keep, swapped(head_send, 2)),
        "vvvv",
        [((seq_n, rows, wide + features + head_all), BF), ((out_count, features), BF)],
        [],
        10_000_000,
        "join_attention",
    )
    total = exchange(total, "seq")
    out_grads = out_grads.reshape(query_parts, rows, features)
    if query_parts == 2:
        out_send = jnp.where(seq % 2 == 0, out_grads[1], out_grads[0])
        out_keep = jnp.where(seq % 2 == 0, out_grads[0], out_grads[1])
        other = lax.ppermute(out_send, "seq", [(i, i ^ 1) for i in range(seq_n)])
        grad_heavy_out = out_keep.astype(F32) + other.astype(F32)
    else:
        out_grads = lax.all_to_all(out_grads, "seq", 0, 0, tiled=True, axis_index_groups=groups)
        grad_heavy_out = jnp.sum(out_grads.astype(F32), axis=0)
    grad_light_in, grad_light_down = call(
        light_results,
        (light_sums,),
        "v",
        [(light_in.shape, F32), (light_down.shape, F32)],
        [],
        10_000_000,
        "light_results",
    )
    grad_h_in = call(
        hidden_results, (backs,), "v", [(heavy_in.shape, F32)], [], 10_000_000, "hidden_results"
    )[0]
    grad_light_qkv, grad_light_out, grad_heads, grad_small = call(
        attention_results,
        (total,),
        "v",
        [(light_qkv.shape, F32), (light_out.shape, F32), (heavy_qkv.shape, F32), ((rows, SMALL), F32)],
        [],
        10_000_000,
        "attention_results",
    )

    from_above = shifted(halo_below, "seq", -1)
    from_below = shifted(halo_above, "seq", 1)
    output, input_grad = call(
        finish,
        (
            x,
            small_rows,
            grad_middle,
            grad_normed,
            from_below,
            from_above,
            back_rows,
            picks_t[0],
            picks_t[1],
            picks_t[2],
            middle,
            ffn,
            f_norm,
        ),
        "v" * 13,
        [((tokens, features), BF), ((tokens, features), F32)],
        [],
        1_000_000_000,
        "finish",
    )
    return (
        output[None],
        input_grad[None],
        grad_small[:, :2],
        grad_small[:, 2:5],
        grad_light_qkv,
        grad_light_out,
        grad_heads,
        grad_heavy_out,
        grad_light_in,
        grad_light_down,
        grad_h_in,
        grad_h_down,
    )


def solution(mesh):
    weight = P(BOTH, None)
    rows = P("batch", "seq", None)
    return jax.shard_map(
        local,
        mesh=mesh,
        in_specs=(rows, rows, P("batch", None), P(None, "batch", "seq")) + (weight,) * 10,
        out_specs=(rows, rows) + (weight,) * 10,
        check_vma=False,
    )
```

```python
import functools

import jax
import jax.numpy as jnp
import numpy as np
from jax import lax
from jax.experimental import pallas as pl
from jax.experimental.pallas import tpu as pltpu
from jax.sharding import PartitionSpec as P

HL = 8
DL = 96
HH = 12
DH = 64
WIN = 128
ROUTE = 8
SMALL = 128
CHUNK = 256
PARTS = 4
LANES = 256
EPS = 1e-06
BF = jnp.bfloat16
F32 = jnp.float32
BOTH = ("seq", "batch")
highest = lax.Precision.HIGHEST
VMEM_LIMIT = 60 * 1024 * 1024


def nn(left, right):
    return jnp.dot(left, right, preferred_element_type=F32)


def nt(left, right):
    return lax.dot_general(left, right, (((1,), (1,)), ((), ())), preferred_element_type=F32)


def tn(left, right):
    return lax.dot_general(left, right, (((0,), (0,)), ((), ())), preferred_element_type=F32)


def exact(left, right):
    return jnp.dot(left, right, precision=highest, preferred_element_type=F32)


def low(values):
    return values.astype(BF)


def row_sum(values):
    return jnp.sum(values, axis=-1, keepdims=True)


def rms_inverse(values):
    return lax.rsqrt(jnp.mean(values * values, axis=-1, keepdims=True) + EPS)


def rms_back(grad, values, inverse, gain):
    scaled = grad * gain
    inner = jnp.mean(scaled * values, axis=-1, keepdims=True)
    return inverse * scaled - values * (inverse * inverse * inverse * inner)


def geglu_parts(pair):
    half = pair.shape[-1] // 2
    u = pair[:, :half]
    up = pair[:, half:]
    c = 0.7978845608028654
    t = jnp.tanh(c * (u + 0.044715 * (u * u * u)))
    gelu = 0.5 * u * (1.0 + t)
    slope = 0.5 * (1.0 + t) + 0.5 * u * (1.0 - t * t) * (c * (1.0 + 3.0 * 0.044715 * (u * u)))
    return gelu, slope, up


def documents(positions, meta):
    found = (positions >= meta[0]).astype(jnp.int32)
    for i in range(1, 4):
        found = found + (positions >= meta[i]).astype(jnp.int32)
    return found


def head_rows(width, size):
    lanes = lax.broadcasted_iota(jnp.int32, (1, width), 1)
    inside = [(lanes >= i * size) & (lanes < (i + 1) * size) for i in range(width // size)]
    return [jnp.where(one, 1.0, 0.0) for one in inside]


def stack_heads(rows, masks):
    return jnp.concatenate([rows * low(mask) for mask in masks], axis=0)


def merge_heads(stacked, masks):
    count = stacked.shape[0] // len(masks)
    total = stacked[:count] * masks[0]
    for i in range(1, len(masks)):
        total = total + stacked[i * count : (i + 1) * count] * masks[i]
    return total


def softmax(scores):
    weights = jnp.exp(scores - jnp.max(scores, axis=-1, keepdims=True))
    return weights * (1.0 / row_sum(weights))


def light_bias(meta, block, tokens):
    query = meta[4] + block * WIN + lax.broadcasted_iota(jnp.int32, (WIN, 1), 0)
    key = meta[4] + (block - 1) * WIN + lax.broadcasted_iota(jnp.int32, (1, 3 * WIN), 1)
    key_doc = jnp.where((key >= 0) & (key < meta[5]), documents(key, meta), -1)
    seen = (jnp.abs(query - key) < WIN) & (documents(query, meta) == key_doc)
    return jnp.where(seen, 0.0, -1e30)


def heavy_bias(meta, count, keys):
    query = (meta[6] + lax.broadcasted_iota(jnp.int32, (count, 1), 0)) * ROUTE
    key = lax.broadcasted_iota(jnp.int32, (1, keys), 1) * ROUTE
    return jnp.where(documents(query, meta) == documents(key, meta), 0.0, -1e30)


def light_units(tokens):
    return [(block, part) for block in range(tokens // WIN) for part in range(2)]


def sigmoid_dot(rows, vector):
    return jax.nn.sigmoid(row_sum(rows * vector))


def load(full_ref, places, sems):
    copies = []
    for i, ((first, last), buffer) in enumerate(places):
        copies.append(pltpu.make_async_copy(full_ref.at[:, first:last], buffer, sems.at[i]))
        copies[-1].start()
    return copies


def two_lanes(column):
    lanes = lax.broadcasted_iota(jnp.int32, (column.shape[0], SMALL), 1)
    high = low(column).astype(F32)
    return low(jnp.where(lanes == 0, high, jnp.where(lanes == 1, column - high, 0.0)))


def from_two_lanes(block):
    lanes = lax.broadcasted_iota(jnp.int32, block.shape, 1)
    return row_sum(jnp.where(lanes < 2, block.astype(F32), 0.0))


def sum_blocks(ref, count, cols=slice(None)):
    total = ref[0:count, cols].astype(F32)
    for i in range(1, ref.shape[0] // count):
        total = total + ref[i * count : (i + 1) * count, cols].astype(F32)
    return total


def heavy_forward(
    meta,
    xq_ref,
    xk_ref,
    wx_ref,
    out_ref,
    raw_ref,
    q_ref,
    kv_ref,
    mixed_ref,
    small_ref,
):
    count = xq_ref.shape[0]
    keys = xk_ref.shape[0]
    at = 0
    small = jnp.transpose(wx_ref[:, 3 * LANES :].astype(F32))[:8]
    small_ref[...] = small
    gain_1 = small[0:1]
    xq = xq_ref[...].astype(F32)
    q_norm = xq * rms_inverse(xq) * gain_1
    q_ref[...] = low(nn(low(q_norm), wx_ref[:, at : at + LANES]))
    size = min(CHUNK, keys)
    for start in range(0, keys, size):
        xk = xk_ref[start : start + size].astype(F32)
        k_norm = xk * rms_inverse(xk) * gain_1
        k_gate = sigmoid_dot(k_norm, small[3:4])
        raw = nn(low(k_norm), wx_ref[:, at + LANES : at + 3 * LANES])
        kv_ref[start : start + size, :LANES] = low(raw[:, :LANES])
        kv_ref[start : start + size, LANES:] = low(raw[:, LANES:] * k_gate)
    masks = head_rows(LANES, DH)[: HH // PARTS]
    bias = jnp.concatenate([heavy_bias(meta, count, keys)] * len(masks), axis=0)
    stacked = stack_heads(q_ref[...], masks)
    probs = softmax(nt(stacked, kv_ref[:, :LANES]) * DH ** (-0.5) + bias)
    mixed = low(merge_heads(nn(low(probs), kv_ref[:, LANES:]), masks))
    mixed_ref[...] = mixed
    raw_ref[...] = jnp.zeros_like(raw_ref)
    raw_ref[pl.ds(pl.multiple_of(meta[6], count), count)] = low(nn(mixed, out_ref[...]))


def light_forward(
    layout,
    meta,
    below_ref,
    x_ref,
    above_ref,
    small_ref,
    full_ref,
    q_ref,
    kv_ref,
    mixed_ref,
    base_ref,
    w_qkv,
    w_lo,
    sems,
):
    tokens, features = x_ref.shape
    copies = load(full_ref, [(layout["light_qkv"], w_qkv), (layout["light_out"], w_lo)], sems)
    gain_1 = small_ref[0:1]
    xe = jnp.concatenate([below_ref[...], x_ref[...], above_ref[...]], axis=0).astype(F32)
    ne = low(xe * rms_inverse(xe) * gain_1)
    copies[0].wait()
    q_ref[...] = low(nn(ne[WIN : WIN + tokens], w_qkv[:, :features]))
    kv_ref[...] = low(nn(ne, w_qkv[:, features:]))
    width = features // 2
    masks = head_rows(width, DL)
    scale = DL ** (-0.5)
    for block, part in light_units(tokens):
        cols = slice(part * width, (part + 1) * width)
        rows = slice(block * WIN, (block + 1) * WIN)
        key_rows = slice(block * WIN, (block + 3) * WIN)
        bias = jnp.concatenate([light_bias(meta, block, tokens)] * len(masks), axis=0)
        stacked = stack_heads(q_ref[rows, cols], masks)
        probs = softmax(nt(stacked, kv_ref[key_rows, cols]) * scale + bias)
        values = kv_ref[key_rows, features + part * width : features + (part + 1) * width]
        mixed_ref[rows, cols] = low(merge_heads(nn(low(probs), values), masks))
    copies[1].wait()
    base_ref[...] = x_ref[...].astype(F32) + nn(mixed_ref[...], w_lo[...])


def second_norm(
    base_ref,
    xq_ref,
    raw_ref,
    pq_t_ref,
    pf_ref,
    small_ref,
    heavy_raw_ref,
    middle_ref,
    normed2_ref,
    f_norm_ref,
    f_sent_ref,
):
    routed = xq_ref.shape[0]
    small = small_ref[...]
    gain_1, gain_2 = small[0:1], small[1:2]
    xq = xq_ref[...].astype(F32)
    q_gate = sigmoid_dot(xq * rms_inverse(xq) * gain_1, small[2:3])
    heavy_raw = sum_blocks(raw_ref, routed)
    heavy_raw_ref[...] = heavy_raw
    middle = base_ref[...] + exact(pq_t_ref[...], heavy_raw * q_gate)
    middle_ref[...] = middle
    normed2 = middle * rms_inverse(middle) * gain_2
    normed2_ref[...] = low(normed2)
    f_norm = exact(pf_ref[...], normed2)
    f_norm_ref[...] = f_norm
    sent = jnp.concatenate([low(f_norm), two_lanes(sigmoid_dot(f_norm, small[4:5]))], axis=1)
    for i in range(f_sent_ref.shape[0] // routed):
        f_sent_ref[i * routed : (i + 1) * routed] = sent


def unpack_down(packed, down_ref, work_ref, devices):
    features = down_ref.shape[1]
    rows = packed.shape[0] // devices
    more = down_ref.shape[0] // devices - rows
    width = packed.shape[1] - features
    if rows % 8 == 0 and more % 8 == 0:
        work_ref[...] = packed.astype(F32)
        for i in range(devices):
            own = work_ref[i * rows : (i + 1) * rows, :features]
            parts = [
                work_ref[i * rows + j * more : i * rows + (j + 1) * more, features:]
                for j in range(rows // more)
            ]
            whole = jnp.concatenate([own, jnp.concatenate(parts, axis=1)], axis=0)
            down_ref[i * (rows + more) : (i + 1) * (rows + more)] = low(whole)
    else:
        for j in range(rows // more):
            cols = slice(j * width, (j + 1) * width)
            first, second = down_places(down_ref.shape[0], packed.shape[0], rows, more, j)
            down_ref[:, cols] = low(nn(first, packed[:, cols]) + nn(second, packed[:, features:]))


def down_places(units, packed_rows, rows, more, j):
    unit = lax.broadcasted_iota(jnp.int32, (units, packed_rows), 0)
    row = lax.broadcasted_iota(jnp.int32, (units, packed_rows), 1)
    total = rows + more
    device, inner = unit // total, unit % total
    first = (inner < rows) & (row == device * rows + inner)
    second = (inner >= rows) & (row == device * rows + j * more + inner - rows)
    return low(jnp.where(first, 1.0, 0.0)), low(jnp.where(second, 1.0, 0.0))


def pack_down(grad, out_ref, at, devices, rows):
    features = grad.shape[1]
    more = grad.shape[0] // devices - rows
    width = features * more // rows
    if rows % 8 == 0 and more % 8 == 0:
        pieces = []
        for i in range(devices):
            start = i * (rows + more)
            rest = grad[start + rows : start + rows + more]
            parts = [rest[:, j * width : (j + 1) * width] for j in range(rows // more)]
            pieces.append(
                jnp.concatenate([grad[start : start + rows], jnp.concatenate(parts, axis=0)], axis=1)
            )
        out_ref[:, at:] = low(jnp.concatenate(pieces, axis=0))
    else:
        total = None
        for j in range(rows // more):
            cols = slice(j * width, (j + 1) * width)
            first, second = down_places(grad.shape[0], devices * rows, rows, more, j)
            block = low(grad[:, cols])
            out_ref[:, at + j * width : at + (j + 1) * width] = low(tn(first, block))
            part = tn(second, block)
            total = part if total is None else total + part
        out_ref[:, at + features :] = low(total)


def light_ffn(
    layout,
    devices,
    normed2_ref,
    g_ref,
    order_ref,
    full_ref,
    ffn_ref,
    grad_ref,
    send_ref,
    keep_ref,
    w_in,
    w_packed,
    w_down,
    work_ref,
    pack_ref,
    sems,
):
    features = normed2_ref.shape[1]
    half = features // 2
    order = order_ref[...]
    copies = []
    for i, (name, buffer) in enumerate([("light_in", w_in), ("light_down", w_packed)]):
        first, last = layout[name]
        copy = pltpu.make_async_copy(full_ref.at[:, first:last], buffer, sems.at[i])
        copy.start()
        copies.append(copy)
    copies[0].wait()
    copies[1].wait()
    unpack_down(w_packed[...], w_down, work_ref, devices)
    gelu, slope, up = geglu_parts(nn(normed2_ref[...], w_in[...]))
    hidden = low(gelu * up)
    ffn_ref[...] = nn(hidden, w_down[...])
    grad_hidden = nt(g_ref[...], w_down[...])
    grad_pair = low(jnp.concatenate([grad_hidden * up * slope, grad_hidden * gelu], axis=1))
    grad_ref[...] = nt(grad_pair, w_in[...])
    wide = w_in.shape[1]
    left = low(nn(normed2_ref[...], order))
    for at in range(0, wide, 512):
        block = low(tn(left, grad_pair[:, at : at + 512]))
        send_ref[:, at : at + 512] = block[:half]
        keep_ref[:, at : at + 512] = block[half:]
    pack_down(tn(hidden, g_ref[...]), pack_ref, 0, devices, features // devices)
    block = low(tn(order, pack_ref[...]))
    send_ref[:, wide:] = block[:half]
    keep_ref[:, wide:] = block[half:]


def heavy_ffn(
    batch_n,
    sent_ref,
    t_ref,
    in_ref,
    down_ref,
    order_ref,
    back_ref,
    ffn_ref,
    grads_ref,
):
    features = in_ref.shape[0]
    hidden_n = down_ref.shape[0]
    w_in = in_ref[...]
    f_in = sent_ref[:, :features]
    gate = from_two_lanes(sent_ref[:, features:])
    t = t_ref[...].astype(F32)
    grad_ffn = low(t * gate)
    gelu, slope, up = geglu_parts(nn(f_in, w_in))
    hidden = low(gelu * up)
    ffn = nn(hidden, down_ref[...])
    ffn_ref[...] = low(ffn)
    grad_hidden = nt(grad_ffn, down_ref[...])
    grad_pair = low(jnp.concatenate([grad_hidden * up * slope, grad_hidden * gelu], axis=1))
    back_ref[:, :features] = low(nt(grad_pair, w_in))
    back_ref[:, features:] = two_lanes(row_sum(t * ffn))
    grad_in = low(tn(low(nn(f_in, order_ref[...])), grad_pair))
    put_blocks(grads_ref, grads_ref, batch_n, grad_in, low(tn(hidden, grad_ffn)))


def put_blocks(send_ref, keep_ref, batch_n, upper, lower):
    upper_rows = upper.shape[0] // batch_n
    lower_rows = lower.shape[0] // batch_n
    total = upper_rows + lower_rows
    width = send_ref.shape[1]
    for i in range(batch_n):
        ref = send_ref if i < batch_n // 2 else keep_ref
        start = i * total if send_ref is keep_ref else i % (batch_n // 2) * total
        places = [(start, upper_rows, upper), (start + upper_rows, lower_rows, lower)]
        for first, count, values in places:
            ref[first : first + count, : values.shape[1]] = values[i * count : (i + 1) * count]
            if values.shape[1] < width:
                ref[first : first + count, values.shape[1] :] = jnp.zeros(
                    (count, width - values.shape[1]), BF
                )


def norm_backward(
    layout,
    xq_ref,
    pq_ref,
    pf_t_ref,
    g_ref,
    heavy_raw_ref,
    middle_ref,
    f_norm_ref,
    small_ref,
    grad_n2_ref,
    back_ref,
    full_ref,
    grad_middle_ref,
    do_ref,
    grad_raw_ref,
    q_back_ref,
    small_grad_ref,
    w_lo,
    sems,
):
    features = g_ref.shape[1]
    routed = xq_ref.shape[0]
    copies = load(full_ref, [(layout["light_out"], w_lo)], sems)
    small = small_ref[...]
    gain_1, gain_2 = small[0:1], small[1:2]
    sums = sum_blocks(back_ref, routed)
    f_norm = f_norm_ref[...]
    f_gate = sigmoid_dot(f_norm, small[4:5])
    f_logit = (sums[:, features : features + 1] + sums[:, features + 1 : features + 2]) * (
        f_gate * (1.0 - f_gate)
    )
    router_f = jnp.sum(f_norm * f_logit, axis=0, keepdims=True)
    f_back = sums[:, :features] + f_logit * small[4:5]
    middle = middle_ref[...]
    grad_n2 = grad_n2_ref[...] + exact(pf_t_ref[...], f_back)
    inverse_2 = rms_inverse(middle)
    gain_2_grad = jnp.sum(grad_n2 * (middle * inverse_2), axis=0, keepdims=True)
    grad_middle = g_ref[...].astype(F32) + rms_back(grad_n2, middle, inverse_2, gain_2)
    grad_middle_ref[...] = grad_middle
    q_rows = exact(pq_ref[...], grad_middle)
    xq = xq_ref[...].astype(F32)
    q_plain = xq * rms_inverse(xq)
    q_norm = q_plain * gain_1
    q_gate = sigmoid_dot(q_norm, small[2:3])
    grad_raw = low(q_rows * q_gate)
    for i in range(grad_raw_ref.shape[0] // routed):
        grad_raw_ref[i * routed : (i + 1) * routed] = grad_raw
    q_logit = row_sum(q_rows * heavy_raw_ref[...]) * q_gate * (1.0 - q_gate)
    q_back = q_logit * small[2:3]
    q_back_ref[...] = q_back
    router_q = jnp.sum(q_norm * q_logit, axis=0, keepdims=True)
    gain_1_grad = jnp.sum(q_back * q_plain, axis=0, keepdims=True)
    rest = jnp.zeros((4, features), F32)
    small_grad_ref[...] = jnp.concatenate(
        [gain_1_grad, gain_2_grad, router_q, router_f, rest], axis=0
    )
    copies[0].wait()
    do_ref[...] = low(nt(low(grad_middle), w_lo[...]))


def light_backward(
    layout,
    meta,
    below_ref,
    x_ref,
    above_ref,
    pq_t_ref,
    q_ref,
    kv_ref,
    mixed_ref,
    grad_middle_ref,
    do_ref,
    q_back_ref,
    small_ref,
    small_part_ref,
    full_ref,
    grad_normed_ref,
    halo_below_ref,
    halo_above_ref,
    small_grad_ref,
    grads_ref,
    w_qkv,
    dq_ref,
    dkv_ref,
    stage,
    sems,
    out_sems,
):
    tokens, features = x_ref.shape
    copies = load(full_ref, [(layout["light_qkv"], w_qkv)], sems)
    gain_1 = small_ref[0:1]
    started = []

    def put(at, grad):
        slot = len(started) % stage.shape[0]
        if len(started) >= stage.shape[0]:
            started[-stage.shape[0]].wait()
        stage[slot] = low(grad)
        place = grads_ref.at[:, at : at + grad.shape[1]]
        started.append(pltpu.make_async_copy(stage.at[slot], place, out_sems.at[slot]))
        started[-1].start()

    put(3 * features, tn(mixed_ref[...], low(grad_middle_ref[...])))
    width = features // 2
    masks = head_rows(width, DL)
    scale = DL ** (-0.5)
    dkv_ref[...] = jnp.zeros_like(dkv_ref)
    for block, part in light_units(tokens):
        cols = slice(part * width, (part + 1) * width)
        value_cols = slice(features + part * width, features + (part + 1) * width)
        rows = slice(block * WIN, (block + 1) * WIN)
        key_rows = slice(block * WIN, (block + 3) * WIN)
        bias = jnp.concatenate([light_bias(meta, block, tokens)] * len(masks), axis=0)
        stacked = stack_heads(q_ref[rows, cols], masks)
        do_stacked = stack_heads(do_ref[rows, cols], masks)
        key = kv_ref[key_rows, cols]
        probs = softmax(nt(stacked, key) * scale + bias)
        grad_probs = nt(do_stacked, kv_ref[key_rows, value_cols])
        ds = low(probs * (grad_probs - row_sum(probs * grad_probs)))
        dq_ref[rows, cols] = low(merge_heads(nn(ds, key), masks) * scale)
        dkv_ref[key_rows, cols] += tn(ds, stacked) * scale
        dkv_ref[key_rows, value_cols] += tn(low(probs), do_stacked)

    copies[0].wait()
    xe = jnp.concatenate([below_ref[...], x_ref[...], above_ref[...]], axis=0).astype(F32)
    plain = xe * rms_inverse(xe)
    left = low(plain * gain_1)
    dk = low(dkv_ref[:, :features])
    dv = low(dkv_ref[:, features:])
    inner = slice(WIN, WIN + tokens)
    put(0, tn(left[inner], dq_ref[...]))
    put(features, tn(left, dk))
    put(2 * features, tn(left, dv))
    back = nt(dk, w_qkv[:, features : 2 * features]) + nt(dv, w_qkv[:, 2 * features :])
    own = back[inner] + nt(dq_ref[...], w_qkv[:, :features])
    halo_below_ref[...] = low(back[:WIN])
    halo_above_ref[...] = low(back[WIN + tokens :])
    part = small_part_ref[...]
    gain_1_grad = part[0:1] + jnp.sum(own * plain[inner], axis=0, keepdims=True)
    gain_1_grad = gain_1_grad + jnp.sum(back[:WIN] * plain[:WIN], axis=0, keepdims=True)
    gain_1_grad = gain_1_grad + jnp.sum(
        back[WIN + tokens :] * plain[WIN + tokens :], axis=0, keepdims=True
    )
    grad_normed_ref[...] = own + exact(pq_t_ref[...], q_back_ref[...])
    small_grad_ref[...] = jnp.concatenate([gain_1_grad, part[1:]], axis=0)
    for copy in started[-stage.shape[0] :]:
        copy.wait()


def heavy_backward(
    batch_n,
    meta,
    xq_ref,
    xk_ref,
    grad_raw_ref,
    q_ref,
    kv_ref,
    mixed_ref,
    small_ref,
    small_grad_ref,
    wx_ref,
    out_ref,
    order_ref,
    order_out_ref,
    backs_ref,
    send_ref,
    keep_ref,
):
    at = 0
    count = xq_ref.shape[0]
    keys = xk_ref.shape[0]
    features = wx_ref.shape[0]
    small = small_ref[...]
    gain_1 = small[0:1]
    place = pl.ds(pl.multiple_of(meta[6], count), count)
    grad_raw = grad_raw_ref[place]
    do = low(nt(grad_raw, out_ref[...]))
    masks = head_rows(LANES, DH)[: HH // PARTS]
    scale = DH ** (-0.5)
    bias = jnp.concatenate([heavy_bias(meta, count, keys)] * len(masks), axis=0)
    stacked = stack_heads(q_ref[...], masks)
    do_stacked = stack_heads(do, masks)
    probs = softmax(nt(stacked, kv_ref[:, :LANES]) * scale + bias)
    grad_probs = nt(do_stacked, kv_ref[:, LANES:])
    ds = low(probs * (grad_probs - row_sum(probs * grad_probs)))
    probs = low(probs)
    dq = low(merge_heads(nn(ds, kv_ref[:, :LANES]), masks) * scale)
    q_back = nt(dq, wx_ref[:, at : at + LANES])
    backs_ref[:, :features] = jnp.zeros((keys, features), BF)
    backs_ref[place, :features] = low(q_back)
    xq = xq_ref[...].astype(F32)
    q_plain = xq * rms_inverse(xq)
    order = order_ref[...]
    gain_1_grad = jnp.sum(q_back * q_plain, axis=0, keepdims=True)
    q_grads = tn(low(nn(low(q_plain * gain_1), order)), dq)
    router_k = None
    size = min(CHUNK, keys)
    for start in range(0, keys, size):
        rows = slice(start, start + size)
        xk = xk_ref[rows].astype(F32)
        k_plain = xk * rms_inverse(xk)
        k_norm = k_plain * gain_1
        k_low = low(k_norm)
        k_gate = sigmoid_dot(k_norm, small[3:4])
        dk = tn(ds[:, rows], stacked) * scale
        dv = tn(probs[:, rows], do_stacked)
        raw = nn(k_low, wx_ref[:, at + 2 * LANES : at + 3 * LANES])
        k_logit = row_sum(dv * raw) * k_gate * (1.0 - k_gate)
        grad_raw_k = low(jnp.concatenate([dk, dv * k_gate], axis=1))
        k_back = nt(grad_raw_k, wx_ref[:, at + LANES : at + 3 * LANES]) + k_logit * small[3:4]
        backs_ref[rows, features:] = low(k_back)
        one_router = jnp.sum(k_norm * k_logit, axis=0, keepdims=True)
        gain_1_grad = gain_1_grad + jnp.sum(k_back * k_plain, axis=0, keepdims=True)
        one_grads = tn(low(nn(k_low, order)), grad_raw_k)
        router_k = one_router if router_k is None else router_k + one_router
        kv_grads = one_grads if start == 0 else kv_grads + one_grads
    out_grads = low(tn(low(nn(mixed_ref[...], order_out_ref[...])), grad_raw))
    start_grads = small_grad_ref[...]
    vectors = [start_grads[0:1] + gain_1_grad, start_grads[1:2], start_grads[2:3], router_k]
    vectors += [start_grads[3:4], jnp.zeros((SMALL - 5, features), F32)]
    vectors = low(jnp.concatenate(vectors, axis=0))
    small_cols = low(jnp.transpose(nn(vectors, order)))
    upper = jnp.concatenate([low(q_grads), low(kv_grads), small_cols], axis=1)
    put_blocks(send_ref, keep_ref, batch_n, upper, out_grads[: HH * DH // PARTS])


def finish(
    x_ref,
    small_ref,
    grad_middle_ref,
    grad_normed_ref,
    from_below_ref,
    from_above_ref,
    backs_ref,
    pq_t_ref,
    pk_t_ref,
    pf_t_ref,
    middle_ref,
    light_ref,
    f_norm_ref,
    output_ref,
    input_grad_ref,
):
    tokens, features = x_ref.shape
    routed = f_norm_ref.shape[0]
    small = small_ref[...]
    gate = sigmoid_dot(f_norm_ref[...], small[4:5])
    backs = sum_blocks(backs_ref, routed, slice(0, 3 * features))
    heavy = exact(pf_t_ref[...], backs[:, 2 * features :] * gate)
    output_ref[...] = low(middle_ref[...] + light_ref[...] + heavy)
    grad = grad_normed_ref[...] + exact(pq_t_ref[...], backs[:, :features])
    grad = grad + exact(pk_t_ref[...], backs[:, features : 2 * features])
    below = from_below_ref[...].astype(F32)
    above = from_above_ref[...].astype(F32)
    grad = grad + jnp.concatenate([below, above], axis=0)
    x = x_ref[...].astype(F32)
    input_grad_ref[...] = grad_middle_ref[...] + rms_back(grad, x, rms_inverse(x), small[0:1])


def pair_sum(keep_ref, got_ref, send_out_ref, keep_out_ref):
    count = send_out_ref.shape[0]
    total = keep_ref[...].astype(F32) + got_ref[...].astype(F32)
    send_out_ref[...] = low(total[:count])
    keep_out_ref[...] = low(total[count:])


def sum_leading(ref, cols):
    total = ref[0, :, cols].astype(F32)
    for i in range(1, ref.shape[0]):
        total = total + ref[i, :, cols].astype(F32)
    return total


def join_blocks(out_ref, at, first_ref, second_ref, width):
    rows = out_ref.shape[1]
    total = first_ref[: out_ref.shape[0] * rows, :width].astype(F32)
    total = total + second_ref[: out_ref.shape[0] * rows, :width].astype(F32)
    for i in range(out_ref.shape[0]):
        out_ref[i, :, at : at + width] = low(total[i * rows : (i + 1) * rows])


def join_light(keep_ref, got_ref, out_ref):
    join_blocks(out_ref, 0, keep_ref, got_ref, keep_ref.shape[1])


def join_back(backs_ref, ffn_ref, grads_ref, out_ref, down_ref):
    blocks, routed, width = out_ref.shape
    features = ffn_ref.shape[1]
    in_rows = grads_ref.shape[0] - down_ref.shape[0]
    rows = in_rows // blocks
    hidden = width - 3 * features
    total = grads_ref[...].astype(F32)
    down_ref[...] = total[in_rows:, :features]
    for i in range(blocks):
        out_ref[i, :, : 2 * features] = backs_ref[i * routed : (i + 1) * routed]
        out_ref[i, :, 2 * features : 3 * features] = ffn_ref[i * routed : (i + 1) * routed]
        out_ref[i, :rows, 3 * features :] = low(total[i * rows : (i + 1) * rows, :hidden])
        out_ref[i, rows:, 3 * features :] = jnp.zeros((routed - rows, hidden), BF)


def join_heads(keep_ref, got_ref, out_ref, rest_ref):
    join_blocks(out_ref, 0, keep_ref, got_ref, out_ref.shape[2])
    start = out_ref.shape[0] * out_ref.shape[1]
    count, features = rest_ref.shape
    rest = keep_ref[start : start + count, :features].astype(F32)
    rest_ref[...] = low(rest + got_ref[start : start + count, :features].astype(F32))


def pack_units(late_ref, down_ref, out_ref):
    blocks, routed, width = late_ref.shape
    features = down_ref.shape[1]
    in_rows = out_ref.shape[0] - down_ref.shape[0]
    rows = in_rows // blocks
    hidden = width - features
    pieces = [late_ref[i, :, features:].astype(F32)[:rows] for i in range(blocks)]
    out_ref[...] = jnp.zeros_like(out_ref)
    out_ref[:in_rows, :hidden] = low(jnp.concatenate(pieces, axis=0))
    out_ref[in_rows:, :features] = down_ref[...]


def pack_late(t_ref, in_ref, out_ref):
    features = t_ref.shape[1]
    rows = in_ref.shape[0]
    hidden = in_ref.shape[1] // 2 // out_ref.shape[0]
    for i in range(out_ref.shape[0]):
        out_ref[i, :, :features] = t_ref[...]
        for half in range(2):
            at = half * in_ref.shape[1] // 2 + i * hidden
            to = features + half * hidden
            out_ref[i, :rows, to : to + hidden] = in_ref[:, at : at + hidden]
            out_ref[i, rows:, to : to + hidden] = jnp.zeros((out_ref.shape[1] - rows, hidden), BF)


def light_results(total_ref, light_in_ref, light_down_ref):
    rows, features = total_ref.shape[1], light_down_ref.shape[1]
    wide = light_in_ref.shape[1]
    more = light_down_ref.shape[0] - rows
    width = features * more // rows
    light_in_ref[...] = sum_leading(total_ref, slice(0, wide))
    light_down_ref[:rows] = sum_leading(total_ref, slice(wide, wide + features))
    rest = sum_leading(total_ref, slice(wide + features, wide + features + width))
    for i in range(rows // more):
        light_down_ref[rows:, i * width : (i + 1) * width] = rest[i * more : (i + 1) * more]


def hidden_results(total_ref, heavy_in_ref):
    blocks = total_ref.shape[0]
    rows = heavy_in_ref.shape[0]
    hidden = heavy_in_ref.shape[1] // 2 // blocks
    first = total_ref.shape[2] - 2 * hidden
    for i in range(blocks):
        for half in range(2):
            at = half * heavy_in_ref.shape[1] // 2 + i * hidden
            cols = slice(first + half * hidden, first + (half + 1) * hidden)
            heavy_in_ref[:, at : at + hidden] = total_ref[i, :, cols].astype(F32)[:rows]


def head_results(total_ref, heavy_ref, small_ref):
    features = heavy_ref.shape[1] // 3
    blocks = total_ref.shape[0]
    first = 0
    each = blocks // PARTS
    width = features // PARTS
    for kind in range(3):
        cols = slice(first + kind * LANES, first + (kind + 1) * LANES)
        pieces = []
        for part in range(PARTS):
            total = total_ref[part * each, :, cols].astype(F32)
            for i in range(1, each):
                total = total + total_ref[part * each + i, :, cols].astype(F32)
            pieces.append(total[:, :width])
        heavy_ref[:, kind * features : (kind + 1) * features] = jnp.concatenate(pieces, axis=1)
    small_ref[...] = sum_leading(total_ref, slice(first + 3 * LANES, first + 3 * LANES + SMALL))


def pack_blocks(*refs):
    out = refs[-1]
    at = 0
    for ref in refs[:-1]:
        out[:, at : at + ref.shape[1]] = ref[...]
        at += ref.shape[1]


def after(kernel, count, extra):
    def body(*refs):
        kernel(*refs[:count], *refs[count + extra :])

    return body if extra else kernel


def call(kernel, args, memory, outs, scratch, flops, name, far=0, needs=()):
    spaces = {"v": pltpu.VMEM, "s": pltpu.SMEM, "h": pl.ANY}
    kernel = after(kernel, len(args), len(needs))
    args = tuple(args) + tuple(needs)
    memory = memory + "h" * len(needs)
    return pl.pallas_call(
        kernel,
        out_shape=[jax.ShapeDtypeStruct(shape, kind) for shape, kind in outs],
        in_specs=[pl.BlockSpec(memory_space=spaces[one]) for one in memory],
        out_specs=[pl.BlockSpec(memory_space=pltpu.VMEM)] * (len(outs) - far)
        + [pl.BlockSpec(memory_space=pl.ANY)] * far,
        scratch_shapes=scratch,
        compiler_params=pltpu.CompilerParams(vmem_limit_bytes=VMEM_LIMIT),
        cost_estimate=pl.CostEstimate(flops=flops, bytes_accessed=flops // 400, transcendentals=0),
        name=name,
    )(*args)


def select_rows(rows, mask):
    blocks = rows.astype(F32).reshape(mask.shape[0], ROUTE, rows.shape[1])
    return jnp.sum(jnp.where(mask[:, :, None], blocks, 0.0), axis=1)


def shifted(block, axis, distance):
    devices = range(lax.axis_size(axis))
    route = [(i - distance, i) for i in devices if i - distance in devices]
    return lax.ppermute(block, axis, route)


def swapped(block, distance):
    return lax.ppermute(block, "batch", [(i, i ^ distance) for i in range(lax.axis_size("batch"))])


def exchange(blocks, axis):
    return lax.all_to_all(blocks, axis, 0, 0, tiled=True)


def spread_to_all(block, axis):
    count = lax.axis_size(axis)
    return exchange(jnp.broadcast_to(block[None], (count,) + block.shape), axis)


def presum(blocks):
    if blocks.shape[0] > 16:
        return jnp.sum(blocks.astype(F32), axis=0)
    return blocks.reshape(-1, blocks.shape[2])


def summed(blocks, axis):
    return jnp.sum(exchange(blocks, axis).astype(F32), axis=0)


def pack_rows(down, rows):
    width = down.shape[1] * (down.shape[0] - rows) // rows
    rest = down[rows:]
    pieces = [rest[:, i : i + width] for i in range(0, down.shape[1], width)]
    return jnp.concatenate([down[:rows], jnp.concatenate(pieces, axis=0)], axis=1)


def halves_summed(keep, got, needs=()):
    height, width = keep.shape
    count = height // 2
    steps = width // 128
    block = 128 * max(i for i in range(1, 9) if steps % i == 0)
    rows_in = pl.BlockSpec((height, block), lambda i: (0, i))
    rows_out = pl.BlockSpec((count, block), lambda i: (0, i))
    return pl.pallas_call(
        after(pair_sum, 2, len(needs)),
        grid=(width // block,),
        out_shape=[jax.ShapeDtypeStruct((count, width), BF)] * 2,
        in_specs=[rows_in] * 2 + [pl.BlockSpec(memory_space=pl.ANY)] * len(needs),
        out_specs=[rows_out] * 2,
        compiler_params=pltpu.CompilerParams(vmem_limit_bytes=VMEM_LIMIT),
        cost_estimate=pl.CostEstimate(
            flops=height * width, bytes_accessed=height * width // 8, transcendentals=0
        ),
        name="pair_sum",
    )(keep, got, *needs)


def canonical(piece, core, pair):
    other = swapped(piece, 2)
    piece = jnp.where(pair == 0, jnp.stack([piece, other]), jnp.stack([other, piece]))
    other = swapped(piece, 1)
    piece = jnp.where(core == 0, jnp.stack([piece, other], 1), jnp.stack([other, piece], 1))
    return piece.reshape((4,) + piece.shape[2:])


def pad_cols(block, width):
    return jnp.pad(block, ((0, 0), (0, width - block.shape[1])))


def order_matrix(order):
    size = order.shape[0]
    return low((lax.broadcasted_iota(jnp.int32, (size, size), 0) == order[None, :]).astype(F32))


def other_first(index, axis, own):
    flipped = np.flip(index, axis)
    return jnp.where(own == 0, jnp.asarray(flipped), jnp.asarray(index))


def local(
    layer_input,
    cotangent,
    doc_lengths,
    routes,
    norm_gains,
    router,
    light_qkv,
    light_out,
    heavy_qkv,
    heavy_out,
    light_in,
    light_down,
    heavy_in,
    heavy_down,
):
    seq_n = lax.axis_size("seq")
    batch_n = lax.axis_size("batch")
    devices = seq_n * batch_n
    rows = light_qkv.shape[0]
    x = layer_input[0]
    g = cotangent[0]
    tokens, features = x.shape
    routed = tokens // ROUTE
    keys = routed * seq_n
    wide = light_qkv.shape[1]
    seq = lax.axis_index("seq")
    own = lax.axis_index("batch")
    core, pair = own % 2, own // 2
    offset = seq * tokens

    small = pad_cols(jnp.concatenate([norm_gains, router], axis=1), SMALL)
    sources = [
        ("light_qkv", light_qkv),
        ("light_out", light_out),
        ("light_in", light_in),
        ("light_down", pack_rows(light_down, rows)),
    ]
    layout = {}
    at = 0
    for name, block in sources:
        layout[name] = (at, at + block.shape[1])
        at += block.shape[1]
    packed = call(
        pack_blocks,
        [block for _, block in sources],
        "v" * len(sources),
        [((rows, at), BF)],
        [],
        1_000_000,
        "pack",
    )[0]
    full = lax.all_gather(packed, BOTH, axis=0, tiled=True)

    masks = [
        lax.broadcasted_iota(jnp.int32, (routed, ROUTE), 1) == routes[i, 0][:, None]
        for i in range(3)
    ]
    xq = low(select_rows(x, masks[0]))
    xk = low(select_rows(x, masks[1]))
    t = low(select_rows(g, masks[2]))
    query_parts = seq_n // PARTS
    count = keys // query_parts
    part = seq // query_parts
    query_first = (seq % query_parts) * count
    head_width = features // PARTS
    head_all = 3 * LANES + SMALL
    hidden = heavy_in.shape[1] // 2 // seq_n
    in_rows = features // batch_n
    every = lambda block: jnp.broadcast_to(block[None], (seq_n,) + block.shape)
    tall = lambda blocks: jnp.pad(blocks, ((0, 0), (0, routed - rows), (0, 0)))
    head_cols = heavy_qkv.reshape(rows, 3, PARTS, head_width)
    head_cols = jnp.pad(head_cols, ((0, 0), (0, 0), (0, 0), (0, LANES - head_width)))
    head_cols = head_cols.transpose(2, 0, 1, 3).reshape(PARTS, rows, 3 * LANES)
    head_cols = jnp.repeat(head_cols, query_parts, axis=0)
    head_cols = jnp.concatenate([head_cols, every(small)], axis=2)
    travelling = every(jnp.concatenate([xq, xk], axis=1))
    travel = exchange(jnp.concatenate([travelling, tall(head_cols)], axis=2), "seq")
    if query_parts == 2:
        other = lax.ppermute(heavy_out, "seq", [(i, i ^ 1) for i in range(seq_n)])
        out_rows = jnp.where(
            seq % 2 == 0, jnp.stack([heavy_out, other]), jnp.stack([other, heavy_out])
        )
    else:
        groups = [list(range(i, i + query_parts)) for i in range(0, seq_n, query_parts)]
        out_rows = jnp.broadcast_to(heavy_out[None], (query_parts,) + heavy_out.shape)
        out_rows = lax.all_to_all(out_rows, "seq", 0, 0, tiled=True, axis_index_groups=groups)
    out_count = query_parts * rows
    out_rows = pad_cols(out_rows.reshape(out_count, features), head_all)
    piece = travel[:, :rows, 2 * features :].reshape(in_rows, head_all)
    piece = canonical(jnp.concatenate([piece, out_rows], axis=0), core, pair)
    index = np.arange(features).reshape(seq_n, 2, 2, rows)
    order_h = order_matrix(jnp.asarray(index.transpose(1, 2, 0, 3).reshape(-1)))
    wx = low(nn(order_h, piece[:, :in_rows].reshape(features, head_all)))
    h_out = piece[:, in_rows:, :features].reshape(batch_n, query_parts, rows, features)
    h_out = h_out.transpose(1, 0, 2, 3).reshape(head_width, features)
    h_out = jnp.pad(h_out, ((0, LANES - head_width), (0, 0)))
    below = shifted(x[tokens - WIN :], "seq", 1)
    above = shifted(x[:WIN], "seq", -1)

    def relative(array):
        array = jnp.where(core == 0, np.flip(array, 0), array)
        return jnp.where(pair == 0, jnp.flip(array, 1), array).reshape(-1)

    order = order_matrix(relative(index.transpose(2, 1, 0, 3)))
    out_index = np.arange(head_width).reshape(query_parts, 2, 2, rows)
    out_index = relative(out_index.transpose(2, 1, 0, 3))
    rest = jnp.arange(head_width, LANES, dtype=out_index.dtype)
    order_out = order_matrix(jnp.concatenate([out_index, rest]))
    ends = jnp.cumsum(doc_lengths[0])
    meta = jnp.stack([ends[0], ends[1], ends[2], ends[3], offset, tokens * seq_n, query_first])
    meta = meta.astype(jnp.int32)
    place = lax.broadcasted_iota(jnp.int32, (routed, tokens), 1)
    first = lax.broadcasted_iota(jnp.int32, (routed, tokens), 0) * ROUTE
    picks = [(place == first + routes[i, 0][:, None]).astype(F32) for i in range(3)]
    place_t = lax.broadcasted_iota(jnp.int32, (tokens, routed), 0)
    first_t = lax.broadcasted_iota(jnp.int32, (tokens, routed), 1) * ROUTE
    picks_t = [(place_t == first_t + routes[i, 0][None, :]).astype(F32) for i in range(3)]

    xq_all = travel[:, :, :features].reshape(keys, features)
    xq_part = lax.dynamic_slice_in_dim(xq_all, query_first, count, 0)
    xk_all = travel[:, :, features : 2 * features].reshape(keys, features)
    raw, heavy_q, heavy_kv, heavy_mixed, small_rows = call(
        heavy_forward,
        (meta, xq_part, xk_all, wx, h_out),
        "svvvv",
        [
            ((keys, features), BF),
            ((count, LANES), BF),
            ((keys, 2 * LANES), BF),
            ((count, LANES), BF),
            ((8, features), F32),
        ],
        [],
        2_000_000_000,
        "heavy_forward",
    )
    raw = presum(exchange(raw.reshape(seq_n, routed, features), "seq"))

    late = call(
        pack_late,
        (t, heavy_in),
        "vv",
        [((seq_n, routed, features + 2 * hidden), BF)],
        [],
        1_000_000,
        "pack_late",
        needs=[travel],
    )[0]
    late = exchange(late, "seq")
    pack_width = max(2 * hidden, features)
    piece = call(
        pack_units,
        (late, heavy_down),
        "vv",
        [((in_rows + heavy_down.shape[0], pack_width), BF)],
        [],
        1_000_000,
        "pack_units",
        needs=[full],
    )[0]
    piece = lax.all_gather(piece, "batch", axis=0, tiled=True)
    piece = piece.reshape(batch_n, -1, pack_width)
    h_in = low(nn(order_h, piece[:, :in_rows, : 2 * hidden].reshape(features, 2 * hidden)))
    h_down = piece[:, in_rows:, :features].reshape(hidden, features)
    t_all = late[:, :, :features].reshape(keys, features)

    weight = lambda columns: pltpu.VMEM((features, columns), BF)
    q, kv, mixed, base = call(
        functools.partial(light_forward, layout),
        (meta, below, x, above, small_rows, full),
        "svvvvh",
        [
            ((tokens, features), BF),
            ((tokens + 2 * WIN, 2 * features), BF),
            ((tokens, features), BF),
            ((tokens, features), F32),
        ],
        [weight(wide), weight(features), pltpu.SemaphoreType.DMA((2,))],
        8_000_000_000,
        "light_forward",
    )
    heavy_raw, middle, normed2, f_norm, f_sent = call(
        second_norm,
        (base, xq, raw, picks_t[0], picks[2], small_rows),
        "vvvvvv",
        [
            ((routed, features), F32),
            ((tokens, features), F32),
            ((tokens, features), BF),
            ((routed, features), F32),
            ((keys, features + SMALL), BF),
        ],
        [],
        1_000_000,
        "second_norm",
    )
    f_sent = exchange(f_sent.reshape(seq_n, routed, features + SMALL), "seq")
    light_hidden = light_in.shape[1] // 2
    down_width = layout["light_down"][1] - layout["light_down"][0]
    half = features // 2
    ffn_width = light_in.shape[1] + down_width
    ffn, grad_n2, light_send, light_keep = call(
        functools.partial(light_ffn, layout, devices),
        (normed2, g, order, full),
        "vvvh",
        [
            ((tokens, features), F32),
            ((tokens, features), F32),
            ((half, ffn_width), BF),
            ((half, ffn_width), BF),
        ],
        [
            weight(light_in.shape[1]),
            weight(down_width),
            pltpu.VMEM((light_hidden, features), BF),
            pltpu.VMEM((features, down_width), F32),
            weight(down_width),
            pltpu.SemaphoreType.DMA((2,)),
        ],
        1_000_000,
        "light_ffn",
    )
    down_rows = hidden // batch_n
    back, ffn_part, ffn_grads = call(
        functools.partial(heavy_ffn, batch_n),
        (f_sent.reshape(keys, features + SMALL), t_all, h_in, h_down, order_h),
        "vvvvv",
        [
            ((keys, features + SMALL), BF),
            ((keys, features), BF),
            ((batch_n * (in_rows + down_rows), pack_width), BF),
        ],
        [],
        4_000_000_000,
        "heavy_ffn",
    )
    back = presum(exchange(back.reshape(seq_n, routed, features + SMALL), "seq"))

    ffn_grads = lax.psum_scatter(ffn_grads, "batch", scatter_dimension=0, tiled=True)
    light_got = swapped(light_send, 1)
    light_send, light_keep = halves_summed(light_keep, light_got)
    light_got = swapped(light_send, 2)

    grad_middle, do, grad_raw, q_back, small_grad = call(
        functools.partial(norm_backward, layout),
        (
            xq,
            picks[0],
            picks_t[2],
            g,
            heavy_raw,
            middle,
            f_norm,
            small_rows,
            grad_n2,
            back,
            full,
        ),
        "v" * 10 + "h",
        [
            ((tokens, features), F32),
            ((tokens, features), BF),
            ((keys, features), BF),
            ((routed, features), F32),
            ((8, features), F32),
        ],
        [weight(features), pltpu.SemaphoreType.DMA((1,))],
        1_000_000,
        "norm_backward",
    )
    grad_normed, halo_below, halo_above, small_grad, attn_grads = call(
        functools.partial(light_backward, layout),
        (
            meta,
            below,
            x,
            above,
            picks_t[0],
            q,
            kv,
            mixed,
            grad_middle,
            do,
            q_back,
            small_rows,
            small_grad,
            full,
        ),
        "s" + "v" * 12 + "h",
        [
            ((tokens, features), F32),
            ((WIN, features), BF),
            ((WIN, features), BF),
            ((8, features), F32),
            ((features, wide + features), BF),
        ],
        [
            weight(wide),
            pltpu.VMEM((tokens, features), BF),
            pltpu.VMEM((tokens + 2 * WIN, 2 * features), F32),
            pltpu.VMEM((3, features, features), BF),
            pltpu.SemaphoreType.DMA((1,)),
            pltpu.SemaphoreType.DMA((3,)),
        ],
        1_000_000,
        "light_backward",
        1,
        [light_keep],
    )

    attn_sums = lax.psum_scatter(attn_grads, BOTH, scatter_dimension=0, tiled=True)
    light_rows = call(
        join_light,
        (light_keep, light_got),
        "vv",
        [((seq_n, rows, ffn_width), BF)],
        [],
        1_000_000,
        "join_light",
    )[0]
    light_sums = exchange(light_rows, "seq")

    grad_raw = exchange(grad_raw.reshape(seq_n, routed, features), "seq").reshape(keys, features)
    head_rows_n = head_width // batch_n
    backs, head_send, head_keep = call(
        functools.partial(heavy_backward, batch_n),
        (
            meta,
            xq_part,
            xk_all,
            grad_raw,
            heavy_q,
            heavy_kv,
            heavy_mixed,
            small_rows,
            small_grad,
            wx,
            h_out,
            order,
            order_out,
        ),
        "s" + "v" * 12,
        [
            ((keys, 2 * features), BF),
            ((batch_n // 2 * (in_rows + head_rows_n), head_all), BF),
            ((batch_n // 2 * (in_rows + head_rows_n), head_all), BF),
        ],
        [],
        1_000_000,
        "heavy_backward",
    )
    backs, grad_h_down = call(
        join_back,
        (backs, ffn_part, ffn_grads),
        "vvv",
        [((seq_n, routed, 3 * features + 2 * hidden), BF), (heavy_down.shape, F32)],
        [],
        1_000_000,
        "join_back",
    )
    backs = exchange(backs, "seq")
    back_rows = presum(backs[:, :, : 3 * features]) if seq_n > 16 else backs.reshape(keys, -1)

    head_got = swapped(head_send, 1)
    head_send, head_keep = halves_summed(head_keep, head_got)
    total, out_grads = call(
        join_heads,
        (head_keep, swapped(head_send, 2)),
        "vv",
        [((seq_n, rows, head_all), BF), ((out_count, features), BF)],
        [],
        1_000_000,
        "join_heads",
    )
    total = exchange(total, "seq")
    out_grads = out_grads.reshape(query_parts, rows, features)
    if query_parts == 2:
        out_send = jnp.where(seq % 2 == 0, out_grads[1], out_grads[0])
        out_keep = jnp.where(seq % 2 == 0, out_grads[0], out_grads[1])
        other = lax.ppermute(out_send, "seq", [(i, i ^ 1) for i in range(seq_n)])
        grad_heavy_out = out_keep.astype(F32) + other.astype(F32)
    else:
        out_grads = lax.all_to_all(out_grads, "seq", 0, 0, tiled=True, axis_index_groups=groups)
        grad_heavy_out = jnp.sum(out_grads.astype(F32), axis=0)
    grad_light_in, grad_light_down = call(
        light_results,
        (light_sums,),
        "v",
        [(light_in.shape, F32), (light_down.shape, F32)],
        [],
        1_000_000,
        "light_results",
    )
    grad_h_in = call(
        hidden_results,
        (backs,),
        "v",
        [(heavy_in.shape, F32)],
        [],
        1_000_000,
        "hidden_results",
    )[0]
    grad_heads, grad_small = call(
        head_results,
        (total,),
        "v",
        [(heavy_qkv.shape, F32), ((rows, SMALL), F32)],
        [],
        1_000_000,
        "head_results",
    )
    attn_sums = attn_sums.astype(F32)

    from_above = shifted(halo_below, "seq", -1)
    from_below = shifted(halo_above, "seq", 1)
    output, input_grad = call(
        finish,
        (
            x,
            small_rows,
            grad_middle,
            grad_normed,
            from_below,
            from_above,
            back_rows,
            picks_t[0],
            picks_t[1],
            picks_t[2],
            middle,
            ffn,
            f_norm,
        ),
        "v" * 13,
        [((tokens, features), BF), ((tokens, features), F32)],
        [],
        1_000_000,
        "finish",
    )
    return (
        output[None],
        input_grad[None],
        grad_small[:, :2],
        grad_small[:, 2:5],
        attn_sums[:, :wide],
        attn_sums[:, wide:],
        grad_heads,
        grad_heavy_out,
        grad_light_in,
        grad_light_down,
        grad_h_in,
        grad_h_down,
    )


def solution(mesh):
    weight = P(BOTH, None)
    rows = P("batch", "seq", None)
    return jax.shard_map(
        local,
        mesh=mesh,
        in_specs=(rows, rows, P("batch", None), P(None, "batch", "seq")) + (weight,) * 10,
        out_specs=(rows, rows) + (weight,) * 10,
        check_vma=False,
    )
```

```python
import functools

import jax
import jax.numpy as jnp
import numpy as np
from jax import lax
from jax.experimental import pallas as pl
from jax.experimental.pallas import tpu as pltpu
from jax.sharding import PartitionSpec as P

HL = 8
DL = 96
HH = 12
DH = 64
WIN = 128
ROUTE = 8
SMALL = 128
CHUNK = 256
PARTS = 4
LANES = 256
EPS = 1e-06
BF = jnp.bfloat16
F32 = jnp.float32
BOTH = ("seq", "batch")
highest = lax.Precision.HIGHEST
VMEM_LIMIT = 60 * 1024 * 1024


def nn(left, right):
    return jnp.dot(left, right, preferred_element_type=F32)


def nt(left, right):
    return lax.dot_general(left, right, (((1,), (1,)), ((), ())), preferred_element_type=F32)


def tn(left, right):
    return lax.dot_general(left, right, (((0,), (0,)), ((), ())), preferred_element_type=F32)


def exact(left, right):
    return jnp.dot(left, right, precision=highest, preferred_element_type=F32)


def low(values):
    return values.astype(BF)


def row_sum(values):
    return jnp.sum(values, axis=-1, keepdims=True)


def rms_inverse(values):
    return lax.rsqrt(jnp.mean(values * values, axis=-1, keepdims=True) + EPS)


def rms_back(grad, values, inverse, gain):
    scaled = grad * gain
    inner = jnp.mean(scaled * values, axis=-1, keepdims=True)
    return inverse * scaled - values * (inverse * inverse * inverse * inner)


def geglu_parts(pair):
    half = pair.shape[-1] // 2
    u = pair[:, :half]
    up = pair[:, half:]
    c = 0.7978845608028654
    t = jnp.tanh(c * (u + 0.044715 * (u * u * u)))
    gelu = 0.5 * u * (1.0 + t)
    slope = 0.5 * (1.0 + t) + 0.5 * u * (1.0 - t * t) * (c * (1.0 + 3.0 * 0.044715 * (u * u)))
    return gelu, slope, up


def documents(positions, meta):
    found = (positions >= meta[0]).astype(jnp.int32)
    for i in range(1, 4):
        found = found + (positions >= meta[i]).astype(jnp.int32)
    return found


def head_rows(width, size):
    lanes = lax.broadcasted_iota(jnp.int32, (1, width), 1)
    inside = [(lanes >= i * size) & (lanes < (i + 1) * size) for i in range(width // size)]
    return [jnp.where(one, 1.0, 0.0) for one in inside]


def stack_heads(rows, masks):
    return jnp.concatenate([rows * low(mask) for mask in masks], axis=0)


def merge_heads(stacked, masks):
    count = stacked.shape[0] // len(masks)
    total = stacked[:count] * masks[0]
    for i in range(1, len(masks)):
        total = total + stacked[i * count : (i + 1) * count] * masks[i]
    return total


def softmax(scores):
    weights = jnp.exp(scores - jnp.max(scores, axis=-1, keepdims=True))
    return weights * (1.0 / row_sum(weights))


def light_bias(meta, block, tokens):
    query = meta[4] + block * WIN + lax.broadcasted_iota(jnp.int32, (WIN, 1), 0)
    key = meta[4] + (block - 1) * WIN + lax.broadcasted_iota(jnp.int32, (1, 3 * WIN), 1)
    key_doc = jnp.where((key >= 0) & (key < meta[5]), documents(key, meta), -1)
    seen = (jnp.abs(query - key) < WIN) & (documents(query, meta) == key_doc)
    return jnp.where(seen, 0.0, -1e30)


def heavy_bias(meta, count, keys):
    query = (meta[6] + lax.broadcasted_iota(jnp.int32, (count, 1), 0)) * ROUTE
    key = lax.broadcasted_iota(jnp.int32, (1, keys), 1) * ROUTE
    return jnp.where(documents(query, meta) == documents(key, meta), 0.0, -1e30)


def light_units(tokens):
    return [(block, part) for block in range(tokens // WIN) for part in range(2)]


def sigmoid_dot(rows, vector):
    return jax.nn.sigmoid(row_sum(rows * vector))


def load(full_ref, places, sems):
    copies = []
    for i, ((first, last), buffer) in enumerate(places):
        copies.append(pltpu.make_async_copy(full_ref.at[:, first:last], buffer, sems.at[i]))
        copies[-1].start()
    return copies


def two_lanes(column):
    lanes = lax.broadcasted_iota(jnp.int32, (column.shape[0], SMALL), 1)
    high = low(column).astype(F32)
    return low(jnp.where(lanes == 0, high, jnp.where(lanes == 1, column - high, 0.0)))


def from_two_lanes(block):
    lanes = lax.broadcasted_iota(jnp.int32, block.shape, 1)
    return row_sum(jnp.where(lanes < 2, block.astype(F32), 0.0))


def sum_blocks(ref, count):
    total = ref[0:count].astype(F32)
    for i in range(1, ref.shape[0] // count):
        total = total + ref[i * count : (i + 1) * count].astype(F32)
    return total


def heavy_forward(
    meta,
    xq_ref,
    xk_ref,
    wx_ref,
    out_ref,
    raw_ref,
    q_ref,
    kv_ref,
    mixed_ref,
    small_ref,
):
    count = xq_ref.shape[0]
    keys = xk_ref.shape[0]
    at = 0
    small = jnp.transpose(wx_ref[:, 3 * LANES :].astype(F32))[:8]
    small_ref[...] = small
    gain_1 = small[0:1]
    xq = xq_ref[...].astype(F32)
    q_norm = xq * rms_inverse(xq) * gain_1
    q_ref[...] = low(nn(low(q_norm), wx_ref[:, at : at + LANES]))
    size = min(CHUNK, keys)
    for start in range(0, keys, size):
        xk = xk_ref[start : start + size].astype(F32)
        k_norm = xk * rms_inverse(xk) * gain_1
        k_gate = sigmoid_dot(k_norm, small[3:4])
        raw = nn(low(k_norm), wx_ref[:, at + LANES : at + 3 * LANES])
        kv_ref[start : start + size, :LANES] = low(raw[:, :LANES])
        kv_ref[start : start + size, LANES:] = low(raw[:, LANES:] * k_gate)
    masks = head_rows(LANES, DH)[: HH // PARTS]
    bias = jnp.concatenate([heavy_bias(meta, count, keys)] * len(masks), axis=0)
    stacked = stack_heads(q_ref[...], masks)
    probs = softmax(nt(stacked, kv_ref[:, :LANES]) * DH ** (-0.5) + bias)
    mixed = low(merge_heads(nn(low(probs), kv_ref[:, LANES:]), masks))
    mixed_ref[...] = mixed
    raw_ref[...] = jnp.zeros_like(raw_ref)
    raw_ref[pl.ds(pl.multiple_of(meta[6], count), count)] = low(nn(mixed, out_ref[...]))


def light_forward(
    layout,
    meta,
    below_ref,
    x_ref,
    above_ref,
    xq_ref,
    raw_ref,
    pq_t_ref,
    pf_ref,
    small_ref,
    full_ref,
    q_ref,
    kv_ref,
    mixed_ref,
    heavy_raw_ref,
    middle_ref,
    normed2_ref,
    f_norm_ref,
    f_sent_ref,
    w_qkv,
    w_lo,
    sems,
):
    tokens, features = x_ref.shape
    routed = xq_ref.shape[0]
    copies = load(full_ref, [(layout["light_qkv"], w_qkv), (layout["light_out"], w_lo)], sems)
    small = small_ref[...]
    gain_1, gain_2 = small[0:1], small[1:2]
    xe = jnp.concatenate([below_ref[...], x_ref[...], above_ref[...]], axis=0).astype(F32)
    ne = low(xe * rms_inverse(xe) * gain_1)
    xq = xq_ref[...].astype(F32)
    q_gate = sigmoid_dot(xq * rms_inverse(xq) * gain_1, small[2:3])
    heavy_raw = sum_blocks(raw_ref, routed)
    heavy_raw_ref[...] = heavy_raw
    base = x_ref[...].astype(F32) + exact(pq_t_ref[...], heavy_raw * q_gate)
    copies[0].wait()
    q_ref[...] = low(nn(ne[WIN : WIN + tokens], w_qkv[:, :features]))
    kv_ref[...] = low(nn(ne, w_qkv[:, features:]))
    width = features // 2
    masks = head_rows(width, DL)
    scale = DL ** (-0.5)
    for block, part in light_units(tokens):
        cols = slice(part * width, (part + 1) * width)
        rows = slice(block * WIN, (block + 1) * WIN)
        key_rows = slice(block * WIN, (block + 3) * WIN)
        bias = jnp.concatenate([light_bias(meta, block, tokens)] * len(masks), axis=0)
        stacked = stack_heads(q_ref[rows, cols], masks)
        probs = softmax(nt(stacked, kv_ref[key_rows, cols]) * scale + bias)
        values = kv_ref[key_rows, features + part * width : features + (part + 1) * width]
        mixed_ref[rows, cols] = low(merge_heads(nn(low(probs), values), masks))
    copies[1].wait()
    middle = base + nn(mixed_ref[...], w_lo[...])
    middle_ref[...] = middle
    normed2 = middle * rms_inverse(middle) * gain_2
    normed2_ref[...] = low(normed2)
    f_norm = exact(pf_ref[...], normed2)
    f_norm_ref[...] = f_norm
    sent = jnp.concatenate([low(f_norm), two_lanes(sigmoid_dot(f_norm, small[4:5]))], axis=1)
    for i in range(f_sent_ref.shape[0] // routed):
        f_sent_ref[i * routed : (i + 1) * routed] = sent


def unpack_down(packed, down_ref, work_ref, devices):
    features = down_ref.shape[1]
    rows = packed.shape[0] // devices
    more = down_ref.shape[0] // devices - rows
    width = packed.shape[1] - features
    if rows % 8 == 0 and more % 8 == 0:
        work_ref[...] = packed.astype(F32)
        for i in range(devices):
            own = work_ref[i * rows : (i + 1) * rows, :features]
            parts = [
                work_ref[i * rows + j * more : i * rows + (j + 1) * more, features:]
                for j in range(rows // more)
            ]
            whole = jnp.concatenate([own, jnp.concatenate(parts, axis=1)], axis=0)
            down_ref[i * (rows + more) : (i + 1) * (rows + more)] = low(whole)
    else:
        for j in range(rows // more):
            cols = slice(j * width, (j + 1) * width)
            first, second = down_places(down_ref.shape[0], packed.shape[0], rows, more, j)
            down_ref[:, cols] = low(nn(first, packed[:, cols]) + nn(second, packed[:, features:]))


def down_places(units, packed_rows, rows, more, j):
    unit = lax.broadcasted_iota(jnp.int32, (units, packed_rows), 0)
    row = lax.broadcasted_iota(jnp.int32, (units, packed_rows), 1)
    total = rows + more
    device, inner = unit // total, unit % total
    first = (inner < rows) & (row == device * rows + inner)
    second = (inner >= rows) & (row == device * rows + j * more + inner - rows)
    return low(jnp.where(first, 1.0, 0.0)), low(jnp.where(second, 1.0, 0.0))


def pack_down(grad, out_ref, at, devices, rows):
    features = grad.shape[1]
    more = grad.shape[0] // devices - rows
    width = features * more // rows
    if rows % 8 == 0 and more % 8 == 0:
        pieces = []
        for i in range(devices):
            start = i * (rows + more)
            rest = grad[start + rows : start + rows + more]
            parts = [rest[:, j * width : (j + 1) * width] for j in range(rows // more)]
            pieces.append(
                jnp.concatenate([grad[start : start + rows], jnp.concatenate(parts, axis=0)], axis=1)
            )
        out_ref[:, at:] = low(jnp.concatenate(pieces, axis=0))
    else:
        total = None
        for j in range(rows // more):
            cols = slice(j * width, (j + 1) * width)
            first, second = down_places(grad.shape[0], devices * rows, rows, more, j)
            block = low(grad[:, cols])
            out_ref[:, at + j * width : at + (j + 1) * width] = low(tn(first, block))
            part = tn(second, block)
            total = part if total is None else total + part
        out_ref[:, at + features :] = low(total)


def light_ffn(
    layout,
    devices,
    normed2_ref,
    g_ref,
    order_ref,
    full_ref,
    ffn_ref,
    grad_ref,
    send_ref,
    keep_ref,
    w_in,
    w_packed,
    w_down,
    work_ref,
    pack_ref,
    sems,
):
    features = normed2_ref.shape[1]
    half = features // 2
    order = order_ref[...]
    copies = []
    for i, (name, buffer) in enumerate([("light_in", w_in), ("light_down", w_packed)]):
        first, last = layout[name]
        copy = pltpu.make_async_copy(full_ref.at[:, first:last], buffer, sems.at[i])
        copy.start()
        copies.append(copy)
    copies[0].wait()
    copies[1].wait()
    unpack_down(w_packed[...], w_down, work_ref, devices)
    gelu, slope, up = geglu_parts(nn(normed2_ref[...], w_in[...]))
    hidden = low(gelu * up)
    ffn_ref[...] = nn(hidden, w_down[...])
    grad_hidden = nt(g_ref[...], w_down[...])
    grad_pair = low(jnp.concatenate([grad_hidden * up * slope, grad_hidden * gelu], axis=1))
    grad_ref[...] = nt(grad_pair, w_in[...])
    wide = w_in.shape[1]
    left = low(nn(normed2_ref[...], order))
    for at in range(0, wide, 512):
        block = low(tn(left, grad_pair[:, at : at + 512]))
        send_ref[:, at : at + 512] = block[:half]
        keep_ref[:, at : at + 512] = block[half:]
    pack_down(tn(hidden, g_ref[...]), pack_ref, 0, devices, features // devices)
    block = low(tn(order, pack_ref[...]))
    send_ref[:, wide:] = block[:half]
    keep_ref[:, wide:] = block[half:]


def heavy_ffn(
    batch_n,
    sent_ref,
    t_ref,
    in_ref,
    down_ref,
    order_ref,
    order_units_ref,
    back_ref,
    ffn_ref,
    send_ref,
    keep_ref,
):
    features = in_ref.shape[0]
    hidden_n = down_ref.shape[0]
    w_in = in_ref[...]
    f_in = sent_ref[:, :features]
    gate = from_two_lanes(sent_ref[:, features:])
    t = t_ref[...].astype(F32)
    grad_ffn = low(t * gate)
    gelu, slope, up = geglu_parts(nn(f_in, w_in))
    hidden = low(gelu * up)
    ffn = nn(hidden, down_ref[...])
    ffn_ref[...] = low(ffn)
    grad_hidden = nt(grad_ffn, down_ref[...])
    grad_pair = low(jnp.concatenate([grad_hidden * up * slope, grad_hidden * gelu], axis=1))
    back_ref[:, :features] = low(nt(grad_pair, w_in))
    back_ref[:, features:] = two_lanes(row_sum(t * ffn))
    grad_in = low(tn(low(nn(f_in, order_ref[...])), grad_pair))
    grad_down = low(tn(low(nn(hidden, order_units_ref[...])), grad_ffn))
    put_blocks(send_ref, keep_ref, batch_n, grad_in, grad_down)


def put_blocks(send_ref, keep_ref, batch_n, upper, lower):
    upper_rows = upper.shape[0] // batch_n
    lower_rows = lower.shape[0] // batch_n
    total = upper_rows + lower_rows
    width = send_ref.shape[1]
    for i in range(batch_n):
        ref = send_ref if i < batch_n // 2 else keep_ref
        start = i % (batch_n // 2) * total
        places = [(start, upper_rows, upper), (start + upper_rows, lower_rows, lower)]
        for first, count, values in places:
            ref[first : first + count, : values.shape[1]] = values[i * count : (i + 1) * count]
            if values.shape[1] < width:
                ref[first : first + count, values.shape[1] :] = jnp.zeros(
                    (count, width - values.shape[1]), BF
                )


def light_backward(
    layout,
    meta,
    below_ref,
    x_ref,
    above_ref,
    xq_ref,
    pq_ref,
    pq_t_ref,
    pf_t_ref,
    g_ref,
    order_ref,
    q_ref,
    kv_ref,
    mixed_ref,
    heavy_raw_ref,
    middle_ref,
    f_norm_ref,
    small_ref,
    grad_n2_ref,
    back_ref,
    full_ref,
    grad_middle_ref,
    grad_normed_ref,
    halo_below_ref,
    halo_above_ref,
    grad_raw_ref,
    small_grad_ref,
    send_ref,
    keep_ref,
    w_qkv,
    w_lo,
    dq_ref,
    dkv_ref,
    stage,
    sems,
    out_sems,
):
    tokens, features = x_ref.shape
    routed = xq_ref.shape[0]
    half = features // 2
    copies = load(full_ref, [(layout["light_out"], w_lo), (layout["light_qkv"], w_qkv)], sems)
    small = small_ref[...]
    gain_1, gain_2 = small[0:1], small[1:2]
    started = []

    def put(at, grad):
        width = grad.shape[1]
        slot = len(started) % stage.shape[0]
        if len(started) >= stage.shape[0]:
            for copy in started[-stage.shape[0]]:
                copy.wait()
        stage[slot, :, :width] = low(grad)
        both = []
        for i, ref in enumerate((send_ref, keep_ref)):
            source = stage.at[slot, i * half : (i + 1) * half, :width]
            both.append(
                pltpu.make_async_copy(source, ref.at[:, at : at + width], out_sems.at[slot, i])
            )
            both[-1].start()
        started.append(both)

    sums = sum_blocks(back_ref, routed)
    f_norm = f_norm_ref[...]
    f_gate = sigmoid_dot(f_norm, small[4:5])
    f_logit = (sums[:, features : features + 1] + sums[:, features + 1 : features + 2]) * (
        f_gate * (1.0 - f_gate)
    )
    router_f = jnp.sum(f_norm * f_logit, axis=0, keepdims=True)
    f_back = sums[:, :features] + f_logit * small[4:5]
    middle = middle_ref[...]
    grad_n2 = grad_n2_ref[...] + exact(pf_t_ref[...], f_back)
    inverse_2 = rms_inverse(middle)
    gain_2_grad = jnp.sum(grad_n2 * (middle * inverse_2), axis=0, keepdims=True)
    grad_middle = g_ref[...].astype(F32) + rms_back(grad_n2, middle, inverse_2, gain_2)
    grad_middle_ref[...] = grad_middle
    middle_low = low(grad_middle)

    q_rows = exact(pq_ref[...], grad_middle)
    xq = xq_ref[...].astype(F32)
    q_plain = xq * rms_inverse(xq)
    q_norm = q_plain * gain_1
    q_gate = sigmoid_dot(q_norm, small[2:3])
    grad_raw = low(q_rows * q_gate)
    for i in range(grad_raw_ref.shape[0] // routed):
        grad_raw_ref[i * routed : (i + 1) * routed] = grad_raw
    q_logit = row_sum(q_rows * heavy_raw_ref[...]) * q_gate * (1.0 - q_gate)
    q_back = q_logit * small[2:3]
    router_q = jnp.sum(q_norm * q_logit, axis=0, keepdims=True)
    gain_1_grad = jnp.sum(q_back * q_plain, axis=0, keepdims=True)

    copies[0].wait()
    order = order_ref[...]
    put(3 * features, tn(low(nn(mixed_ref[...], order)), middle_low))
    do = low(nt(middle_low, w_lo[...]))
    width = features // 2
    masks = head_rows(width, DL)
    scale = DL ** (-0.5)
    dkv_ref[...] = jnp.zeros_like(dkv_ref)
    for block, part in light_units(tokens):
        cols = slice(part * width, (part + 1) * width)
        value_cols = slice(features + part * width, features + (part + 1) * width)
        rows = slice(block * WIN, (block + 1) * WIN)
        key_rows = slice(block * WIN, (block + 3) * WIN)
        bias = jnp.concatenate([light_bias(meta, block, tokens)] * len(masks), axis=0)
        stacked = stack_heads(q_ref[rows, cols], masks)
        do_stacked = stack_heads(do[rows, cols], masks)
        key = kv_ref[key_rows, cols]
        probs = softmax(nt(stacked, key) * scale + bias)
        grad_probs = nt(do_stacked, kv_ref[key_rows, value_cols])
        ds = low(probs * (grad_probs - row_sum(probs * grad_probs)))
        dq_ref[rows, cols] = low(merge_heads(nn(ds, key), masks) * scale)
        dkv_ref[key_rows, cols] += tn(ds, stacked) * scale
        dkv_ref[key_rows, value_cols] += tn(low(probs), do_stacked)

    copies[1].wait()
    xe = jnp.concatenate([below_ref[...], x_ref[...], above_ref[...]], axis=0).astype(F32)
    plain = xe * rms_inverse(xe)
    left = low(nn(low(plain * gain_1), order))
    dk = low(dkv_ref[:, :features])
    dv = low(dkv_ref[:, features:])
    inner = slice(WIN, WIN + tokens)
    put(0, tn(left[inner], dq_ref[...]))
    put(features, tn(left, dk))
    put(2 * features, tn(left, dv))
    back = nt(dk, w_qkv[:, features : 2 * features]) + nt(dv, w_qkv[:, 2 * features :])
    own = back[inner] + nt(dq_ref[...], w_qkv[:, :features])
    halo_below_ref[...] = low(back[:WIN])
    halo_above_ref[...] = low(back[WIN + tokens :])
    gain_1_grad = gain_1_grad + jnp.sum(own * plain[inner], axis=0, keepdims=True)
    gain_1_grad = gain_1_grad + jnp.sum(back[:WIN] * plain[:WIN], axis=0, keepdims=True)
    gain_1_grad = gain_1_grad + jnp.sum(
        back[WIN + tokens :] * plain[WIN + tokens :], axis=0, keepdims=True
    )
    grad_normed_ref[...] = own + exact(pq_t_ref[...], q_back)
    rest = jnp.zeros((4, features), F32)
    small_grad_ref[...] = jnp.concatenate(
        [gain_1_grad, gain_2_grad, router_q, router_f, rest], axis=0
    )
    for both in started[-stage.shape[0] :]:
        for copy in both:
            copy.wait()


def heavy_backward(
    batch_n,
    meta,
    xq_ref,
    xk_ref,
    grad_raw_ref,
    q_ref,
    kv_ref,
    mixed_ref,
    small_ref,
    small_grad_ref,
    wx_ref,
    out_ref,
    order_ref,
    order_out_ref,
    backs_ref,
    send_ref,
    keep_ref,
):
    at = 0
    count = xq_ref.shape[0]
    keys = xk_ref.shape[0]
    features = wx_ref.shape[0]
    small = small_ref[...]
    gain_1 = small[0:1]
    place = pl.ds(pl.multiple_of(meta[6], count), count)
    grad_raw = grad_raw_ref[place]
    do = low(nt(grad_raw, out_ref[...]))
    masks = head_rows(LANES, DH)[: HH // PARTS]
    scale = DH ** (-0.5)
    bias = jnp.concatenate([heavy_bias(meta, count, keys)] * len(masks), axis=0)
    stacked = stack_heads(q_ref[...], masks)
    do_stacked = stack_heads(do, masks)
    probs = softmax(nt(stacked, kv_ref[:, :LANES]) * scale + bias)
    grad_probs = nt(do_stacked, kv_ref[:, LANES:])
    ds = low(probs * (grad_probs - row_sum(probs * grad_probs)))
    probs = low(probs)
    dq = low(merge_heads(nn(ds, kv_ref[:, :LANES]), masks) * scale)
    q_back = nt(dq, wx_ref[:, at : at + LANES])
    backs_ref[:, :features] = jnp.zeros((keys, features), BF)
    backs_ref[place, :features] = low(q_back)
    xq = xq_ref[...].astype(F32)
    q_plain = xq * rms_inverse(xq)
    order = order_ref[...]
    gain_1_grad = jnp.sum(q_back * q_plain, axis=0, keepdims=True)
    q_grads = tn(low(nn(low(q_plain * gain_1), order)), dq)
    router_k = None
    size = min(CHUNK, keys)
    for start in range(0, keys, size):
        rows = slice(start, start + size)
        xk = xk_ref[rows].astype(F32)
        k_plain = xk * rms_inverse(xk)
        k_norm = k_plain * gain_1
        k_low = low(k_norm)
        k_gate = sigmoid_dot(k_norm, small[3:4])
        dk = tn(ds[:, rows], stacked) * scale
        dv = tn(probs[:, rows], do_stacked)
        raw = nn(k_low, wx_ref[:, at + 2 * LANES : at + 3 * LANES])
        k_logit = row_sum(dv * raw) * k_gate * (1.0 - k_gate)
        grad_raw_k = low(jnp.concatenate([dk, dv * k_gate], axis=1))
        k_back = nt(grad_raw_k, wx_ref[:, at + LANES : at + 3 * LANES]) + k_logit * small[3:4]
        backs_ref[rows, features:] = low(k_back)
        one_router = jnp.sum(k_norm * k_logit, axis=0, keepdims=True)
        gain_1_grad = gain_1_grad + jnp.sum(k_back * k_plain, axis=0, keepdims=True)
        one_grads = tn(low(nn(k_low, order)), grad_raw_k)
        router_k = one_router if router_k is None else router_k + one_router
        kv_grads = one_grads if start == 0 else kv_grads + one_grads
    out_grads = low(tn(low(nn(mixed_ref[...], order_out_ref[...])), grad_raw))
    start_grads = small_grad_ref[...]
    vectors = [start_grads[0:1] + gain_1_grad, start_grads[1:2], start_grads[2:3], router_k]
    vectors += [start_grads[3:4], jnp.zeros((SMALL - 5, features), F32)]
    vectors = low(jnp.concatenate(vectors, axis=0))
    small_cols = low(jnp.transpose(nn(vectors, order)))
    upper = jnp.concatenate([low(q_grads), low(kv_grads), small_cols], axis=1)
    put_blocks(send_ref, keep_ref, batch_n, upper, out_grads[: HH * DH // PARTS])


def finish(
    x_ref,
    small_ref,
    grad_middle_ref,
    grad_normed_ref,
    from_below_ref,
    from_above_ref,
    backs_ref,
    pq_t_ref,
    pk_t_ref,
    pf_t_ref,
    middle_ref,
    light_ref,
    f_norm_ref,
    output_ref,
    input_grad_ref,
):
    tokens, features = x_ref.shape
    routed = f_norm_ref.shape[0]
    small = small_ref[...]
    gate = sigmoid_dot(f_norm_ref[...], small[4:5])
    backs = sum_blocks(backs_ref, routed)
    heavy = exact(pf_t_ref[...], backs[:, 2 * features :] * gate)
    output_ref[...] = low(middle_ref[...] + light_ref[...] + heavy)
    grad = grad_normed_ref[...] + exact(pq_t_ref[...], backs[:, :features])
    grad = grad + exact(pk_t_ref[...], backs[:, features : 2 * features])
    below = from_below_ref[...].astype(F32)
    above = from_above_ref[...].astype(F32)
    grad = grad + jnp.concatenate([below, above], axis=0)
    x = x_ref[...].astype(F32)
    input_grad_ref[...] = grad_middle_ref[...] + rms_back(grad, x, rms_inverse(x), small[0:1])


def pair_sum(keep_ref, got_ref, send_out_ref, keep_out_ref):
    count = send_out_ref.shape[0]
    total = keep_ref[...].astype(F32) + got_ref[...].astype(F32)
    send_out_ref[...] = low(total[:count])
    keep_out_ref[...] = low(total[count:])


def sum_leading(ref, cols):
    total = ref[0, :, cols].astype(F32)
    for i in range(1, ref.shape[0]):
        total = total + ref[i, :, cols].astype(F32)
    return total


def join_blocks(out_ref, at, first_ref, second_ref, width):
    rows = out_ref.shape[1]
    total = first_ref[: out_ref.shape[0] * rows, :width].astype(F32)
    total = total + second_ref[: out_ref.shape[0] * rows, :width].astype(F32)
    for i in range(out_ref.shape[0]):
        out_ref[i, :, at : at + width] = low(total[i * rows : (i + 1) * rows])


def join_ffn(light_keep_ref, light_got_ref, ffn_keep_ref, ffn_got_ref, out_ref, down_ref):
    wide = light_keep_ref.shape[1]
    join_blocks(out_ref, 0, light_keep_ref, light_got_ref, wide)
    join_blocks(out_ref, wide, ffn_keep_ref, ffn_got_ref, out_ref.shape[2] - wide)
    start = out_ref.shape[0] * out_ref.shape[1]
    count, features = down_ref.shape
    down = ffn_keep_ref[start : start + count, :features].astype(F32)
    down_ref[...] = down + ffn_got_ref[start : start + count, :features].astype(F32)


def join_attention(keep_ref, got_ref, head_keep_ref, head_got_ref, out_ref, rest_ref):
    wide = keep_ref.shape[1]
    join_blocks(out_ref, 0, keep_ref, got_ref, wide)
    join_blocks(out_ref, wide, head_keep_ref, head_got_ref, out_ref.shape[2] - wide)
    start = out_ref.shape[0] * out_ref.shape[1]
    count, features = rest_ref.shape
    rest = head_keep_ref[start : start + count, :features].astype(F32)
    rest_ref[...] = low(rest + head_got_ref[start : start + count, :features].astype(F32))


def ffn_results(total_ref, light_in_ref, light_down_ref, heavy_in_ref):
    blocks = total_ref.shape[0]
    rows, features = total_ref.shape[1], light_down_ref.shape[1]
    wide = light_in_ref.shape[1]
    more = light_down_ref.shape[0] - rows
    width = features * more // rows
    light_in_ref[...] = sum_leading(total_ref, slice(0, wide))
    light_down_ref[:rows] = sum_leading(total_ref, slice(wide, wide + features))
    rest = sum_leading(total_ref, slice(wide + features, wide + features + width))
    for i in range(rows // more):
        light_down_ref[rows:, i * width : (i + 1) * width] = rest[i * more : (i + 1) * more]
    first = wide + features + width
    hidden = heavy_in_ref.shape[1] // 2 // blocks
    for i in range(blocks):
        for half in range(2):
            at = half * heavy_in_ref.shape[1] // 2 + i * hidden
            cols = slice(first + half * hidden, first + (half + 1) * hidden)
            heavy_in_ref[:, at : at + hidden] = total_ref[i, :, cols].astype(F32)


def attention_results(total_ref, light_qkv_ref, light_out_ref, heavy_ref, small_ref):
    blocks = total_ref.shape[0]
    wide = light_qkv_ref.shape[1]
    features = light_out_ref.shape[1]
    light_qkv_ref[...] = sum_leading(total_ref, slice(0, wide))
    light_out_ref[...] = sum_leading(total_ref, slice(wide, wide + features))
    first = wide + features
    each = blocks // PARTS
    width = features // PARTS
    for kind in range(3):
        cols = slice(first + kind * LANES, first + (kind + 1) * LANES)
        pieces = []
        for part in range(PARTS):
            total = total_ref[part * each, :, cols].astype(F32)
            for i in range(1, each):
                total = total + total_ref[part * each + i, :, cols].astype(F32)
            pieces.append(total[:, :width])
        heavy_ref[:, kind * features : (kind + 1) * features] = jnp.concatenate(pieces, axis=1)
    small_ref[...] = sum_leading(total_ref, slice(first + 3 * LANES, first + 3 * LANES + SMALL))


def pack_blocks(*refs):
    out = refs[-1]
    at = 0
    for ref in refs[:-1]:
        out[:, at : at + ref.shape[1]] = ref[...]
        at += ref.shape[1]


def after(kernel, count, extra):
    def body(*refs):
        kernel(*refs[:count], *refs[count + extra :])

    return body if extra else kernel


def call(kernel, args, memory, outs, scratch, flops, name, far=0, needs=()):
    spaces = {"v": pltpu.VMEM, "s": pltpu.SMEM, "h": pl.ANY}
    kernel = after(kernel, len(args), len(needs))
    args = tuple(args) + tuple(needs)
    memory = memory + "h" * len(needs)
    return pl.pallas_call(
        kernel,
        out_shape=[jax.ShapeDtypeStruct(shape, kind) for shape, kind in outs],
        in_specs=[pl.BlockSpec(memory_space=spaces[one]) for one in memory],
        out_specs=[pl.BlockSpec(memory_space=pltpu.VMEM)] * (len(outs) - far)
        + [pl.BlockSpec(memory_space=pl.ANY)] * far,
        scratch_shapes=scratch,
        compiler_params=pltpu.CompilerParams(vmem_limit_bytes=VMEM_LIMIT),
        cost_estimate=pl.CostEstimate(flops=flops, bytes_accessed=20_000_000, transcendentals=0),
        name=name,
    )(*args)


def select_rows(rows, mask):
    blocks = rows.astype(F32).reshape(mask.shape[0], ROUTE, rows.shape[1])
    return jnp.sum(jnp.where(mask[:, :, None], blocks, 0.0), axis=1)


def shifted(block, axis, distance):
    devices = range(lax.axis_size(axis))
    route = [(i - distance, i) for i in devices if i - distance in devices]
    return lax.ppermute(block, axis, route)


def swapped(block, distance):
    return lax.ppermute(block, "batch", [(i, i ^ distance) for i in range(lax.axis_size("batch"))])


def exchange(blocks, axis):
    return lax.all_to_all(blocks, axis, 0, 0, tiled=True)


def spread_to_all(block, axis):
    count = lax.axis_size(axis)
    return exchange(jnp.broadcast_to(block[None], (count,) + block.shape), axis)


def presum(blocks):
    if blocks.shape[0] > 16:
        return jnp.sum(blocks.astype(F32), axis=0)
    return blocks.reshape(-1, blocks.shape[2])


def summed(blocks, axis):
    return jnp.sum(exchange(blocks, axis).astype(F32), axis=0)


def pack_rows(down, rows):
    width = down.shape[1] * (down.shape[0] - rows) // rows
    rest = down[rows:]
    pieces = [rest[:, i : i + width] for i in range(0, down.shape[1], width)]
    return jnp.concatenate([down[:rows], jnp.concatenate(pieces, axis=0)], axis=1)


def halves_summed(keep, got, needs=()):
    height, width = keep.shape
    count = height // 2
    steps = width // 128
    block = 128 * max(i for i in range(1, 9) if steps % i == 0)
    rows_in = pl.BlockSpec((height, block), lambda i: (0, i))
    rows_out = pl.BlockSpec((count, block), lambda i: (0, i))
    return pl.pallas_call(
        after(pair_sum, 2, len(needs)),
        grid=(width // block,),
        out_shape=[jax.ShapeDtypeStruct((count, width), BF)] * 2,
        in_specs=[rows_in] * 2 + [pl.BlockSpec(memory_space=pl.ANY)] * len(needs),
        out_specs=[rows_out] * 2,
        compiler_params=pltpu.CompilerParams(vmem_limit_bytes=VMEM_LIMIT),
        cost_estimate=pl.CostEstimate(
            flops=height * width, bytes_accessed=6 * height * width, transcendentals=0
        ),
        name="pair_sum",
    )(keep, got, *needs)


def canonical(piece, core, pair):
    other = swapped(piece, 2)
    piece = jnp.where(pair == 0, jnp.stack([piece, other]), jnp.stack([other, piece]))
    other = swapped(piece, 1)
    piece = jnp.where(core == 0, jnp.stack([piece, other], 1), jnp.stack([other, piece], 1))
    return piece.reshape((4,) + piece.shape[2:])


def pad_cols(block, width):
    return jnp.pad(block, ((0, 0), (0, width - block.shape[1])))


def order_matrix(order):
    size = order.shape[0]
    return low((lax.broadcasted_iota(jnp.int32, (size, size), 0) == order[None, :]).astype(F32))


def other_first(index, axis, own):
    flipped = np.flip(index, axis)
    return jnp.where(own == 0, jnp.asarray(flipped), jnp.asarray(index))


def local(
    layer_input,
    cotangent,
    doc_lengths,
    routes,
    norm_gains,
    router,
    light_qkv,
    light_out,
    heavy_qkv,
    heavy_out,
    light_in,
    light_down,
    heavy_in,
    heavy_down,
):
    seq_n = lax.axis_size("seq")
    batch_n = lax.axis_size("batch")
    devices = seq_n * batch_n
    rows = light_qkv.shape[0]
    x = layer_input[0]
    g = cotangent[0]
    tokens, features = x.shape
    routed = tokens // ROUTE
    keys = routed * seq_n
    wide = light_qkv.shape[1]
    seq = lax.axis_index("seq")
    own = lax.axis_index("batch")
    core, pair = own % 2, own // 2
    offset = seq * tokens

    small = pad_cols(jnp.concatenate([norm_gains, router], axis=1), SMALL)
    sources = [
        ("light_qkv", light_qkv),
        ("light_out", light_out),
        ("light_in", light_in),
        ("light_down", pack_rows(light_down, rows)),
    ]
    layout = {}
    at = 0
    for name, block in sources:
        layout[name] = (at, at + block.shape[1])
        at += block.shape[1]
    packed = call(
        pack_blocks,
        [block for _, block in sources],
        "v" * len(sources),
        [((rows, at), BF)],
        [],
        1_000_000,
        "pack",
    )[0]
    full = lax.all_gather(packed, BOTH, axis=0, tiled=True)

    masks = [
        lax.broadcasted_iota(jnp.int32, (routed, ROUTE), 1) == routes[i, 0][:, None]
        for i in range(3)
    ]
    xq = low(select_rows(x, masks[0]))
    xk = low(select_rows(x, masks[1]))
    t = low(select_rows(g, masks[2]))
    query_parts = seq_n // PARTS
    count = keys // query_parts
    part = seq // query_parts
    query_first = (seq % query_parts) * count
    head_width = features // PARTS
    head_all = 3 * LANES + SMALL
    hidden = heavy_in.shape[1] // 2 // seq_n
    in_rows = features // batch_n
    every = lambda block: jnp.broadcast_to(block[None], (seq_n,) + block.shape)
    tall = lambda blocks: jnp.pad(blocks, ((0, 0), (0, routed - rows), (0, 0)))
    head_cols = heavy_qkv.reshape(rows, 3, PARTS, head_width)
    head_cols = jnp.pad(head_cols, ((0, 0), (0, 0), (0, 0), (0, LANES - head_width)))
    head_cols = head_cols.transpose(2, 0, 1, 3).reshape(PARTS, rows, 3 * LANES)
    head_cols = jnp.repeat(head_cols, query_parts, axis=0)
    head_cols = jnp.concatenate([head_cols, every(small)], axis=2)
    sent = jnp.concatenate([every(jnp.concatenate([xq, xk], axis=1)), tall(head_cols)], axis=2)
    travel = exchange(sent, "seq")
    in_cols = heavy_in.reshape(rows, 2, seq_n, hidden).transpose(2, 0, 1, 3)
    in_cols = in_cols.reshape(seq_n, rows, 2 * hidden)
    late = exchange(jnp.concatenate([every(t), tall(in_cols)], axis=2), "seq")
    if query_parts == 2:
        other = lax.ppermute(heavy_out, "seq", [(i, i ^ 1) for i in range(seq_n)])
        out_rows = jnp.where(
            seq % 2 == 0, jnp.stack([heavy_out, other]), jnp.stack([other, heavy_out])
        )
    else:
        groups = [list(range(i, i + query_parts)) for i in range(0, seq_n, query_parts)]
        out_rows = jnp.broadcast_to(heavy_out[None], (query_parts,) + heavy_out.shape)
        out_rows = lax.all_to_all(out_rows, "seq", 0, 0, tiled=True, axis_index_groups=groups)
    out_count = query_parts * rows
    out_rows = pad_cols(out_rows.reshape(out_count, features), head_all)
    piece = travel[:, :rows, 2 * features :].reshape(in_rows, head_all)
    piece = canonical(jnp.concatenate([piece, out_rows], axis=0), core, pair)
    index = np.arange(features).reshape(seq_n, 2, 2, rows)
    order_h = order_matrix(jnp.asarray(index.transpose(1, 2, 0, 3).reshape(-1)))
    wx = low(nn(order_h, piece[:, :in_rows].reshape(features, head_all)))
    h_out = piece[:, in_rows:, :features].reshape(batch_n, query_parts, rows, features)
    h_out = h_out.transpose(1, 0, 2, 3).reshape(head_width, features)
    h_out = jnp.pad(h_out, ((0, LANES - head_width), (0, 0)))
    pack_width = max(2 * hidden, features)
    piece = late[:, :rows, features:].reshape(in_rows, 2 * hidden)
    piece = [pad_cols(piece, pack_width), pad_cols(heavy_down, pack_width)]
    piece = canonical(jnp.concatenate(piece, axis=0), core, pair)
    h_in = low(nn(order_h, piece[:, :in_rows, : 2 * hidden].reshape(features, 2 * hidden)))
    h_down = piece[:, in_rows:, :features].reshape(hidden, features)
    t_all = late[:, :, :features].reshape(keys, features)
    below = shifted(x[tokens - WIN :], "seq", 1)
    above = shifted(x[:WIN], "seq", -1)

    def relative(array):
        array = jnp.where(core == 0, np.flip(array, 0), array)
        return jnp.where(pair == 0, jnp.flip(array, 1), array).reshape(-1)

    order = order_matrix(relative(index.transpose(2, 1, 0, 3)))
    units = np.arange(hidden).reshape(2, 2, -1)
    order_units = order_matrix(relative(units.transpose(1, 0, 2)))
    out_index = np.arange(head_width).reshape(query_parts, 2, 2, rows)
    out_index = relative(out_index.transpose(2, 1, 0, 3))
    rest = jnp.arange(head_width, LANES, dtype=out_index.dtype)
    order_out = order_matrix(jnp.concatenate([out_index, rest]))
    ends = jnp.cumsum(doc_lengths[0])
    meta = jnp.stack([ends[0], ends[1], ends[2], ends[3], offset, tokens * seq_n, query_first])
    meta = meta.astype(jnp.int32)
    place = lax.broadcasted_iota(jnp.int32, (routed, tokens), 1)
    first = lax.broadcasted_iota(jnp.int32, (routed, tokens), 0) * ROUTE
    picks = [(place == first + routes[i, 0][:, None]).astype(F32) for i in range(3)]
    place_t = lax.broadcasted_iota(jnp.int32, (tokens, routed), 0)
    first_t = lax.broadcasted_iota(jnp.int32, (tokens, routed), 1) * ROUTE
    picks_t = [(place_t == first_t + routes[i, 0][None, :]).astype(F32) for i in range(3)]

    xq_all = travel[:, :, :features].reshape(keys, features)
    xq_part = lax.dynamic_slice_in_dim(xq_all, query_first, count, 0)
    xk_all = travel[:, :, features : 2 * features].reshape(keys, features)
    raw, heavy_q, heavy_kv, heavy_mixed, small_rows = call(
        heavy_forward,
        (meta, xq_part, xk_all, wx, h_out),
        "svvvv",
        [
            ((keys, features), BF),
            ((count, LANES), BF),
            ((keys, 2 * LANES), BF),
            ((count, LANES), BF),
            ((8, features), F32),
        ],
        [],
        2_000_000_000,
        "heavy_forward",
    )
    raw = presum(exchange(raw.reshape(seq_n, routed, features), "seq"))

    weight = lambda columns: pltpu.VMEM((features, columns), BF)
    q, kv, mixed, heavy_raw, middle, normed2, f_norm, f_sent = call(
        functools.partial(light_forward, layout),
        (meta, below, x, above, xq, raw, picks_t[0], picks[2], small_rows, full),
        "svvvvvvvvh",
        [
            ((tokens, features), BF),
            ((tokens + 2 * WIN, 2 * features), BF),
            ((tokens, features), BF),
            ((routed, features), F32),
            ((tokens, features), F32),
            ((tokens, features), BF),
            ((routed, features), F32),
            ((keys, features + SMALL), BF),
        ],
        [weight(wide), weight(features), pltpu.SemaphoreType.DMA((2,))],
        8_000_000_000,
        "light_forward",
    )
    f_sent = exchange(f_sent.reshape(seq_n, routed, features + SMALL), "seq")
    light_hidden = light_in.shape[1] // 2
    down_width = layout["light_down"][1] - layout["light_down"][0]
    half = features // 2
    ffn_width = light_in.shape[1] + down_width
    ffn, grad_n2, light_send, light_keep = call(
        functools.partial(light_ffn, layout, devices),
        (normed2, g, order, full),
        "vvvh",
        [
            ((tokens, features), F32),
            ((tokens, features), F32),
            ((half, ffn_width), BF),
            ((half, ffn_width), BF),
        ],
        [
            weight(light_in.shape[1]),
            weight(down_width),
            pltpu.VMEM((light_hidden, features), BF),
            pltpu.VMEM((features, down_width), F32),
            weight(down_width),
            pltpu.SemaphoreType.DMA((2,)),
        ],
        8_000_000_000,
        "light_ffn",
    )
    down_rows = hidden // batch_n
    back, ffn_part, ffn_send, ffn_keep = call(
        functools.partial(heavy_ffn, batch_n),
        (f_sent.reshape(keys, features + SMALL), t_all, h_in, h_down, order, order_units),
        "vvvvvv",
        [
            ((keys, features + SMALL), BF),
            ((keys, features), BF),
            ((batch_n // 2 * (in_rows + down_rows), pack_width), BF),
            ((batch_n // 2 * (in_rows + down_rows), pack_width), BF),
        ],
        [],
        4_000_000_000,
        "heavy_ffn",
    )
    back = presum(exchange(back.reshape(seq_n, routed, features + SMALL), "seq"))

    light_got = swapped(light_send, 1)
    ffn_got = swapped(ffn_send, 1)
    light_send, light_keep = halves_summed(light_keep, light_got)
    light_got = swapped(light_send, 2)
    ffn_send, ffn_keep = halves_summed(ffn_keep, ffn_got)
    ffn_got = swapped(ffn_send, 2)

    (
        grad_middle,
        grad_normed,
        halo_below,
        halo_above,
        grad_raw,
        small_grad,
        attn_send,
        attn_keep,
    ) = call(
        functools.partial(light_backward, layout),
        (
            meta,
            below,
            x,
            above,
            xq,
            picks[0],
            picks_t[0],
            picks_t[2],
            g,
            order,
            q,
            kv,
            mixed,
            heavy_raw,
            middle,
            f_norm,
            small_rows,
            grad_n2,
            back,
            full,
        ),
        "s" + "v" * 18 + "h",
        [
            ((tokens, features), F32),
            ((tokens, features), F32),
            ((WIN, features), BF),
            ((WIN, features), BF),
            ((keys, features), BF),
            ((8, features), F32),
            ((half, wide + features), BF),
            ((half, wide + features), BF),
        ],
        [
            weight(wide),
            weight(features),
            pltpu.VMEM((tokens, features), BF),
            pltpu.VMEM((tokens + 2 * WIN, 2 * features), F32),
            pltpu.VMEM((3, features, features), BF),
            pltpu.SemaphoreType.DMA((2,)),
            pltpu.SemaphoreType.DMA((3, 2)),
        ],
        16_000_000_000,
        "light_backward",
        2,
    )

    attn_got = swapped(attn_send, 1)
    attn_send, attn_keep = halves_summed(attn_keep, attn_got)
    attn_got = swapped(attn_send, 2)
    grad_raw = exchange(grad_raw.reshape(seq_n, routed, features), "seq").reshape(keys, features)
    head_rows_n = head_width // batch_n
    backs, head_send, head_keep = call(
        functools.partial(heavy_backward, batch_n),
        (
            meta,
            xq_part,
            xk_all,
            grad_raw,
            heavy_q,
            heavy_kv,
            heavy_mixed,
            small_rows,
            small_grad,
            wx,
            h_out,
            order,
            order_out,
        ),
        "s" + "v" * 12,
        [
            ((keys, 2 * features), BF),
            ((batch_n // 2 * (in_rows + head_rows_n), head_all), BF),
            ((batch_n // 2 * (in_rows + head_rows_n), head_all), BF),
        ],
        [],
        4_000_000_000,
        "heavy_backward",
        needs=[attn_keep],
    )
    backs = jnp.concatenate([backs, ffn_part], axis=1)
    backs = presum(exchange(backs.reshape(seq_n, routed, 3 * features), "seq"))

    head_got = swapped(head_send, 1)
    head_send, head_keep = halves_summed(head_keep, head_got)
    total, out_grads = call(
        join_attention,
        (attn_keep, attn_got, head_keep, swapped(head_send, 2)),
        "vvvv",
        [((seq_n, rows, wide + features + head_all), BF), ((out_count, features), BF)],
        [],
        10_000_000,
        "join_attention",
        needs=[light_keep, ffn_keep, backs],
    )
    total = exchange(total, "seq")
    out_grads = out_grads.reshape(query_parts, rows, features)
    ffn_rows, grad_h_down = call(
        join_ffn,
        (light_keep, light_got, ffn_keep, ffn_got),
        "vvvv",
        [((seq_n, rows, ffn_width + 2 * hidden), BF), (heavy_down.shape, F32)],
        [],
        10_000_000,
        "join_ffn",
        needs=[total],
    )
    ffn_rows = exchange(ffn_rows, "seq")
    if query_parts == 2:
        out_send = jnp.where(seq % 2 == 0, out_grads[1], out_grads[0])
        out_keep = jnp.where(seq % 2 == 0, out_grads[0], out_grads[1])
        other = lax.ppermute(out_send, "seq", [(i, i ^ 1) for i in range(seq_n)])
        grad_heavy_out = out_keep.astype(F32) + other.astype(F32)
    else:
        out_grads = lax.all_to_all(out_grads, "seq", 0, 0, tiled=True, axis_index_groups=groups)
        grad_heavy_out = jnp.sum(out_grads.astype(F32), axis=0)
    grad_light_in, grad_light_down, grad_h_in = call(
        ffn_results,
        (ffn_rows,),
        "v",
        [(light_in.shape, F32), (light_down.shape, F32), (heavy_in.shape, F32)],
        [],
        10_000_000,
        "ffn_results",
    )
    grad_light_qkv, grad_light_out, grad_heads, grad_small = call(
        attention_results,
        (total,),
        "v",
        [(light_qkv.shape, F32), (light_out.shape, F32), (heavy_qkv.shape, F32), ((rows, SMALL), F32)],
        [],
        10_000_000,
        "attention_results",
    )

    from_above = shifted(halo_below, "seq", -1)
    from_below = shifted(halo_above, "seq", 1)
    output, input_grad = call(
        finish,
        (
            x,
            small_rows,
            grad_middle,
            grad_normed,
            from_below,
            from_above,
            backs,
            picks_t[0],
            picks_t[1],
            picks_t[2],
            middle,
            ffn,
            f_norm,
        ),
        "v" * 13,
        [((tokens, features), BF), ((tokens, features), F32)],
        [],
        1_000_000_000,
        "finish",
    )
    return (
        output[None],
        input_grad[None],
        grad_small[:, :2],
        grad_small[:, 2:5],
        grad_light_qkv,
        grad_light_out,
        grad_heads,
        grad_heavy_out,
        grad_light_in,
        grad_light_down,
        grad_h_in,
        grad_h_down,
    )


def solution(mesh):
    weight = P(BOTH, None)
    rows = P("batch", "seq", None)
    return jax.shard_map(
        local,
        mesh=mesh,
        in_specs=(rows, rows, P("batch", None), P(None, "batch", "seq")) + (weight,) * 10,
        out_specs=(rows, rows) + (weight,) * 10,
        check_vma=False,
    )
```
